32 devices in a mesh: parts: 2 (over y), blk: 4 (over z), grp: 4 (over x, core).
Axes of the slice: x: 2, y: 2, z: 4, core: 2. Of those that a mesh axis runs over, the one named last changes fastest.
Arguments:
- features: bfloat16 [512, 65536], P('grp', ('parts', 'blk')), parts along dimension 1, may hold values from -6 to 6
- tile_rows: int32 [8, 4, 20], P(('parts', 'blk')), parts along dimension 0, may hold values from 0 to 63, as said below
- tile_cols: int32 [8, 4, 20], P(('parts', 'blk')), parts along dimension 0, may hold values from 0 to 63, as said below
- tile_weights: bfloat16 [8, 4, 20, 128, 128], P(('parts', 'blk')), parts along dimension 0, may hold values from 0 to 3, as said below
- order: int32 [65536], P(('parts', 'blk')), parts along dimension 0, may hold values from 0 to 8191, as said below
- weight: bfloat16 [512, 512], replicated, may hold values from -0.25 to 0.25
- bias: float32 [512], replicated, may hold values from -3 to 3
Outputs:
- activations: bfloat16 [512, 65536], P(None, ('parts', 'blk', 'grp')), parts along dimension 1
The draws below stay inside these ranges and needn't reach their ends.
There are 2 independent parts, one for each index of `parts`. The reference program is written for one: setup_inputs(seed, part) draws one part's arguments, and reference() takes and returns one part's arrays. A program takes and returns all parts, laid end to end along the dimension named above; an argument that names none is the same for every part. Nothing has to cross between parts.
Inputs may be any that keep to these rules, and one draw needn't show every extreme that they name: `tile_rows`: row tiles of a block. For each destination block and offset the slots hold distinct (row, column) pairs among their live slots; the slots after the live ones have zero weights and coordinates 0; offset 0 has all 20 slots live. `tile_cols`: column tiles of a block, as for tile_rows. `tile_weights`: whole numbers. `order`: the 8192 entries of each vertex block are a permutation of 0 to 8191.
All inputs are finite; a program needn't handle non-finite values.
Results may differ from the reference program's by a relative error of at most 0.0031.
Values may be sent and summed in bfloat16 or wider, within the bound.
No kernel may reach another device: no remote copies, remote signals or barrier semaphores. Data moves between devices by JAX's collectives and lax.ppermute only.
A program may use at most 64 MiB of HBM per device.

```python
import jax
import jax.numpy as jnp
from jax import lax

F = 512
HID = 512
TILE = 128
TS = 20
R = 8192
NODES = 32768


def tile_layout(key):
    blocks = NODES // R
    row_tiles = R // TILE
    sparsity = max(1, TILE * blocks * TS // row_tiles // 4)
    key_live, key_pos, key_val, key_hit = jax.random.split(key, 4)
    live = jax.random.randint(key_live, (blocks, blocks), 1, TS + 1)
    live = live.at[:, 0].set(TS)
    keys = jax.random.split(key_pos, blocks * blocks)
    picks = jax.vmap(lambda single: jax.random.permutation(single, row_tiles * row_tiles)[:TS])(keys)
    picks = picks.reshape(blocks, blocks, TS).astype(jnp.int32)
    used = jnp.arange(TS)[None, None, :] < live[:, :, None]
    rows = jnp.where(used, picks // row_tiles, 0).astype(jnp.int32)
    cols = jnp.where(used, picks % row_tiles, 0).astype(jnp.int32)
    shape = (blocks, blocks, TS, TILE, TILE)
    counts = jax.random.randint(key_val, shape, 1, 4)
    hits = jax.random.randint(key_hit, shape, 0, sparsity) == 0
    weights = jnp.where(hits & used[:, :, :, None, None], counts, 0).astype(jnp.float32)
    return (rows, cols, weights)


def draw_tile_rows(key, part):
    rows, cols, weights = tile_layout(key)
    return rows


def draw_tile_cols(key, part):
    rows, cols, weights = tile_layout(key)
    return cols


def draw_tile_weights(key, part):
    rows, cols, weights = tile_layout(key)
    return weights.astype(jnp.bfloat16)


def draw_order(key, part):
    key = jax.random.fold_in(key, 7)
    blocks = NODES // R
    keys = jax.random.split(key, blocks)
    perms = jax.vmap(lambda single: jax.random.permutation(single, R))(keys)
    return perms.reshape(NODES).astype(jnp.int32)


def block_scale(key, extent, pieces, least, largest):
    loudness, own = 1.0, jax.random.fold_in(key, 6)
    for axis_at, parts in pieces:
        steps = jnp.exp(jax.random.uniform(jax.random.fold_in(own, axis_at), (parts,), jnp.float32, least / len(pieces), largest / len(pieces)))
        loudness = loudness * jnp.repeat(steps, extent[axis_at] // parts).reshape([-1 if axis == axis_at else 1 for axis in range(len(extent))])
    return loudness


def noise(rng, dims, spread, limit, pieces=(), held_as=jnp.bfloat16):
    factor_of = block_scale(rng, dims, pieces, -0.22, 0.18) if pieces else 1.0
    entries = jax.random.normal(rng, dims, jnp.float32) * spread * factor_of
    return jnp.minimum(jnp.maximum(entries, -limit), limit).astype(held_as)


def setup_inputs(seed: int = 0, part: int = 0) -> dict:
    seeds = jax.random.split(jax.random.key(seed), 8)
    own_keys = jax.random.split(jax.random.fold_in(seeds[7], part), 8)
    return {
        "features": noise(own_keys[0], (F, NODES), 1.0, 6.0, ((0, 4), (1, 4))),
        "tile_rows": draw_tile_rows(jax.random.fold_in(jax.random.fold_in(seeds[7], part), 71), part),
        "tile_cols": draw_tile_cols(jax.random.fold_in(jax.random.fold_in(seeds[7], part), 71), part),
        "tile_weights": draw_tile_weights(jax.random.fold_in(jax.random.fold_in(seeds[7], part), 71), part),
        "order": draw_order(jax.random.fold_in(jax.random.fold_in(seeds[7], part), 71), part),
        "weight": noise(seeds[5], (F, HID), F ** -0.5, 0.25),
        "bias": noise(seeds[6], (HID,), 0.5, 3.0, (), jnp.float32),
    }


def reference(features, tile_rows, tile_cols, tile_weights, order, weight, bias):
    blocks = NODES // R
    row_tiles = R // TILE
    whole = features.astype(jnp.float32).reshape(F, blocks, row_tiles, TILE)
    positions = jnp.arange(row_tiles, dtype=jnp.int32)

    def one_block(block):
        rows = tile_rows[block]
        cols = tile_cols[block]
        counts = tile_weights[block].astype(jnp.float32)
        source = ((block - jnp.arange(blocks, dtype=jnp.int32)) % blocks).astype(jnp.int32)
        gathered = whole[:, source[:, None], cols, :]
        product = jnp.einsum('fstj,stij->fsti', gathered, counts, precision=lax.Precision.HIGHEST)
        onehot = (rows[:, :, None] == positions[None, None, :]).astype(jnp.float32)
        summed = jnp.einsum('fsti,str->fri', product, onehot, precision=lax.Precision.HIGHEST)
        degree = jnp.einsum('sti,str->ri', jnp.sum(counts, axis=-1), onehot, precision=lax.Precision.HIGHEST)
        own = lax.dynamic_index_in_dim(whole, block, 1, keepdims=False)
        aggregated = ((summed + own) / (degree + 1.0)[None]).reshape(F, R)
        picks = lax.dynamic_slice(order, ((block * R).astype(jnp.int32),), (R,))
        reordered = jnp.take(aggregated, picks, axis=1).astype(jnp.bfloat16)
        mixed = jnp.dot(weight.T, reordered, preferred_element_type=jnp.float32) + bias[:, None]
        return jnp.maximum(mixed, 0.0).astype(jnp.bfloat16)

    stacked = lax.map(one_block, jnp.arange(blocks, dtype=jnp.int32))
    return jnp.transpose(stacked, (1, 0, 2)).reshape(HID, NODES)
```

```python
import functools

import jax
import jax.numpy as jnp
from jax import lax
from jax.experimental import pallas as pl
from jax.experimental.pallas import tpu as pltpu
from jax.sharding import PartitionSpec as P

NT = (((1,), (1,)), ((), ()))
VMEM = pl.BlockSpec(memory_space=pltpu.VMEM)
SMEM = pl.BlockSpec(memory_space=pltpu.SMEM)
LIMIT = 48 * 2**20


def params():
    return pltpu.CompilerParams(vmem_limit_bytes=LIMIT)


def cost(flops, moved):
    return pl.CostEstimate(flops=flops, bytes_accessed=moved, transcendentals=0)


def shifted(value, axis, steps):
    count = lax.axis_size(axis)
    pairs = [(source, (source + steps) % count) for source in range(count)]
    return lax.ppermute(value, axis, pairs)


def partner(index, k, count):
    return index ^ k if count & (count - 1) == 0 else (k - index) % count


def traded(value, axis, k):
    count = lax.axis_size(axis)
    return lax.ppermute(value, axis, [(i, partner(i, k, count)) for i in range(count)])


def cuts(width):
    first = width // 2
    return ((0, first), (first, width - first))


def pack_kernel(ranges, offsets, slots, tile, *refs):
    asked, panel, outs = refs[:offsets], refs[offsets], refs[offsets + 1 :]
    for s in range(offsets):

        def body(t, carry, s=s):
            at = pl.multiple_of(asked[s][t] * tile, tile)
            for p, (low, size) in enumerate(ranges):
                outs[p * offsets + s][t] = panel[pl.ds(low, size), pl.ds(at, tile)]
            return carry

        lax.fori_loop(0, slots, body, 0, unroll=4)


def pack(panel, asked, ranges, tile):
    offsets, slots = len(asked), asked[0].shape[0]
    shapes = [
        jax.ShapeDtypeStruct((slots, size, tile), panel.dtype)
        for _, size in ranges
        for _ in range(offsets)
    ]
    outs = pl.pallas_call(
        functools.partial(pack_kernel, ranges, offsets, slots, tile),
        out_shape=shapes,
        in_specs=[SMEM] * offsets + [VMEM],
        out_specs=[VMEM] * len(shapes),
        compiler_params=params(),
        cost_estimate=cost(0, 4 * panel.size),
        name="pack",
    )(*asked, panel)
    return [outs[p * offsets : (p + 1) * offsets] for p in range(len(ranges))]


def own_kernel(ranges, blocks, slots, tile, rows, cols, panel, counts, *outs):
    accs, inverse = outs[:-1], outs[-1]
    lanes = inverse.shape[1]
    row_tiles = panel.shape[1] // tile
    eye = (
        lax.broadcasted_iota(jnp.int32, (tile, tile), 0)
        == lax.broadcasted_iota(jnp.int32, (tile, tile), 1)
    ).astype(jnp.float32).astype(jnp.bfloat16)
    ones = jnp.ones((lanes, tile), jnp.bfloat16)

    def start(r, carry):
        at = pl.multiple_of(r * tile, tile)
        for acc, (low, size) in zip(accs, ranges):
            acc[pl.ds(at, tile), :] = lax.dot_general(
                eye,
                panel[pl.ds(low, size), pl.ds(at, tile)],
                NT,
                preferred_element_type=jnp.float32,
            )
        inverse[pl.ds(at, tile), :] = jnp.ones((tile, lanes), jnp.float32)
        return carry

    lax.fori_loop(0, row_tiles, start, 0)

    def add(t, carry):
        at = pl.multiple_of(rows[0, t] * tile, tile)
        col = pl.multiple_of(cols[0, t] * tile, tile)
        for acc, (low, size) in zip(accs, ranges):
            acc[pl.ds(at, tile), :] += lax.dot_general(
                counts[t],
                panel[pl.ds(low, size), pl.ds(col, tile)],
                NT,
                preferred_element_type=jnp.float32,
            )
        return carry

    lax.fori_loop(0, slots, add, 0)

    for s in range(blocks):

        def degree(t, carry, s=s):
            at = pl.multiple_of(rows[s, t] * tile, tile)
            inverse[pl.ds(at, tile), :] += lax.dot_general(
                counts[s * slots + t], ones, NT, preferred_element_type=jnp.float32
            )
            return carry

        lax.fori_loop(0, slots, degree, 0)

    def invert(r, carry):
        at = pl.multiple_of(r * tile, tile)
        inverse[pl.ds(at, tile), :] = 1.0 / inverse[pl.ds(at, tile), :]
        return carry

    lax.fori_loop(0, row_tiles, invert, 0)


def own(panel, rows, cols, counts, ranges):
    blocks, slots = rows.shape
    nodes, tile = panel.shape[1], counts.shape[-1]
    lanes = max(size for _, size in ranges)
    shapes = [jax.ShapeDtypeStruct((nodes, size), jnp.float32) for _, size in ranges]
    shapes.append(jax.ShapeDtypeStruct((nodes, lanes), jnp.float32))
    outs = pl.pallas_call(
        functools.partial(own_kernel, ranges, blocks, slots, tile),
        out_shape=shapes,
        in_specs=[SMEM, SMEM, VMEM, VMEM],
        out_specs=[VMEM] * len(shapes),
        compiler_params=params(),
        cost_estimate=cost(2 * nodes * tile * tile, 16 * 2**20),
        name="own",
    )(rows, cols, panel, counts)
    return outs[:-1], outs[-1]


def pick(order, first, count, nodes_ref, stage, out, out_first):
    step = stage.shape[0]

    def chunk(c, carry):
        def group(i, inner):
            at = pl.multiple_of(i * 16, 16)
            for u in range(16):
                source = order[first + c * step + at + u]
                stage[pl.ds(at + u, 1), :] = nodes_ref[pl.ds(source, 1), :]
            return inner

        lax.fori_loop(0, step // 16, group, 0)
        to = pl.multiple_of(out_first + c * step, step)
        out[pl.ds(to, step), :] = stage[...].astype(out.dtype)
        return carry

    lax.fori_loop(0, count // step, chunk, 0)


def gather_kernel(offsets, slots, tile, far, rows, order, acc, inverse, counts, *refs):
    got, total, out, stage = refs[:offsets], refs[offsets], refs[offsets + 1], refs[offsets + 2]
    size = acc.shape[1]
    total[...] = acc[...]
    for s in range(offsets):

        def add(t, carry, s=s):
            at = pl.multiple_of(rows[s + 1, t] * tile, tile)
            total[pl.ds(at, tile), :] += lax.dot_general(
                counts[(s + 1) * slots + t], got[s][t], NT, preferred_element_type=jnp.float32
            )
            return carry

        lax.fori_loop(0, slots, add, 0, unroll=2)

    def scale(r, carry):
        at = pl.multiple_of(r * tile, tile)
        total[pl.ds(at, tile), :] = total[pl.ds(at, tile), :] * inverse[pl.ds(at, tile), :size]
        return carry

    lax.fori_loop(0, total.shape[0] // tile, scale, 0)
    pick(order, 0, far, total, stage, out, 0)


def gather_far(acc, inverse, rows, order, counts, got, far):
    nodes, size = acc.shape
    slots, tile = rows.shape[1], counts.shape[-1]
    return pl.pallas_call(
        functools.partial(gather_kernel, len(got), slots, tile, far),
        out_shape=[
            jax.ShapeDtypeStruct((nodes, size), jnp.float32),
            jax.ShapeDtypeStruct((far, size), jnp.bfloat16),
        ],
        in_specs=[SMEM, SMEM] + [VMEM] * (3 + len(got)),
        out_specs=[VMEM, VMEM],
        scratch_shapes=[pltpu.VMEM((256, size), jnp.float32)],
        compiler_params=params(),
        cost_estimate=cost(2 * nodes * tile * tile, 32 * 2**20),
        name="gather_far",
    )(rows, order, acc, inverse, counts, *got)


def near_kernel(first, count, order, total, out, stage):
    pick(order, first, count, total, stage, out, 0)


def gather_near(total, order, first):
    nodes, size = total.shape
    count = order.shape[0] - first
    return pl.pallas_call(
        functools.partial(near_kernel, first, count),
        out_shape=jax.ShapeDtypeStruct((count, size), jnp.bfloat16),
        in_specs=[SMEM, VMEM],
        out_specs=VMEM,
        scratch_shapes=[pltpu.VMEM((256, size), jnp.float32)],
        compiler_params=params(),
        cost_estimate=cost(0, 24 * 2**20),
        name="gather_near",
    )(order, total)


def mix_kernel(weight, bias, *refs):
    pieces, out = refs[:-1], refs[-1]
    nodes = jnp.concatenate([piece[...] for piece in pieces], axis=1)
    mixed = lax.dot_general(weight[...], nodes, NT, preferred_element_type=jnp.float32)
    out[...] = jnp.maximum(mixed + bias[...], 0.0).astype(out.dtype)


def mix(weight, bias, pieces):
    hidden = weight.shape[0]
    nodes = pieces[0].shape[0]
    step = min(512, nodes)
    return pl.pallas_call(
        mix_kernel,
        grid=(nodes // step,),
        out_shape=jax.ShapeDtypeStruct((hidden, nodes), jnp.bfloat16),
        in_specs=[
            pl.BlockSpec(weight.shape, lambda i: (0, 0)),
            pl.BlockSpec(bias.shape, lambda i: (0, 0)),
        ]
        + [pl.BlockSpec((step, piece.shape[1]), lambda i: (i, 0)) for piece in pieces],
        out_specs=pl.BlockSpec((hidden, step), lambda i: (0, i)),
        compiler_params=params(),
        cost_estimate=cost(2 * hidden * weight.shape[1] * nodes, 5 * 2**20),
        name="mix",
    )(weight, bias, *pieces)


def on_device(features, tile_rows, tile_cols, tile_weights, order, weight, bias):
    width, nodes = features.shape
    _, blocks, slots, tile, _ = tile_weights.shape
    groups = lax.axis_size("grp")
    me = lax.axis_index("grp")
    share = nodes // groups
    ranges = cuts(width)
    rows = tile_rows[0]
    cols = tile_cols[0]
    counts = tile_weights.reshape(blocks * slots, tile, tile)

    asked = [shifted(cols[s], "blk", -s) for s in range(1, blocks)]
    packed = pack(features, asked, ranges, tile)

    ranks = list(range(groups - 1, -1, -1))
    far = max(groups - 2, 1) * share
    whose = [partner(me, k, groups) for k in ranks]
    picks = jnp.concatenate([lax.dynamic_slice(order, (w * share,), (share,)) for w in whose])
    from_rank = {k: lax.dynamic_slice(weight, (w * width, 0), (width, weight.shape[1]))
                 for k, w in zip(ranks, whose)}
    mixing = jnp.concatenate(
        [from_rank[k][low : low + size] for low, size in ranges for k in ranks], axis=0
    ).T

    accs, inverse = own(features, rows, cols, counts, ranges)
    pieces = []
    got = None
    for p in range(len(ranges)):
        sent = packed[p]
        if got is not None:
            sent = [lax.optimization_barrier((a, b))[0] for a, b in zip(sent, got)]
        got = [shifted(value, "blk", s + 1) for s, value in enumerate(sent)]
        total, out_far = gather_far(accs[p], inverse, rows, picks, counts, got, far)
        near = gather_near(total, picks, far)
        both = (out_far, near)
        for position, k in enumerate(ranks):
            at = position * share
            source, at = (out_far, at) if at < far else (near, at - far)
            piece = lax.slice_in_dim(source, at, at + share, axis=0)
            pieces.append(piece if k == 0 else traded(piece, "grp", k))
    return mix(mixing, bias[:, None], pieces)


def solution(mesh):
    in_specs = (
        P("grp", ("parts", "blk")),
        P(("parts", "blk"), None, None),
        P(("parts", "blk"), None, None),
        P(("parts", "blk"), None, None, None, None),
        P(("parts", "blk")),
        P(),
        P(),
    )
    out_specs = P(None, ("parts", "blk", "grp"))
    return jax.shard_map(
        on_device, mesh=mesh, in_specs=in_specs, out_specs=out_specs, check_vma=False
    )
```

```python
import functools

import jax
import jax.numpy as jnp
from jax import lax
from jax.experimental import pallas as pl
from jax.experimental.pallas import tpu as pltpu
from jax.sharding import PartitionSpec as P

NN = (((1,), (0,)), ((), ()))
NT = (((1,), (1,)), ((), ()))
VMEM = pl.BlockSpec(memory_space=pltpu.VMEM)
SMEM = pl.BlockSpec(memory_space=pltpu.SMEM)
CHUNK = 256


def dot(a, b, dims):
    return lax.dot_general(a, b, dims, preferred_element_type=jnp.float32)


def padded(shape, dtype):
    rows = 1
    for extent in shape[:-1]:
        rows *= extent
    return rows * -(-shape[-1] // 128) * 128 * jnp.dtype(dtype).itemsize


def call(kernel, name, scalars, arrays, outs, scratch=(), flops=0, twice=False, **kwargs):
    held = sum(padded(a.shape, a.dtype) for a in list(arrays) + list(outs))
    held += sum(padded(shape, dtype) for shape, dtype in scratch)
    return pl.pallas_call(
        kernel,
        out_shape=list(outs),
        in_specs=[SMEM] * len(scalars) + [VMEM] * len(arrays),
        out_specs=[VMEM] * len(outs),
        scratch_shapes=[pltpu.VMEM(shape, dtype) for shape, dtype in scratch],
        compiler_params=pltpu.CompilerParams(vmem_limit_bytes=held + 4 * 2**20),
        cost_estimate=pl.CostEstimate(flops=flops, bytes_accessed=held, transcendentals=0),
        name=name,
        **kwargs,
    )(*scalars, *arrays)


def shifted(value, axis, steps):
    count = lax.axis_size(axis)
    pairs = [(source, (source + steps) % count) for source in range(count)]
    return lax.ppermute(value, axis, pairs)


def traded(value, axis, k):
    return lax.ppermute(value, axis, [(i, i ^ k) for i in range(lax.axis_size(axis))])


def cuts(width):
    first = width // 2
    return ((0, first), (first, width - first))


def identity(size):
    row = lax.broadcasted_iota(jnp.int32, (size, size), 0)
    col = lax.broadcasted_iota(jnp.int32, (size, size), 1)
    return (row == col).astype(jnp.float32).astype(jnp.bfloat16)


def pack_kernel(low, size, offsets, slots, tile, *refs):
    asked, panel, outs = refs[:offsets], refs[offsets], refs[offsets + 1 :]
    for s in range(offsets):

        def body(t, carry, s=s):
            at = pl.multiple_of(asked[s][s + 1, t] * tile, tile)
            outs[s][t] = panel[pl.ds(low, size), pl.ds(at, tile)]
            return carry

        lax.fori_loop(0, slots, body, 0, unroll=4)


def pack(panel, asked, low, size, tile):
    offsets, slots = len(asked), asked[0].shape[1]
    shape = jax.ShapeDtypeStruct((slots, size, tile), panel.dtype)
    return call(
        functools.partial(pack_kernel, low, size, offsets, slots, tile),
        "pack",
        asked,
        [panel],
        [shape] * offsets,
    )


def own_kernel(ranges, blocks, slots, tile, rows, cols, panel, counts, *refs):
    accs, inverse, product = refs[: len(ranges)], refs[len(ranges)], refs[len(ranges) + 1]
    lanes = inverse.shape[1]
    row_tiles = panel.shape[1] // tile
    eye = identity(tile)
    ones = jnp.ones((tile, lanes), jnp.bfloat16)

    def start(r, carry):
        at = pl.multiple_of(r * tile, tile)
        for acc, (low, size) in zip(accs, ranges):
            acc[pl.ds(at, tile), :] = dot(eye, panel[pl.ds(low, size), pl.ds(at, tile)], NT)
        inverse[pl.ds(at, tile), :] = jnp.ones((tile, lanes), jnp.float32)
        return carry

    lax.fori_loop(0, row_tiles, start, 0, unroll=4)

    for acc, (low, size) in zip(accs, ranges):

        def multiply(t, carry, low=low, size=size):
            col = pl.multiple_of(cols[0, t] * tile, tile)
            product[t, :, :size] = dot(counts[t], panel[pl.ds(low, size), pl.ds(col, tile)], NT)
            return carry

        def add(t, carry, acc=acc, size=size):
            at = pl.multiple_of(rows[0, t] * tile, tile)
            acc[pl.ds(at, tile), :] += product[t, :, :size]
            return carry

        lax.fori_loop(0, slots, multiply, 0, unroll=4)
        lax.fori_loop(0, slots, add, 0)

    def degree(s, carry):
        def multiply(t, inner):
            product[t] = dot(counts[s * slots + t], ones, NN)
            return inner

        def add(t, inner):
            at = pl.multiple_of(rows[s, t] * tile, tile)
            inverse[pl.ds(at, tile), :] += product[t]
            return inner

        lax.fori_loop(0, slots, multiply, 0, unroll=4)
        lax.fori_loop(0, slots, add, 0)
        return carry

    lax.fori_loop(0, blocks, degree, 0)

    def invert(r, carry):
        at = pl.multiple_of(r * tile, tile)
        inverse[pl.ds(at, tile), :] = 1.0 / inverse[pl.ds(at, tile), :]
        return carry

    lax.fori_loop(0, row_tiles, invert, 0, unroll=2)


def own(panel, rows, cols, counts, ranges):
    blocks, slots = rows.shape
    nodes, tile = panel.shape[1], counts.shape[-1]
    lanes = max(size for _, size in ranges)
    shapes = [jax.ShapeDtypeStruct((nodes, size), jnp.float32) for _, size in ranges]
    shapes.append(jax.ShapeDtypeStruct((nodes, lanes), jnp.float32))
    outs = call(
        functools.partial(own_kernel, ranges, blocks, slots, tile),
        "own",
        [rows, cols],
        [panel, counts],
        shapes,
        [((slots, tile, lanes), jnp.float32)],
    )
    return outs[:-1], outs[-1]


def pick(order, base, nodes, stage, out):
    size = nodes.shape[1]
    eye = identity(size)

    def chunk(c, carry):
        def group(i, inner):
            at = pl.multiple_of(i * 16, 16)
            for u in range(16):
                source = order[base + c * CHUNK + at + u]
                stage[pl.ds(at + u, 1), :] = nodes[pl.ds(source, 1), :]
            return inner

        lax.fori_loop(0, CHUNK // 16, group, 0)
        to = pl.multiple_of(c * CHUNK, CHUNK)
        turned = dot(eye, stage[...].astype(jnp.bfloat16), NT)
        out[:, pl.ds(to, CHUNK)] = turned.astype(out.dtype)
        return carry

    lax.fori_loop(0, out.shape[1] // CHUNK, chunk, 0)


def far_kernel(offsets, slots, tile, bases, rows, order, acc, inverse, counts, *refs):
    got, total, outs = refs[:offsets], refs[offsets], refs[offsets + 1 : -2]
    product, stage = refs[-2:]
    size = acc.shape[1]
    total[...] = acc[...]
    for s in range(offsets):

        def multiply(t, carry, s=s):
            product[t] = dot(counts[(s + 1) * slots + t], got[s][t], NT)
            return carry

        def add(t, carry, s=s):
            at = pl.multiple_of(rows[s + 1, t] * tile, tile)
            total[pl.ds(at, tile), :] += product[t]
            return carry

        lax.fori_loop(0, slots, multiply, 0, unroll=4)
        lax.fori_loop(0, slots, add, 0)

    def scale(r, carry):
        at = pl.multiple_of(r * tile, tile)
        total[pl.ds(at, tile), :] = total[pl.ds(at, tile), :] * inverse[pl.ds(at, tile), :size]
        return carry

    lax.fori_loop(0, total.shape[0] // tile, scale, 0, unroll=2)
    for i, out in enumerate(outs):
        pick(order, bases[i], total, stage, out)


def gather_far(acc, inverse, bases, rows, order, counts, got, share, ranks):
    nodes, size = acc.shape
    slots, tile = rows.shape[1], counts.shape[-1]
    piece = jax.ShapeDtypeStruct((size, share), jnp.bfloat16)
    outs = call(
        functools.partial(far_kernel, len(got), slots, tile),
        "gather_far",
        [bases, rows, order],
        [acc, inverse, counts, *got],
        [jax.ShapeDtypeStruct((nodes, size), jnp.float32)] + [piece] * ranks,
        [((slots, tile, size), jnp.float32), ((CHUNK, size), jnp.float32)],
    )
    return outs[0], outs[1:]


def near_kernel(skip, bases, order, total, *refs):
    outs, stage = refs[:-1], refs[-1]
    for i, out in enumerate(outs):
        pick(order, bases[skip + i], total, stage, out)


def gather_near(total, bases, order, share, skip, ranks):
    size = total.shape[1]
    return call(
        functools.partial(near_kernel, skip),
        "gather_near",
        [bases, order],
        [total],
        [jax.ShapeDtypeStruct((size, share), jnp.bfloat16)] * ranks,
        [((CHUNK, size), jnp.float32)],
    )


def mix_kernel(places, starts, weight, bias, *refs):
    pieces, out, nodes = refs[:-2], refs[-2], refs[-1]
    for piece, (i, low) in zip(pieces, places):
        at = pl.multiple_of(starts[i] + low, 16)
        nodes[pl.ds(at, piece.shape[0]), :] = piece[...]
    mixed = dot(weight[...], nodes[...], NN)
    out[...] = jnp.maximum(mixed + bias[...], 0.0).astype(out.dtype)


def mix(starts, weight, bias, pieces, places):
    hidden, width = weight.shape
    nodes = pieces[0].shape[1]
    step = min(512, nodes)
    return pl.pallas_call(
        functools.partial(mix_kernel, places),
        grid=(nodes // step,),
        out_shape=jax.ShapeDtypeStruct((hidden, nodes), jnp.bfloat16),
        in_specs=[
            SMEM,
            pl.BlockSpec(weight.shape, lambda i: (0, 0)),
            pl.BlockSpec(bias.shape, lambda i: (0, 0)),
        ]
        + [pl.BlockSpec((piece.shape[0], step), lambda i: (0, i)) for piece in pieces],
        out_specs=pl.BlockSpec((hidden, step), lambda i: (0, i)),
        scratch_shapes=[pltpu.VMEM((width, step), jnp.bfloat16)],
        compiler_params=pltpu.CompilerParams(vmem_limit_bytes=16 * 2**20),
        cost_estimate=pl.CostEstimate(
            flops=2 * hidden * width * nodes, bytes_accessed=5 * 2**20, transcendentals=0
        ),
        name="mix",
    )(starts, weight, bias, *pieces)


def on_device(features, tile_rows, tile_cols, tile_weights, order, weight, bias):
    width, nodes = features.shape
    _, blocks, slots, tile, _ = tile_weights.shape
    groups = lax.axis_size("grp")
    me = lax.axis_index("grp")
    share = nodes // groups
    ranges = cuts(width)
    rows = tile_rows.reshape(blocks, slots)
    cols = tile_cols.reshape(blocks, slots)
    counts = tile_weights.reshape(blocks * slots, tile, tile)

    asked = [shifted(cols, "blk", -s) for s in range(1, blocks)]
    got = []
    for low, size in ranges:
        sent = pack(features, asked, low, size, tile)
        asked = lax.optimization_barrier((*asked, sent[0]))[:-1]
        got.append([shifted(value, "blk", s + 1) for s, value in enumerate(sent)])

    ranks = list(range(groups - 1, -1, -1))
    whose = me ^ jnp.asarray(ranks, jnp.int32)
    bases = whose * share
    far = groups - 2

    accs, inverse = own(features, rows, cols, counts, ranges)
    pieces, places = [], []
    for p, (low, size) in enumerate(ranges):
        total, out_far = gather_far(
            accs[p], inverse, bases, rows, order, counts, got[p], share, far
        )
        near = gather_near(total, bases, order, share, far, groups - far)
        for i, (k, piece) in enumerate(zip(ranks, [*out_far, *near])):
            pieces.append(piece if k == 0 else traded(piece, "grp", k))
            places.append((i, low))
    return mix(whose * width, weight.T, bias[:, None], pieces, tuple(places))


def solution(mesh):
    in_specs = (
        P("grp", ("parts", "blk")),
        P(("parts", "blk"), None, None),
        P(("parts", "blk"), None, None),
        P(("parts", "blk"), None, None, None, None),
        P(("parts", "blk")),
        P(),
        P(),
    )
    out_specs = P(None, ("parts", "blk", "grp"))
    return jax.shard_map(
        on_device, mesh=mesh, in_specs=in_specs, out_specs=out_specs, check_vma=False
    )
```

```python
import functools

import jax
import jax.numpy as jnp
from jax import lax
from jax.experimental import pallas as pl
from jax.experimental.pallas import tpu as pltpu
from jax.sharding import PartitionSpec as P

NN = (((1,), (0,)), ((), ()))
NT = (((1,), (1,)), ((), ()))
VMEM = pl.BlockSpec(memory_space=pltpu.VMEM)
SMEM = pl.BlockSpec(memory_space=pltpu.SMEM)
CHUNK = 256
UNROLL = 64


def dot(a, b, dims):
    return lax.dot_general(a, b, dims, preferred_element_type=jnp.float32)


def padded(shape, dtype):
    rows = 1
    for extent in shape[:-1]:
        rows *= extent
    return rows * -(-shape[-1] // 128) * 128 * jnp.dtype(dtype).itemsize


def call(kernel, name, scalars, arrays, outs, scratch=(), moved=2**16):
    held = sum(padded(a.shape, a.dtype) for a in list(arrays) + list(outs))
    held += sum(padded(shape, dtype) for shape, dtype in scratch)
    return pl.pallas_call(
        kernel,
        out_shape=list(outs),
        in_specs=[SMEM] * len(scalars) + [VMEM] * len(arrays),
        out_specs=[VMEM] * len(outs),
        scratch_shapes=[pltpu.VMEM(shape, dtype) for shape, dtype in scratch],
        compiler_params=pltpu.CompilerParams(vmem_limit_bytes=held + 4 * 2**20),
        cost_estimate=pl.CostEstimate(flops=0, bytes_accessed=moved, transcendentals=0),
        name=name,
    )(*scalars, *arrays)


def shifted(value, axis, steps):
    count = lax.axis_size(axis)
    pairs = [(source, (source + steps) % count) for source in range(count)]
    return lax.ppermute(value, axis, pairs)


def traded(value, axis, k):
    return lax.ppermute(value, axis, [(i, i ^ k) for i in range(lax.axis_size(axis))])


def cuts(width):
    first = width // 2
    return ((0, first), (first, width - first))


def identity(size):
    row = lax.broadcasted_iota(jnp.int32, (size, size), 0)
    col = lax.broadcasted_iota(jnp.int32, (size, size), 1)
    return (row == col).astype(jnp.float32).astype(jnp.bfloat16)


def pack_kernel(low, size, offsets, slots, tile, *refs):
    asked, panel, outs = refs[:offsets], refs[offsets], refs[offsets + 1 :]
    for s in range(offsets):

        def body(t, carry, s=s):
            at = pl.multiple_of(asked[s][s + 1, t] * tile, tile)
            outs[s][t] = panel[pl.ds(low, size), pl.ds(at, tile)]
            return carry

        lax.fori_loop(0, slots, body, 0, unroll=4)


def pack(panel, asked, low, size, tile):
    offsets, slots = len(asked), asked[0].shape[1]
    shape = jax.ShapeDtypeStruct((slots, size, tile), panel.dtype)
    return call(
        functools.partial(pack_kernel, low, size, offsets, slots, tile),
        "pack",
        asked,
        [panel],
        [shape] * offsets,
    )


def degree_kernel(blocks, slots, tile, rows, counts, inverse, product):
    lanes = inverse.shape[1]
    row_tiles = inverse.shape[0] // tile
    ones = jnp.ones((tile, lanes), jnp.bfloat16)
    inverse[...] = jnp.ones(inverse.shape, jnp.float32)

    def block(s, carry):
        def multiply(t, inner):
            product[t] = dot(counts[s * slots + t], ones, NN)
            return inner

        def add(t, inner):
            at = pl.multiple_of(rows[s, t] * tile, tile)
            inverse[pl.ds(at, tile), :] += product[t]
            return inner

        lax.fori_loop(0, slots, multiply, 0, unroll=10)
        lax.fori_loop(0, slots, add, 0)
        return carry

    lax.fori_loop(0, blocks, block, 0)

    def invert(r, carry):
        at = pl.multiple_of(r * tile, tile)
        inverse[pl.ds(at, tile), :] = 1.0 / inverse[pl.ds(at, tile), :]
        return carry

    lax.fori_loop(0, row_tiles, invert, 0, unroll=2)


def degrees(rows, counts, nodes, lanes):
    blocks, slots = rows.shape
    tile = counts.shape[-1]
    return call(
        functools.partial(degree_kernel, blocks, slots, tile),
        "degrees",
        [rows],
        [counts],
        [jax.ShapeDtypeStruct((nodes, lanes), jnp.float32)],
        [((slots, tile, lanes), jnp.float32)],
    )[0]


def own_kernel(ranges, slots, tile, rows, cols, panel, counts, inverse, *refs):
    accs, product = refs[:-1], refs[-1]
    row_tiles = panel.shape[1] // tile
    eye = identity(tile)

    def start(r, carry):
        at = pl.multiple_of(r * tile, tile)
        for acc, (low, size) in zip(accs, ranges):
            here = dot(eye, panel[pl.ds(low, size), pl.ds(at, tile)], NT)
            acc[pl.ds(at, tile), :] = here * inverse[pl.ds(at, tile), :size]
        return carry

    lax.fori_loop(0, row_tiles, start, 0, unroll=4)

    for acc, (low, size) in zip(accs, ranges):

        def multiply(t, carry, low=low, size=size):
            col = pl.multiple_of(cols[0, t] * tile, tile)
            product[t, :, :size] = dot(counts[t], panel[pl.ds(low, size), pl.ds(col, tile)], NT)
            return carry

        def add(t, carry, acc=acc, size=size):
            at = pl.multiple_of(rows[0, t] * tile, tile)
            acc[pl.ds(at, tile), :] += product[t, :, :size] * inverse[pl.ds(at, tile), :size]
            return carry

        lax.fori_loop(0, slots, multiply, 0, unroll=10)
        lax.fori_loop(0, slots, add, 0)


def own(panel, rows, cols, counts, inverse, ranges):
    slots = rows.shape[1]
    nodes, tile = panel.shape[1], counts.shape[-1]
    lanes = max(size for _, size in ranges)
    return call(
        functools.partial(own_kernel, ranges, slots, tile),
        "own",
        [rows, cols],
        [panel, counts, inverse],
        [jax.ShapeDtypeStruct((nodes, size), jnp.float32) for _, size in ranges],
        [((slots, tile, lanes), jnp.float32)],
    )


def pick(order, base, nodes, stage, outs):
    count, size = stage.shape
    eye = identity(size)

    def group(i, carry):
        at = pl.multiple_of(i * UNROLL, UNROLL)
        for u in range(UNROLL):
            source = order[base + at + u]
            stage[pl.ds(at + u, 1), :] = nodes[pl.ds(source, 1), :]
        return carry

    lax.fori_loop(0, count // UNROLL, group, 0)

    def turn(c, carry):
        at = pl.multiple_of(c * CHUNK, CHUNK)
        turned = dot(eye, stage[pl.ds(at, CHUNK), :].astype(jnp.bfloat16), NT)
        low = 0
        for out in outs:
            out[:, pl.ds(at, CHUNK)] = turned[low : low + out.shape[0]].astype(out.dtype)
            low += out.shape[0]
        return carry

    lax.fori_loop(0, count // CHUNK, turn, 0, unroll=4)


def far_kernel(offsets, slots, tile, bases, rows, order, acc, inverse, counts, *refs):
    got, total, outs = refs[:offsets], refs[offsets], refs[offsets + 1 : -2]
    product, stage = refs[-2:]
    size = acc.shape[1]
    total[...] = acc[...]
    for s in range(offsets):

        def multiply(t, carry, s=s):
            product[t] = dot(counts[(s + 1) * slots + t], got[s][t], NT)
            return carry

        def add(t, carry, s=s):
            at = pl.multiple_of(rows[s + 1, t] * tile, tile)
            total[pl.ds(at, tile), :] += product[t] * inverse[pl.ds(at, tile), :size]
            return carry

        lax.fori_loop(0, slots, multiply, 0, unroll=10)
        lax.fori_loop(0, slots, add, 0)

    for i, out in enumerate(outs):
        pick(order, bases[i], total, stage, [out])


def gather_far(acc, inverse, bases, rows, order, counts, got, share, ranks):
    nodes, size = acc.shape
    slots, tile = rows.shape[1], counts.shape[-1]
    piece = jax.ShapeDtypeStruct((size, share), jnp.bfloat16)
    outs = call(
        functools.partial(far_kernel, len(got), slots, tile),
        "gather_far",
        [bases, rows, order],
        [acc, inverse, counts, *got],
        [jax.ShapeDtypeStruct((nodes, size), jnp.float32)] + [piece] * ranks,
        [((slots, tile, size), jnp.float32), ((share, size), jnp.float32)],
    )
    return outs[0], outs[1:]


def near_kernel(rank, bases, order, total, *refs):
    pick(order, bases[rank], total, refs[-1], refs[:-1])


def gather_near(total, bases, order, share, rank, heights, moved):
    return call(
        functools.partial(near_kernel, rank),
        "gather_near",
        [bases, order],
        [total],
        [jax.ShapeDtypeStruct((height, share), jnp.bfloat16) for height in heights],
        [((share, total.shape[1]), jnp.float32)],
        moved,
    )


def mix_kernel(places, starts, weight, bias, *refs):
    pieces, out, nodes = refs[:-2], refs[-2], refs[-1]
    for piece, (i, low) in zip(pieces, places):
        at = pl.multiple_of(starts[i] + low, 16)
        nodes[pl.ds(at, piece.shape[0]), :] = piece[...]
    mixed = dot(weight[...], nodes[...], NN)
    out[...] = jnp.maximum(mixed + bias[...], 0.0).astype(out.dtype)


def mix(starts, weight, bias, placed):
    places, pieces = tuple(placed), list(placed.values())
    hidden, width = weight.shape
    nodes = pieces[0].shape[1]
    step = min(512, nodes)
    return pl.pallas_call(
        functools.partial(mix_kernel, places),
        grid=(nodes // step,),
        out_shape=jax.ShapeDtypeStruct((hidden, nodes), jnp.bfloat16),
        in_specs=[
            SMEM,
            pl.BlockSpec(weight.shape, lambda i: (0, 0)),
            pl.BlockSpec(bias.shape, lambda i: (0, 0)),
        ]
        + [pl.BlockSpec((piece.shape[0], step), lambda i: (0, i)) for piece in pieces],
        out_specs=pl.BlockSpec((hidden, step), lambda i: (0, i)),
        scratch_shapes=[pltpu.VMEM((width, step), jnp.bfloat16)],
        compiler_params=pltpu.CompilerParams(vmem_limit_bytes=16 * 2**20),
        cost_estimate=pl.CostEstimate(
            flops=2 * hidden * width * nodes, bytes_accessed=5 * 2**20, transcendentals=0
        ),
        name="mix",
    )(starts, weight, bias, *pieces)


def on_device(features, tile_rows, tile_cols, tile_weights, order, weight, bias):
    width, nodes = features.shape
    _, blocks, slots, tile, _ = tile_weights.shape
    groups = lax.axis_size("grp")
    me = lax.axis_index("grp")
    share = nodes // groups
    ranges = cuts(width)
    rows = tile_rows.reshape(blocks, slots)
    cols = tile_cols.reshape(blocks, slots)
    counts = tile_weights.reshape(blocks * slots, tile, tile)

    ranks = list(range(groups - 1, -1, -1))
    whose = me ^ jnp.asarray(ranks, jnp.int32)
    bases = whose * share
    far = groups - 2

    asked = [shifted(cols, "blk", -s) for s in range(1, blocks)]
    inverse = degrees(rows, counts, nodes, max(size for _, size in ranges))
    *asked, inverse = lax.optimization_barrier((*asked, inverse))
    sent = []
    for low, size in ranges:
        sent.append(list(pack(features, asked, low, size, tile)))
        *asked, sent[-1][0] = lax.optimization_barrier((*asked, sent[-1][0]))
    accs = list(own(features, rows, cols, counts, inverse, ranges))

    got = [[shifted(value, "blk", s + 1) for s, value in enumerate(sent[0])]]
    for later in sent[1:]:
        tied = [lax.optimization_barrier((a, b, accs)) for a, b in zip(later, got[-1])]
        got[-1] = [b for _, b, _ in tied]
        got.append([shifted(a, "blk", s + 1) for s, (a, _, _) in enumerate(tied)])

    pieces, waits = {}, {}
    for p, (low, size) in enumerate(ranges):
        last = p == len(ranges) - 1
        acc, waits = lax.optimization_barrier((accs[p], waits))
        pieces.update(waits)
        total, out_far = gather_far(
            acc, inverse, bases, rows, order, counts, got[p], share, far
        )
        waits = {
            (i, low): traded(piece, "grp", ranks[i]) for i, piece in enumerate(out_far)
        }
        waits[far + 1, low] = gather_near(
            total, bases, order, share, far + 1, (size,), 2**16
        )[0]
        half = size // 32 * 16
        heights = (half, size - half) if last else (size,)
        moved = 2**24 if last else 2**16
        for piece in gather_near(total, bases, order, share, far, heights, moved):
            pieces[far, low] = traded(piece, "grp", 1)
            low += piece.shape[0]
    pieces.update(waits)
    return mix(whose * width, weight.T, bias[:, None], pieces)


def solution(mesh):
    in_specs = (
        P("grp", ("parts", "blk")),
        P(("parts", "blk"), None, None),
        P(("parts", "blk"), None, None),
        P(("parts", "blk"), None, None, None, None),
        P(("parts", "blk")),
        P(),
        P(),
    )
    out_specs = P(None, ("parts", "blk", "grp"))
    return jax.shard_map(
        on_device, mesh=mesh, in_specs=in_specs, out_specs=out_specs, check_vma=False
    )
```

```python
import functools

import jax
import jax.numpy as jnp
from jax import lax
from jax.experimental import pallas as pl
from jax.experimental.pallas import tpu as pltpu
from jax.sharding import PartitionSpec as P

NN = (((1,), (0,)), ((), ()))
NT = (((1,), (1,)), ((), ()))
VMEM = pl.BlockSpec(memory_space=pltpu.VMEM)
SMEM = pl.BlockSpec(memory_space=pltpu.SMEM)
CHUNK = 256
UNROLL = 64


def dot(a, b, dims):
    return lax.dot_general(a, b, dims, preferred_element_type=jnp.float32)


def padded(shape, dtype):
    rows = 1
    for extent in shape[:-1]:
        rows *= extent
    return rows * -(-shape[-1] // 128) * 128 * jnp.dtype(dtype).itemsize


def call(kernel, name, scalars, arrays, outs, scratch=(), moved=2**16):
    held = sum(padded(a.shape, a.dtype) for a in list(arrays) + list(outs))
    held += sum(padded(shape, dtype) for shape, dtype in scratch)
    return pl.pallas_call(
        kernel,
        out_shape=list(outs),
        in_specs=[SMEM] * len(scalars) + [VMEM] * len(arrays),
        out_specs=[VMEM] * len(outs),
        scratch_shapes=[pltpu.VMEM(shape, dtype) for shape, dtype in scratch],
        compiler_params=pltpu.CompilerParams(vmem_limit_bytes=held + 4 * 2**20),
        cost_estimate=pl.CostEstimate(flops=0, bytes_accessed=moved, transcendentals=0),
        name=name,
    )(*scalars, *arrays)


def shifted(value, axis, steps):
    count = lax.axis_size(axis)
    pairs = [(source, (source + steps) % count) for source in range(count)]
    return lax.ppermute(value, axis, pairs)


def traded(value, axis, k):
    return lax.ppermute(value, axis, [(i, i ^ k) for i in range(lax.axis_size(axis))])


def cuts(width):
    first = width * 5 // 8 // 16 * 16
    return ((0, first), (first, width - first))


def identity(size):
    row = lax.broadcasted_iota(jnp.int32, (size, size), 0)
    col = lax.broadcasted_iota(jnp.int32, (size, size), 1)
    return (row == col).astype(jnp.float32).astype(jnp.bfloat16)


def stage_kernel(panel, bias, out, column):
    out[...] = panel[...]
    column[...] = jnp.broadcast_to(bias[...], column.shape[::-1]).T


def staged(panel, bias):
    return call(
        stage_kernel,
        "stage",
        [],
        [panel, bias[None, :]],
        [
            jax.ShapeDtypeStruct(panel.shape, panel.dtype),
            jax.ShapeDtypeStruct((bias.shape[0], 128), bias.dtype),
        ],
    )


def pack_kernel(low, size, offsets, slots, tile, *refs):
    asked, panel, outs = refs[:offsets], refs[offsets], refs[offsets + 1 :]
    for s in range(offsets):

        def body(t, carry, s=s):
            at = pl.multiple_of(asked[s][s + 1, t] * tile, tile)
            outs[s][t] = panel[pl.ds(low, size), pl.ds(at, tile)]
            return carry

        lax.fori_loop(0, slots, body, 0, unroll=4)


def pack(panel, asked, low, size, tile):
    offsets, slots = len(asked), asked[0].shape[1]
    shape = jax.ShapeDtypeStruct((slots, size, tile), panel.dtype)
    return call(
        functools.partial(pack_kernel, low, size, offsets, slots, tile),
        "pack",
        asked,
        [panel],
        [shape] * offsets,
    )


def degree_kernel(blocks, slots, tile, rows, counts, inverse, product):
    lanes = inverse.shape[1]
    row_tiles = inverse.shape[0] // tile
    ones = jnp.ones((tile, lanes), jnp.bfloat16)
    inverse[...] = jnp.ones(inverse.shape, jnp.float32)

    def block(s, carry):
        def multiply(t, inner):
            product[t] = dot(counts[s * slots + t], ones, NN)
            return inner

        def add(t, inner):
            at = pl.multiple_of(rows[s, t] * tile, tile)
            inverse[pl.ds(at, tile), :] += product[t]
            return inner

        lax.fori_loop(0, slots, multiply, 0, unroll=10)
        lax.fori_loop(0, slots, add, 0)
        return carry

    lax.fori_loop(0, blocks, block, 0)

    def invert(r, carry):
        at = pl.multiple_of(r * tile, tile)
        inverse[pl.ds(at, tile), :] = 1.0 / inverse[pl.ds(at, tile), :]
        return carry

    lax.fori_loop(0, row_tiles, invert, 0, unroll=2)


def degrees(rows, counts, nodes, lanes):
    blocks, slots = rows.shape
    tile = counts.shape[-1]
    return call(
        functools.partial(degree_kernel, blocks, slots, tile),
        "degrees",
        [rows],
        [counts],
        [jax.ShapeDtypeStruct((nodes, lanes), jnp.float32)],
        [((slots, tile, lanes), jnp.float32)],
    )[0]


def own_kernel(ranges, slots, tile, rows, cols, panel, counts, inverse, *refs):
    accs, product = refs[:-1], refs[-1]
    row_tiles = panel.shape[1] // tile
    eye = identity(tile)

    def start(r, carry):
        at = pl.multiple_of(r * tile, tile)
        for acc, (low, size) in zip(accs, ranges):
            here = dot(eye, panel[pl.ds(low, size), pl.ds(at, tile)], NT)
            acc[pl.ds(at, tile), :] = here * inverse[pl.ds(at, tile), :size]
        return carry

    lax.fori_loop(0, row_tiles, start, 0, unroll=4)

    for acc, (low, size) in zip(accs, ranges):

        def multiply(t, carry, low=low, size=size):
            col = pl.multiple_of(cols[0, t] * tile, tile)
            product[t, :, :size] = dot(counts[t], panel[pl.ds(low, size), pl.ds(col, tile)], NT)
            return carry

        def add(t, carry, acc=acc, size=size):
            at = pl.multiple_of(rows[0, t] * tile, tile)
            acc[pl.ds(at, tile), :] += product[t, :, :size] * inverse[pl.ds(at, tile), :size]
            return carry

        lax.fori_loop(0, slots, multiply, 0, unroll=10)
        lax.fori_loop(0, slots, add, 0)


def own(panel, rows, cols, counts, inverse, ranges):
    slots = rows.shape[1]
    nodes, tile = panel.shape[1], counts.shape[-1]
    lanes = max(size for _, size in ranges)
    return call(
        functools.partial(own_kernel, ranges, slots, tile),
        "own",
        [rows, cols],
        [panel, counts, inverse],
        [jax.ShapeDtypeStruct((nodes, size), jnp.float32) for _, size in ranges],
        [((slots, tile, lanes), jnp.float32)],
    )


def pick(order, base, nodes, stage, outs):
    count, size = stage.shape
    eye = identity(size)

    def group(i, carry):
        at = pl.multiple_of(i * UNROLL, UNROLL)
        for u in range(UNROLL):
            source = order[base + at + u]
            stage[pl.ds(at + u, 1), :] = nodes[pl.ds(source, 1), :]
        return carry

    lax.fori_loop(0, count // UNROLL, group, 0)
    first = 0
    for out in outs:
        columns = out.shape[1]
        for at in range(0, columns, CHUNK):
            chunk = stage[pl.ds(first + at, CHUNK), :].astype(jnp.bfloat16)
            out[:, pl.ds(at, CHUNK)] = dot(eye, chunk, NT).astype(out.dtype)
        first += columns


def first_kernel(offsets, slots, tile, bases, rows, order, acc, inverse, counts, *refs):
    got, total, out, product, stage = refs[:offsets], *refs[offsets:]
    size = acc.shape[1]
    total[...] = acc[...]
    for s in range(offsets):

        def multiply(t, carry, s=s):
            product[t] = dot(counts[(s + 1) * slots + t], got[s][t], NT)
            return carry

        def add(t, carry, s=s):
            at = pl.multiple_of(rows[s + 1, t] * tile, tile)
            total[pl.ds(at, tile), :] += product[t] * inverse[pl.ds(at, tile), :size]
            return carry

        lax.fori_loop(0, slots, multiply, 0, unroll=10)
        lax.fori_loop(0, slots, add, 0)
    pick(order, bases[0], total, stage, [out])


def gather_first(acc, inverse, bases, rows, order, counts, got, share):
    nodes, size = acc.shape
    slots, tile = rows.shape[1], counts.shape[-1]
    return call(
        functools.partial(first_kernel, len(got), slots, tile),
        "gather_first",
        [bases, rows, order],
        [acc, inverse, counts, *got],
        [
            jax.ShapeDtypeStruct((nodes, size), jnp.float32),
            jax.ShapeDtypeStruct((size, share), jnp.bfloat16),
        ],
        [((slots, tile, size), jnp.float32), ((share, size), jnp.float32)],
        2**22,
    )


def next_kernel(rank, bases, order, total, *refs):
    pick(order, bases[rank], total, refs[-1], refs[:-1])


def gather_next(total, bases, order, rank, widths):
    size = total.shape[1]
    return call(
        functools.partial(next_kernel, rank),
        "gather_next",
        [bases, order],
        [total],
        [jax.ShapeDtypeStruct((size, width), jnp.bfloat16) for width in widths],
        [((sum(widths), size), jnp.float32)],
    )


def mix_kernel(places, starts, weight, bias, *refs):
    pieces, (out, nodes, ready, sems) = refs[:-4], refs[-4:]
    for piece, (i, low, first) in zip(pieces, places):
        height, columns = piece.shape
        at = pl.multiple_of(starts[i] + low, 16)
        nodes[pl.ds(at, height), pl.ds(first, columns)] = piece[...]
    copies = []
    for c in range(ready.shape[0]):
        step = ready.shape[2]
        mixed = dot(weight[...], nodes[:, pl.ds(c * step, step)], NN)
        ready[c] = jnp.maximum(mixed + bias[:, :1], 0.0).astype(out.dtype)
        copies.append(
            pltpu.make_async_copy(ready.at[c], out.at[:, pl.ds(c * step, step)], sems.at[c])
        )
        copies[-1].start()
    for copy in copies:
        copy.wait()


def mix(starts, weight, bias, placed, nodes):
    places, pieces = tuple(placed), list(placed.values())
    hidden, width = weight.shape
    step = min(512, nodes)
    return pl.pallas_call(
        functools.partial(mix_kernel, places),
        out_shape=jax.ShapeDtypeStruct((hidden, nodes), jnp.bfloat16),
        in_specs=[SMEM] + [VMEM] * (2 + len(pieces)),
        out_specs=pl.BlockSpec(memory_space=pl.ANY),
        scratch_shapes=[
            pltpu.VMEM((width, nodes), jnp.bfloat16),
            pltpu.VMEM((nodes // step, hidden, step), jnp.bfloat16),
            pltpu.SemaphoreType.DMA((nodes // step,)),
        ],
        compiler_params=pltpu.CompilerParams(vmem_limit_bytes=16 * 2**20),
        cost_estimate=pl.CostEstimate(
            flops=2 * hidden * width * nodes, bytes_accessed=5 * 2**20, transcendentals=0
        ),
        name="mix",
    )(starts, weight, bias, *pieces)


def on_device(features, tile_rows, tile_cols, tile_weights, order, weight, bias):
    width, nodes = features.shape
    _, blocks, slots, tile, _ = tile_weights.shape
    groups = lax.axis_size("grp")
    me = lax.axis_index("grp")
    share = nodes // groups
    ranges = cuts(width)
    rows = tile_rows.reshape(blocks, slots)
    cols = tile_cols.reshape(blocks, slots)
    counts = tile_weights.reshape(blocks * slots, tile, tile)

    ranks = list(range(groups - 1, -1, -1))
    whose = me ^ jnp.asarray(ranks, jnp.int32)
    bases = whose * share
    far = groups - 2

    asked = [shifted(cols, "blk", -s) for s in range(1, blocks)]
    *asked, panel, column = lax.optimization_barrier((*asked, *staged(features, bias)))
    sent = []
    for low, size in ranges:
        sent.append(list(pack(panel, asked, low, size, tile)))
        *asked, sent[-1][0] = lax.optimization_barrier((*asked, sent[-1][0]))
    inverse = degrees(rows, counts, nodes, max(size for _, size in ranges))
    accs = own(panel, rows, cols, counts, inverse, ranges)
    accs, across = lax.optimization_barrier((accs, weight.T))

    got = [[shifted(value, "blk", s + 1) for s, value in enumerate(sent[0])]]
    for later in sent[1:]:
        tied = [lax.optimization_barrier((a, b, accs)) for a, b in zip(later, got[-1])]
        got[-1] = [b for _, b, _ in tied]
        got.append([shifted(a, "blk", s + 1) for s, (a, _, _) in enumerate(tied)])

    pieces, waits, kept = {}, {}, {}
    for p, (low, size) in enumerate(ranges):
        last = p == len(ranges) - 1
        acc, kept = lax.optimization_barrier((accs[p], kept))
        pieces.update(kept)
        total, piece = gather_first(acc, inverse, bases, rows, order, counts, got[p], share)
        now = {(0, low, 0): traded(piece, "grp", ranks[0])}
        for i in range(1, groups - 1):
            widths = (share,)
            if last and i == far:
                total, waits = lax.optimization_barrier((total, waits))
                pieces.update(waits)
                widths = (share // 2, share // 2)
            elif last and i == far - 1:
                widths = (share // 4 * 3, share // 4)
            first = 0
            for piece in gather_next(total, bases, order, i, widths):
                if i == far and not last:
                    piece, got[p + 1][0] = lax.optimization_barrier((piece, got[p + 1][0]))
                now[i, low, first] = traded(piece, "grp", ranks[i])
                first += piece.shape[1]
        kept = {(groups - 1, low, 0): gather_next(total, bases, order, groups - 1, (share,))[0]}
        waits = now
    pieces.update(waits)
    pieces.update(kept)
    return mix(whose * width, across, column, pieces, share)


def solution(mesh):
    in_specs = (
        P("grp", ("parts", "blk")),
        P(("parts", "blk"), None, None),
        P(("parts", "blk"), None, None),
        P(("parts", "blk"), None, None, None, None),
        P(("parts", "blk")),
        P(),
        P(),
    )
    out_specs = P(None, ("parts", "blk", "grp"))
    return jax.shard_map(
        on_device, mesh=mesh, in_specs=in_specs, out_specs=out_specs, check_vma=False
    )
```

```python
import functools

import jax
import jax.numpy as jnp
from jax import lax
from jax.experimental import pallas as pl
from jax.experimental.pallas import tpu as pltpu
from jax.sharding import PartitionSpec as P

NN = (((1,), (0,)), ((), ()))
NT = (((1,), (1,)), ((), ()))
VMEM = pl.BlockSpec(memory_space=pltpu.VMEM)
SMEM = pl.BlockSpec(memory_space=pltpu.SMEM)
ANY = pl.BlockSpec(memory_space=pl.ANY)
CHUNK = 256
UNROLL = 64


def dot(a, b, dims):
    return lax.dot_general(a, b, dims, preferred_element_type=jnp.float32)


def padded(shape, dtype):
    rows = 1
    for extent in shape[:-1]:
        rows *= extent
    return rows * -(-shape[-1] // 128) * 128 * jnp.dtype(dtype).itemsize


def call(kernel, name, scalars, arrays, outs, scratch=(), moved=2**16):
    held = sum(padded(a.shape, a.dtype) for a in list(arrays) + list(outs))
    held += sum(padded(shape, dtype) for shape, dtype in scratch)
    return pl.pallas_call(
        kernel,
        out_shape=list(outs),
        in_specs=[SMEM] * len(scalars) + [VMEM] * len(arrays),
        out_specs=[VMEM] * len(outs),
        scratch_shapes=[pltpu.VMEM(shape, dtype) for shape, dtype in scratch],
        compiler_params=pltpu.CompilerParams(vmem_limit_bytes=held + 2**20),
        cost_estimate=pl.CostEstimate(flops=0, bytes_accessed=moved, transcendentals=0),
        name=name,
    )(*scalars, *arrays)


def shifted(value, axis, steps):
    count = lax.axis_size(axis)
    pairs = [(source, (source + steps) % count) for source in range(count)]
    return lax.ppermute(value, axis, pairs)


def traded(value, axis, k):
    return lax.ppermute(value, axis, [(i, i ^ k) for i in range(lax.axis_size(axis))])


def cuts(width):
    first = width * 5 // 8 // 16 * 16
    return ((0, first), (first, width - first))


def identity(size):
    row = lax.broadcasted_iota(jnp.int32, (size, size), 0)
    col = lax.broadcasted_iota(jnp.int32, (size, size), 1)
    return (row == col).astype(jnp.float32).astype(jnp.bfloat16)


def stage_kernel(panel, out):
    out[...] = panel[...]


def staged(panel):
    shape = jax.ShapeDtypeStruct(panel.shape, panel.dtype)
    return call(stage_kernel, "stage", [], [panel], [shape])[0]


def pack_kernel(low, size, offsets, slots, tile, *refs):
    asked, panel = refs[:offsets], refs[offsets]
    outs, sems = refs[offsets + 1 : -1], refs[-1]
    for s in range(offsets):

        def body(t, carry, s=s):
            at = pl.multiple_of(asked[s][s + 1, t] * tile, tile)
            pltpu.make_async_copy(
                panel.at[pl.ds(low, size), pl.ds(at, tile)], outs[s].at[t], sems.at[s]
            ).start()
            return carry

        lax.fori_loop(0, slots, body, 0, unroll=4)
    for s in range(offsets):
        pltpu.make_async_copy(outs[s], outs[s], sems.at[s]).wait()


def pack(panel, asked, low, size, tile):
    offsets, slots = len(asked), asked[0].shape[1]
    return pl.pallas_call(
        functools.partial(pack_kernel, low, size, offsets, slots, tile),
        out_shape=[jax.ShapeDtypeStruct((slots, size, tile), panel.dtype)] * offsets,
        in_specs=[SMEM] * offsets + [ANY],
        out_specs=[ANY] * offsets,
        scratch_shapes=[pltpu.SemaphoreType.DMA((offsets,))],
        compiler_params=pltpu.CompilerParams(vmem_limit_bytes=2**20),
        cost_estimate=pl.CostEstimate(flops=0, bytes_accessed=2**16, transcendentals=0),
        name="pack",
    )(*asked, panel)


def own_kernel(ranges, blocks, slots, tile, rows, cols, panel, counts, bias, *refs):
    accs, (column, inverse, product) = refs[:-3], refs[-3:]
    lanes = inverse.shape[1]
    row_tiles = panel.shape[1] // tile
    eye = identity(tile)
    ones = jnp.ones((tile, lanes), jnp.bfloat16)
    column[...] = jnp.broadcast_to(bias[...], column.shape[::-1]).T
    inverse[...] = jnp.ones(inverse.shape, jnp.float32)

    def block(s, carry):
        def multiply(t, inner):
            product[t] = dot(counts[s * slots + t], ones, NN)
            return inner

        def add(t, inner):
            at = pl.multiple_of(rows[s, t] * tile, tile)
            inverse[pl.ds(at, tile), :] += product[t]
            return inner

        lax.fori_loop(0, slots, multiply, 0, unroll=10)
        lax.fori_loop(0, slots, add, 0)
        return carry

    lax.fori_loop(0, blocks, block, 0)

    def start(r, carry):
        at = pl.multiple_of(r * tile, tile)
        scale = 1.0 / inverse[pl.ds(at, tile), :]
        inverse[pl.ds(at, tile), :] = scale
        for acc, (low, size) in zip(accs, ranges):
            here = dot(eye, panel[pl.ds(low, size), pl.ds(at, tile)], NT)
            acc[pl.ds(at, tile), pl.ds(0, size)] = here * scale[:, :size]
            acc[pl.ds(at, tile), pl.ds(size, 1)] = scale[:, :1]
        return carry

    lax.fori_loop(0, row_tiles, start, 0, unroll=4)

    for acc, (low, size) in zip(accs, ranges):

        def multiply(t, carry, low=low, size=size):
            col = pl.multiple_of(cols[0, t] * tile, tile)
            product[t, :, :size] = dot(counts[t], panel[pl.ds(low, size), pl.ds(col, tile)], NT)
            return carry

        def add(t, carry, acc=acc, size=size):
            at = pl.multiple_of(rows[0, t] * tile, tile)
            acc[pl.ds(at, tile), pl.ds(0, size)] += (
                product[t, :, :size] * inverse[pl.ds(at, tile), :size]
            )
            return carry

        lax.fori_loop(0, slots, multiply, 0, unroll=10)
        lax.fori_loop(0, slots, add, 0)


def own(panel, rows, cols, counts, bias, ranges):
    blocks, slots = rows.shape
    nodes, tile = panel.shape[1], counts.shape[-1]
    lanes = max(size for _, size in ranges)
    shapes = [jax.ShapeDtypeStruct((nodes, size + 1), jnp.float32) for _, size in ranges]
    shapes.append(jax.ShapeDtypeStruct((bias.shape[0], 128), bias.dtype))
    outs = call(
        functools.partial(own_kernel, ranges, blocks, slots, tile),
        "own",
        [rows, cols],
        [panel, counts, bias[None, :]],
        shapes,
        [((nodes, lanes), jnp.float32), ((slots, tile, lanes), jnp.float32)],
    )
    return outs[:-1], outs[-1]


def pick(order, nodes, stage, outs):
    count, size = stage.shape
    eye = identity(size)

    def group(i, carry):
        at = pl.multiple_of(i * UNROLL, UNROLL)
        for u in range(UNROLL):
            source = order[at + u]
            stage[pl.ds(at + u, 1), :] = nodes[pl.ds(source, 1), :]
        return carry

    lax.fori_loop(0, count // UNROLL, group, 0)
    first = 0
    for out in outs:
        columns = out.shape[1]
        for at in range(0, columns, CHUNK):
            chunk = stage[pl.ds(first + at, CHUNK), :].astype(jnp.bfloat16)
            out[:, pl.ds(at, CHUNK)] = dot(eye, chunk, NT).astype(out.dtype)
        first += columns


def far_kernel(offsets, slots, tile, far, rows, *refs):
    orders, acc, counts = refs[:far], refs[far], refs[far + 1]
    got, total = refs[far + 2 : far + 2 + offsets], refs[far + 2 + offsets]
    outs, (product, stage) = refs[far + 3 + offsets : -2], refs[-2:]
    size = total.shape[1]
    total[...] = acc[:, :size]
    for s in range(offsets):

        def multiply(t, carry, s=s):
            product[t] = dot(counts[(s + 1) * slots + t], got[s][t], NT)
            return carry

        def add(t, carry, s=s):
            at = pl.multiple_of(rows[s + 1, t] * tile, tile)
            total[pl.ds(at, tile), :] += product[t] * acc[pl.ds(at, tile), pl.ds(size, 1)]
            return carry

        lax.fori_loop(0, slots, multiply, 0, unroll=10)
        lax.fori_loop(0, slots, add, 0)
    for order, out in zip(orders, outs):
        pick(order, total, stage, [out])


def gather_far(acc, rows, orders, counts, got):
    nodes, size = acc.shape[0], acc.shape[1] - 1
    slots, tile = rows.shape[1], counts.shape[-1]
    share, far = orders[0].shape[0], len(orders)
    outs = call(
        functools.partial(far_kernel, len(got), slots, tile, far),
        "gather_far",
        [rows, *orders],
        [acc, counts, *got],
        [jax.ShapeDtypeStruct((nodes, size), jnp.float32)]
        + [jax.ShapeDtypeStruct((size, share), jnp.bfloat16)] * far,
        [((slots, tile, size), jnp.float32), ((share, size), jnp.float32)],
        2**22,
    )
    return outs[0], outs[1:]


def next_kernel(order, total, *refs):
    pick(order, total, refs[-1], refs[:-1])


def gather_next(total, order, widths):
    size = total.shape[1]
    return call(
        next_kernel,
        "gather_next",
        [order],
        [total],
        [jax.ShapeDtypeStruct((size, width), jnp.bfloat16) for width in widths],
        [((sum(widths), size), jnp.float32)],
    )


def mix_kernel(places, starts, weight, bias, *refs):
    pieces, (out, nodes, ready, sems) = refs[:-4], refs[-4:]
    for piece, (i, low, first) in zip(pieces, places):
        height, columns = piece.shape
        at = pl.multiple_of(starts[i] + low, 16)
        nodes[pl.ds(at, height), pl.ds(first, columns)] = piece[...]
    copies = []
    for c in range(ready.shape[0]):
        step = ready.shape[2]
        mixed = dot(weight[...], nodes[:, pl.ds(c * step, step)], NN)
        ready[c] = jnp.maximum(mixed + bias[:, :1], 0.0).astype(out.dtype)
        copies.append(
            pltpu.make_async_copy(ready.at[c], out.at[:, pl.ds(c * step, step)], sems.at[c])
        )
        copies[-1].start()
    for copy in copies:
        copy.wait()


def mix(starts, weight, bias, placed, nodes):
    places, pieces = tuple(placed), list(placed.values())
    hidden, width = weight.shape
    step = min(512, nodes)
    return pl.pallas_call(
        functools.partial(mix_kernel, places),
        out_shape=jax.ShapeDtypeStruct((hidden, nodes), jnp.bfloat16),
        in_specs=[SMEM] + [VMEM] * (2 + len(pieces)),
        out_specs=ANY,
        scratch_shapes=[
            pltpu.VMEM((width, nodes), jnp.bfloat16),
            pltpu.VMEM((nodes // step, hidden, step), jnp.bfloat16),
            pltpu.SemaphoreType.DMA((nodes // step,)),
        ],
        compiler_params=pltpu.CompilerParams(vmem_limit_bytes=16 * 2**20),
        cost_estimate=pl.CostEstimate(
            flops=2 * hidden * width * nodes, bytes_accessed=5 * 2**20, transcendentals=0
        ),
        name="mix",
    )(starts, weight, bias, *pieces)


def on_device(features, tile_rows, tile_cols, tile_weights, order, weight, bias):
    width, nodes = features.shape
    _, blocks, slots, tile, _ = tile_weights.shape
    groups = lax.axis_size("grp")
    me = lax.axis_index("grp")
    share = nodes // groups
    ranges = cuts(width)
    rows = tile_rows.reshape(blocks, slots)
    cols = tile_cols.reshape(blocks, slots)
    counts = tile_weights.reshape(blocks * slots, tile, tile)

    ranks = list(range(groups - 1, -1, -1))
    whose = me ^ jnp.asarray(ranks, jnp.int32)
    far = groups - 2
    picks = [lax.dynamic_slice(order, ((me ^ k) * share,), (share,)) for k in ranks]

    asked = [shifted(cols, "blk", -s) for s in range(1, blocks)]
    *asked, panel = lax.optimization_barrier((*asked, staged(features)))
    sent = []
    for low, size in ranges:
        source = features if sent else panel
        sent.append(list(pack(source, asked, low, size, tile)))
        *asked, sent[-1][0] = lax.optimization_barrier((*asked, sent[-1][0]))
    accs, column = own(features, rows, cols, counts, bias, ranges)
    accs, across, picks, starts = lax.optimization_barrier(
        (accs, weight.T, picks, whose * width)
    )

    got = [[shifted(value, "blk", s + 1) for s, value in enumerate(sent[0])]]
    for later in sent[1:]:
        later, got[-1], accs = lax.optimization_barrier((later, got[-1], accs))
        got.append([shifted(value, "blk", s + 1) for s, value in enumerate(later)])

    pieces, waits, kept = {}, {}, {}
    for p, (low, size) in enumerate(ranges):
        last = p == len(ranges) - 1
        acc, kept = lax.optimization_barrier((accs[p], kept))
        pieces.update(kept)
        total, out_far = gather_far(acc, rows, picks[:far], counts, got[p])
        now = {(i, low, 0): traded(piece, "grp", ranks[i]) for i, piece in enumerate(out_far)}
        widths = (share,)
        if not last:
            kept = gather_next(total, picks[-1], (share,))[0]
            total, kept = lax.optimization_barrier((total, kept))
        else:
            total, waits = lax.optimization_barrier((total, waits))
            pieces.update(waits)
            widths = (share // 2, share // 2)
        first = 0
        for piece in gather_next(total, picks[far], widths):
            if not last:
                piece, got[p + 1] = lax.optimization_barrier((piece, got[p + 1]))
            now[far, low, first] = traded(piece, "grp", ranks[far])
            first += piece.shape[1]
        if last:
            kept = gather_next(total, picks[-1], (share,))[0]
        kept = {(groups - 1, low, 0): kept}
        waits = now
    pieces.update(waits)
    pieces.update(kept)
    return mix(starts, across, column, pieces, share)


def solution(mesh):
    in_specs = (
        P("grp", ("parts", "blk")),
        P(("parts", "blk"), None, None),
        P(("parts", "blk"), None, None),
        P(("parts", "blk"), None, None, None, None),
        P(("parts", "blk")),
        P(),
        P(),
    )
    out_specs = P(None, ("parts", "blk", "grp"))
    return jax.shard_map(
        on_device, mesh=mesh, in_specs=in_specs, out_specs=out_specs, check_vma=False
    )
```

```python
import functools

import jax
import jax.numpy as jnp
from jax import lax
from jax.experimental import pallas as pl
from jax.experimental.pallas import tpu as pltpu
from jax.sharding import PartitionSpec as P

NN = (((1,), (0,)), ((), ()))
NT = (((1,), (1,)), ((), ()))
VMEM = pl.BlockSpec(memory_space=pltpu.VMEM)
SMEM = pl.BlockSpec(memory_space=pltpu.SMEM)
ANY = pl.BlockSpec(memory_space=pl.ANY)
CHUNK = 256
UNROLL = 64


def dot(a, b, dims):
    return lax.dot_general(a, b, dims, preferred_element_type=jnp.float32)


def padded(shape, dtype):
    rows = 1
    for extent in shape[:-1]:
        rows *= extent
    return rows * -(-shape[-1] // 128) * 128 * jnp.dtype(dtype).itemsize


def call(kernel, name, scalars, arrays, outs, scratch=(), moved=2**16):
    held = sum(padded(a.shape, a.dtype) for a in list(arrays) + list(outs))
    held += sum(padded(shape, dtype) for shape, dtype in scratch)
    return pl.pallas_call(
        kernel,
        out_shape=list(outs),
        in_specs=[SMEM] * len(scalars) + [VMEM] * len(arrays),
        out_specs=[VMEM] * len(outs),
        scratch_shapes=[pltpu.VMEM(shape, dtype) for shape, dtype in scratch],
        compiler_params=pltpu.CompilerParams(vmem_limit_bytes=held + 2**20),
        cost_estimate=pl.CostEstimate(flops=0, bytes_accessed=moved, transcendentals=0),
        name=name,
    )(*scalars, *arrays)


def shifted(value, axis, steps):
    count = lax.axis_size(axis)
    pairs = [(source, (source + steps) % count) for source in range(count)]
    return lax.ppermute(value, axis, pairs)


def traded(value, axis, k):
    return lax.ppermute(value, axis, [(i, i ^ k) for i in range(lax.axis_size(axis))])


def cuts(width):
    first = width * 3 // 4
    return ((0, first), (first, width - first))


def identity(size):
    row = lax.broadcasted_iota(jnp.int32, (size, size), 0)
    col = lax.broadcasted_iota(jnp.int32, (size, size), 1)
    return (row == col).astype(jnp.float32).astype(jnp.bfloat16)


def stage_kernel(panel, out):
    out[...] = panel[...]


def staged(panel):
    shape = jax.ShapeDtypeStruct(panel.shape, panel.dtype)
    return call(stage_kernel, "stage", [], [panel], [shape])[0]


def pack_kernel(low, size, offsets, slots, tile, *refs):
    asked, panel = refs[:offsets], refs[offsets]
    outs, sems = refs[offsets + 1 : -1], refs[-1]
    for s in range(offsets):

        def body(t, carry, s=s):
            at = pl.multiple_of(asked[s][s + 1, t] * tile, tile)
            pltpu.make_async_copy(
                panel.at[pl.ds(low, size), pl.ds(at, tile)], outs[s].at[t], sems.at[s]
            ).start()
            return carry

        lax.fori_loop(0, slots, body, 0, unroll=4)
    for s in range(offsets):
        pltpu.make_async_copy(outs[s], outs[s], sems.at[s]).wait()


def pack(panel, asked, low, size, tile):
    offsets, slots = len(asked), asked[0].shape[1]
    return pl.pallas_call(
        functools.partial(pack_kernel, low, size, offsets, slots, tile),
        out_shape=[jax.ShapeDtypeStruct((slots, size, tile), panel.dtype)] * offsets,
        in_specs=[SMEM] * offsets + [ANY],
        out_specs=[ANY] * offsets,
        scratch_shapes=[pltpu.SemaphoreType.DMA((offsets,))],
        compiler_params=pltpu.CompilerParams(vmem_limit_bytes=2**20),
        cost_estimate=pl.CostEstimate(flops=0, bytes_accessed=2**16, transcendentals=0),
        name="pack",
    )(*asked, panel)


def own_kernel(ranges, blocks, slots, tile, rows, cols, panel, counts, bias, *refs):
    accs, (inverse, column, product) = refs[:-3], refs[-3:]
    lanes = inverse.shape[1]
    row_tiles = panel.shape[1] // tile
    eye = identity(tile)
    ones = jnp.ones((tile, lanes), jnp.bfloat16)
    column[...] = jnp.broadcast_to(bias[...], column.shape[::-1]).T
    inverse[...] = jnp.ones(inverse.shape, jnp.float32)

    def block(s, carry):
        def multiply(t, inner):
            product[t] = dot(counts[s * slots + t], ones, NN)
            return inner

        def add(t, inner):
            at = pl.multiple_of(rows[s, t] * tile, tile)
            inverse[pl.ds(at, tile), :] += product[t]
            return inner

        lax.fori_loop(0, slots, multiply, 0, unroll=10)
        lax.fori_loop(0, slots, add, 0)
        return carry

    lax.fori_loop(0, blocks, block, 0)

    def start(r, carry):
        at = pl.multiple_of(r * tile, tile)
        scale = 1.0 / inverse[pl.ds(at, tile), :]
        inverse[pl.ds(at, tile), :] = scale
        for acc, (low, size) in zip(accs, ranges):
            here = dot(eye, panel[pl.ds(low, size), pl.ds(at, tile)], NT)
            acc[pl.ds(at, tile), :] = here * scale[:, :size]
        return carry

    lax.fori_loop(0, row_tiles, start, 0, unroll=4)

    for acc, (low, size) in zip(accs, ranges):

        def multiply(t, carry, low=low, size=size):
            col = pl.multiple_of(cols[0, t] * tile, tile)
            product[t, :, :size] = dot(counts[t], panel[pl.ds(low, size), pl.ds(col, tile)], NT)
            return carry

        def add(t, carry, acc=acc, size=size):
            at = pl.multiple_of(rows[0, t] * tile, tile)
            acc[pl.ds(at, tile), :] += product[t, :, :size] * inverse[pl.ds(at, tile), :size]
            return carry

        lax.fori_loop(0, slots, multiply, 0, unroll=10)
        lax.fori_loop(0, slots, add, 0)


def own(panel, rows, cols, counts, bias, ranges):
    blocks, slots = rows.shape
    nodes, tile = panel.shape[1], counts.shape[-1]
    lanes = max(size for _, size in ranges)
    shapes = [jax.ShapeDtypeStruct((nodes, size), jnp.float32) for _, size in ranges]
    shapes.append(jax.ShapeDtypeStruct((nodes, lanes), jnp.float32))
    shapes.append(jax.ShapeDtypeStruct((bias.shape[0], 128), bias.dtype))
    outs = call(
        functools.partial(own_kernel, ranges, blocks, slots, tile),
        "own",
        [rows, cols],
        [panel, counts, bias[None, :]],
        shapes,
        [((slots, tile, lanes), jnp.float32)],
    )
    return outs[:-2], outs[-2], outs[-1]


def pick(order, nodes, stage, outs):
    count, size = stage.shape
    eye = identity(size)

    def group(i, carry):
        at = pl.multiple_of(i * UNROLL, UNROLL)
        for u in range(UNROLL):
            source = order[at + u]
            stage[pl.ds(at + u, 1), :] = nodes[pl.ds(source, 1), :]
        return carry

    lax.fori_loop(0, count // UNROLL, group, 0)
    first = 0
    for out in outs:
        columns = out.shape[1]
        for at in range(0, columns, CHUNK):
            chunk = stage[pl.ds(first + at, CHUNK), :].astype(jnp.bfloat16)
            out[:, pl.ds(at, CHUNK)] = dot(eye, chunk, NT).astype(out.dtype)
        first += columns


def add_tiles(first, rows, acc, inverse, counts, got, total, product):
    slots, tile, size = product.shape
    total[...] = acc[...]
    for s, tiles in enumerate(got, first):

        def multiply(t, carry, s=s, tiles=tiles):
            product[t] = dot(counts[s * slots + t], tiles[t], NT)
            return carry

        def add(t, carry, s=s):
            at = pl.multiple_of(rows[s, t] * tile, tile)
            total[pl.ds(at, tile), :] += product[t] * inverse[pl.ds(at, tile), :size]
            return carry

        lax.fori_loop(0, slots, multiply, 0, unroll=10)
        lax.fori_loop(0, slots, add, 0, unroll=2)


def early_kernel(first, offsets, rows, acc, inverse, counts, *refs):
    add_tiles(first, rows, acc, inverse, counts, refs[:offsets], *refs[offsets:])


def add_early(acc, inverse, rows, counts, got, first):
    slots, tile = rows.shape[1], counts.shape[-1]
    return call(
        functools.partial(early_kernel, first, len(got)),
        "add_early",
        [rows],
        [acc, inverse, counts, *got],
        [jax.ShapeDtypeStruct(acc.shape, jnp.float32)],
        [((slots, tile, acc.shape[1]), jnp.float32)],
    )[0]


def far_kernel(first, offsets, far, rows, *refs):
    orders, (acc, inverse, counts) = refs[:far], refs[far : far + 3]
    got, total = refs[far + 3 : far + 3 + offsets], refs[far + 3 + offsets]
    outs, (product, stage) = refs[far + 4 + offsets : -2], refs[-2:]
    add_tiles(first, rows, acc, inverse, counts, got, total, product)
    for order, out in zip(orders, outs):
        pick(order, total, stage, [out])


def gather_far(acc, inverse, rows, orders, counts, got, first):
    nodes, size = acc.shape
    slots, tile = rows.shape[1], counts.shape[-1]
    share, far = orders[0].shape[0], len(orders)
    outs = call(
        functools.partial(far_kernel, first, len(got), far),
        "gather_far",
        [rows, *orders],
        [acc, inverse, counts, *got],
        [jax.ShapeDtypeStruct((nodes, size), jnp.float32)]
        + [jax.ShapeDtypeStruct((size, share), jnp.bfloat16)] * far,
        [((slots, tile, size), jnp.float32), ((share, size), jnp.float32)],
        2**22,
    )
    return outs[0], outs[1:]


def next_kernel(order, total, *refs):
    pick(order, total, refs[-1], refs[:-1])


def gather_next(total, order, widths):
    size = total.shape[1]
    return call(
        next_kernel,
        "gather_next",
        [order],
        [total],
        [jax.ShapeDtypeStruct((size, width), jnp.bfloat16) for width in widths],
        [((sum(widths), size), jnp.float32)],
    )


def mix_kernel(places, starts, weight, bias, *refs):
    pieces, (out, nodes, ready, sems) = refs[:-4], refs[-4:]
    for piece, (i, low, first) in zip(pieces, places):
        height, columns = piece.shape
        at = pl.multiple_of(starts[i] + low, 16)
        nodes[pl.ds(at, height), pl.ds(first, columns)] = piece[...]
    copies = []
    for c in range(ready.shape[0]):
        step = ready.shape[2]
        mixed = dot(weight[...], nodes[:, pl.ds(c * step, step)], NN)
        ready[c] = jnp.maximum(mixed + bias[:, :1], 0.0).astype(out.dtype)
        copies.append(
            pltpu.make_async_copy(ready.at[c], out.at[:, pl.ds(c * step, step)], sems.at[c])
        )
        copies[-1].start()
    for copy in copies:
        copy.wait()


def mix(starts, weight, bias, placed, nodes):
    places, pieces = tuple(placed), list(placed.values())
    hidden, width = weight.shape
    step = min(512, nodes)
    return pl.pallas_call(
        functools.partial(mix_kernel, places),
        out_shape=jax.ShapeDtypeStruct((hidden, nodes), jnp.bfloat16),
        in_specs=[SMEM] + [VMEM] * (2 + len(pieces)),
        out_specs=ANY,
        scratch_shapes=[
            pltpu.VMEM((width, nodes), jnp.bfloat16),
            pltpu.VMEM((nodes // step, hidden, step), jnp.bfloat16),
            pltpu.SemaphoreType.DMA((nodes // step,)),
        ],
        compiler_params=pltpu.CompilerParams(vmem_limit_bytes=16 * 2**20),
        cost_estimate=pl.CostEstimate(
            flops=2 * hidden * width * nodes, bytes_accessed=5 * 2**20, transcendentals=0
        ),
        name="mix",
    )(starts, weight, bias, *pieces)


def on_device(features, tile_rows, tile_cols, tile_weights, order, weight, bias):
    width, nodes = features.shape
    _, blocks, slots, tile, _ = tile_weights.shape
    groups = lax.axis_size("grp")
    me = lax.axis_index("grp")
    share = nodes // groups
    ranges = cuts(width)
    rows = tile_rows.reshape(blocks, slots)
    cols = tile_cols.reshape(blocks, slots)
    counts = tile_weights.reshape(blocks * slots, tile, tile)

    ranks = list(range(groups - 1, -1, -1))
    whose = me ^ jnp.asarray(ranks, jnp.int32)
    far = groups - 2
    picks = [lax.dynamic_slice(order, ((me ^ k) * share,), (share,)) for k in ranks]

    asked = [shifted(cols, "blk", -s) for s in range(1, blocks)]
    *asked, panel = lax.optimization_barrier((*asked, staged(features)))
    sent = []
    for low, size in ranges:
        source = features if sent else panel
        sent.append(list(pack(source, asked, low, size, tile)))
        *asked, sent[-1][0] = lax.optimization_barrier((*asked, sent[-1][0]))
    accs, inverse, column = own(features, rows, cols, counts, bias, ranges)
    accs, across, picks, starts = lax.optimization_barrier(
        (accs, weight.T, picks, whose * width)
    )

    got, early = [], []
    for p, leaving in enumerate(sent):
        if p:
            leaving, got[-1], early[-1], accs = lax.optimization_barrier(
                (leaving, got[-1], early[-1], accs)
            )
        got.append([shifted(value, "blk", s + 1) for s, value in enumerate(leaving)])
        early.append(add_early(accs[p], inverse, rows, counts, got[p][:-1], 1))

    pieces, waits, kept = {}, {}, {}
    for p, (low, size) in enumerate(ranges):
        last = p == len(ranges) - 1
        acc, kept = lax.optimization_barrier((early[p], kept))
        pieces.update(kept)
        total, out_far = gather_far(
            acc, inverse, rows, picks[:far], counts, got[p][-1:], blocks - 1
        )
        now = {(i, low, 0): traded(piece, "grp", ranks[i]) for i, piece in enumerate(out_far)}
        widths = (share,)
        if not last:
            kept = gather_next(total, picks[-1], (share,))[0]
            total, kept = lax.optimization_barrier((total, kept))
        else:
            total, waits = lax.optimization_barrier((total, waits))
            pieces.update(waits)
            widths = (share // 2, share // 2)
        first = 0
        for piece in gather_next(total, picks[far], widths):
            if not last:
                piece, got[p + 1], early[p + 1] = lax.optimization_barrier(
                    (piece, got[p + 1], early[p + 1])
                )
            now[far, low, first] = traded(piece, "grp", ranks[far])
            first += piece.shape[1]
        if last:
            kept = gather_next(total, picks[-1], (share,))[0]
        kept = {(groups - 1, low, 0): kept}
        waits = now
    pieces.update(waits)
    pieces.update(kept)
    return mix(starts, across, column, pieces, share)


def solution(mesh):
    in_specs = (
        P("grp", ("parts", "blk")),
        P(("parts", "blk"), None, None),
        P(("parts", "blk"), None, None),
        P(("parts", "blk"), None, None, None, None),
        P(("parts", "blk")),
        P(),
        P(),
    )
    out_specs = P(None, ("parts", "blk", "grp"))
    return jax.shard_map(
        on_device, mesh=mesh, in_specs=in_specs, out_specs=out_specs, check_vma=False
    )
```

```python
import functools

import jax
import jax.numpy as jnp
from jax import lax
from jax.experimental import pallas as pl
from jax.experimental.pallas import tpu as pltpu
from jax.sharding import PartitionSpec as P

NN = (((1,), (0,)), ((), ()))
NT = (((1,), (1,)), ((), ()))
VMEM = pl.BlockSpec(memory_space=pltpu.VMEM)
SMEM = pl.BlockSpec(memory_space=pltpu.SMEM)
ANY = pl.BlockSpec(memory_space=pl.ANY)
CHUNK = 256
UNROLL = 64


def dot(a, b, dims):
    return lax.dot_general(a, b, dims, preferred_element_type=jnp.float32)


def padded(shape, dtype):
    rows = 1
    for extent in shape[:-1]:
        rows *= extent
    return rows * -(-shape[-1] // 128) * 128 * jnp.dtype(dtype).itemsize


def call(kernel, name, scalars, arrays, outs, scratch=(), moved=2**16):
    held = sum(padded(a.shape, a.dtype) for a in list(arrays) + list(outs))
    held += sum(padded(shape, dtype) for shape, dtype in scratch)
    return pl.pallas_call(
        kernel,
        out_shape=list(outs),
        in_specs=[SMEM] * len(scalars) + [VMEM] * len(arrays),
        out_specs=[VMEM] * len(outs),
        scratch_shapes=[pltpu.VMEM(shape, dtype) for shape, dtype in scratch],
        compiler_params=pltpu.CompilerParams(vmem_limit_bytes=held + 2**20),
        cost_estimate=pl.CostEstimate(flops=0, bytes_accessed=moved, transcendentals=0),
        name=name,
    )(*scalars, *arrays)


def shifted(value, axis, steps):
    count = lax.axis_size(axis)
    pairs = [(source, (source + steps) % count) for source in range(count)]
    return lax.ppermute(value, axis, pairs)


def traded(value, axis, k):
    return lax.ppermute(value, axis, [(i, i ^ k) for i in range(lax.axis_size(axis))])


def cuts(width):
    first = width * 5 // 8 // 16 * 16
    return ((0, first), (first, width - first))


def identity(size):
    row = lax.broadcasted_iota(jnp.int32, (size, size), 0)
    col = lax.broadcasted_iota(jnp.int32, (size, size), 1)
    return (row == col).astype(jnp.float32).astype(jnp.bfloat16)


def stage_kernel(panel, out):
    out[...] = panel[...]


def staged(panel):
    shape = jax.ShapeDtypeStruct(panel.shape, panel.dtype)
    return call(stage_kernel, "stage", [], [panel], [shape])[0]


def pack_kernel(low, size, offsets, slots, tile, *refs):
    asked, panel = refs[:offsets], refs[offsets]
    outs, sems = refs[offsets + 1 : -1], refs[-1]
    for s in range(offsets):

        def body(t, carry, s=s):
            at = pl.multiple_of(asked[s][s + 1, t] * tile, tile)
            pltpu.make_async_copy(
                panel.at[pl.ds(low, size), pl.ds(at, tile)], outs[s].at[t], sems.at[s]
            ).start()
            return carry

        lax.fori_loop(0, slots, body, 0, unroll=4)
    for s in range(offsets):
        pltpu.make_async_copy(outs[s], outs[s], sems.at[s]).wait()


def pack(panel, asked, low, size, tile):
    offsets, slots = len(asked), asked[0].shape[1]
    return pl.pallas_call(
        functools.partial(pack_kernel, low, size, offsets, slots, tile),
        out_shape=[jax.ShapeDtypeStruct((slots, size, tile), panel.dtype)] * offsets,
        in_specs=[SMEM] * offsets + [ANY],
        out_specs=[ANY] * offsets,
        scratch_shapes=[pltpu.SemaphoreType.DMA((offsets,))],
        compiler_params=pltpu.CompilerParams(vmem_limit_bytes=2**20),
        cost_estimate=pl.CostEstimate(flops=0, bytes_accessed=2**16, transcendentals=0),
        name="pack",
    )(*asked, panel)


def own_kernel(ranges, blocks, slots, tile, rows, cols, panel, counts, bias, *refs):
    accs, (inverse, column, product) = refs[:-3], refs[-3:]
    lanes = inverse.shape[1]
    row_tiles = panel.shape[1] // tile
    eye = identity(tile)
    ones = jnp.ones((tile, lanes), jnp.bfloat16)
    column[...] = jnp.broadcast_to(bias[...], column.shape[::-1]).T
    inverse[...] = jnp.ones(inverse.shape, jnp.float32)

    def block(s, carry):
        def multiply(t, inner):
            product[t] = dot(counts[s * slots + t], ones, NN)
            return inner

        def add(t, inner):
            at = pl.multiple_of(rows[s, t] * tile, tile)
            inverse[pl.ds(at, tile), :] += product[t]
            return inner

        lax.fori_loop(0, slots, multiply, 0, unroll=10)
        lax.fori_loop(0, slots, add, 0)
        return carry

    lax.fori_loop(0, blocks, block, 0)

    def start(r, carry):
        at = pl.multiple_of(r * tile, tile)
        scale = 1.0 / inverse[pl.ds(at, tile), :]
        inverse[pl.ds(at, tile), :] = scale
        for acc, (low, size) in zip(accs, ranges):
            here = dot(eye, panel[pl.ds(low, size), pl.ds(at, tile)], NT)
            acc[pl.ds(at, tile), :] = here * scale[:, :size]
        return carry

    lax.fori_loop(0, row_tiles, start, 0, unroll=4)

    for acc, (low, size) in zip(accs, ranges):

        def multiply(t, carry, low=low, size=size):
            col = pl.multiple_of(cols[0, t] * tile, tile)
            product[t, :, :size] = dot(counts[t], panel[pl.ds(low, size), pl.ds(col, tile)], NT)
            return carry

        def add(t, carry, acc=acc, size=size):
            at = pl.multiple_of(rows[0, t] * tile, tile)
            acc[pl.ds(at, tile), :] += product[t, :, :size] * inverse[pl.ds(at, tile), :size]
            return carry

        lax.fori_loop(0, slots, multiply, 0, unroll=10)
        lax.fori_loop(0, slots, add, 0)


def own(panel, rows, cols, counts, bias, ranges):
    blocks, slots = rows.shape
    nodes, tile = panel.shape[1], counts.shape[-1]
    lanes = max(size for _, size in ranges)
    shapes = [jax.ShapeDtypeStruct((nodes, size), jnp.float32) for _, size in ranges]
    shapes.append(jax.ShapeDtypeStruct((nodes, lanes), jnp.float32))
    shapes.append(jax.ShapeDtypeStruct((bias.shape[0], 128), bias.dtype))
    outs = call(
        functools.partial(own_kernel, ranges, blocks, slots, tile),
        "own",
        [rows, cols],
        [panel, counts, bias[None, :]],
        shapes,
        [((slots, tile, lanes), jnp.float32)],
    )
    return outs[:-2], outs[-2], outs[-1]


def pick(order, nodes, stage, outs):
    count, size = stage.shape
    eye = identity(size)

    def group(i, carry):
        at = pl.multiple_of(i * UNROLL, UNROLL)
        for u in range(UNROLL):
            source = order[at + u]
            stage[pl.ds(at + u, 1), :] = nodes[pl.ds(source, 1), :]
        return carry

    lax.fori_loop(0, count // UNROLL, group, 0)
    first = 0
    for out in outs:
        columns = out.shape[1]
        for at in range(0, columns, CHUNK):
            chunk = stage[pl.ds(first + at, CHUNK), :].astype(jnp.bfloat16)
            out[:, pl.ds(at, CHUNK)] = dot(eye, chunk, NT).astype(out.dtype)
        first += columns


def add_tiles(first, rows, acc, inverse, counts, got, total, product):
    slots, tile, size = product.shape
    total[...] = acc[...]
    for s, tiles in enumerate(got, first):

        def multiply(t, carry, s=s, tiles=tiles):
            product[t] = dot(counts[s * slots + t], tiles[t], NT)
            return carry

        def add(t, carry, s=s):
            at = pl.multiple_of(rows[s, t] * tile, tile)
            total[pl.ds(at, tile), :] += product[t] * inverse[pl.ds(at, tile), :size]
            return carry

        lax.fori_loop(0, slots, multiply, 0, unroll=10)
        lax.fori_loop(0, slots, add, 0, unroll=2)


def early_kernel(first, offsets, rows, acc, inverse, counts, *refs):
    add_tiles(first, rows, acc, inverse, counts, refs[:offsets], *refs[offsets:])


def add_early(acc, inverse, rows, counts, got, first):
    slots, tile = rows.shape[1], counts.shape[-1]
    return call(
        functools.partial(early_kernel, first, len(got)),
        "add_early",
        [rows],
        [acc, inverse, counts, *got],
        [jax.ShapeDtypeStruct(acc.shape, jnp.float32)],
        [((slots, tile, acc.shape[1]), jnp.float32)],
    )[0]


def far_kernel(first, offsets, far, rows, *refs):
    orders, (acc, inverse, counts) = refs[:far], refs[far : far + 3]
    got, total = refs[far + 3 : far + 3 + offsets], refs[far + 3 + offsets]
    outs, (product, stage) = refs[far + 4 + offsets : -2], refs[-2:]
    add_tiles(first, rows, acc, inverse, counts, got, total, product)
    for order, out in zip(orders, outs):
        pick(order, total, stage, [out])


def gather_far(acc, inverse, rows, orders, counts, got, first):
    nodes, size = acc.shape
    slots, tile = rows.shape[1], counts.shape[-1]
    share, far = orders[0].shape[0], len(orders)
    outs = call(
        functools.partial(far_kernel, first, len(got), far),
        "gather_far",
        [rows, *orders],
        [acc, inverse, counts, *got],
        [jax.ShapeDtypeStruct((nodes, size), jnp.float32)]
        + [jax.ShapeDtypeStruct((size, share), jnp.bfloat16)] * far,
        [((slots, tile, size), jnp.float32), ((share, size), jnp.float32)],
        2**22,
    )
    return outs[0], outs[1:]


def next_kernel(orders, cuts_of, *refs):
    order, total, outs, stage = refs[:orders], refs[orders], refs[orders + 1 : -1], refs[-1]
    first = 0
    for indices, count in zip(order, cuts_of):
        pick(indices, total, stage, outs[first : first + count])
        first += count


def gather_next(total, orders, widths):
    size = total.shape[1]
    return call(
        functools.partial(next_kernel, len(orders), tuple(len(w) for w in widths)),
        "gather_next",
        orders,
        [total],
        [jax.ShapeDtypeStruct((size, width), jnp.bfloat16) for w in widths for width in w],
        [((orders[0].shape[0], size), jnp.float32)],
    )


def mix_kernel(places, starts, weight, bias, *refs):
    pieces, (out, nodes, ready, sems) = refs[:-4], refs[-4:]
    for piece, (i, low, first) in zip(pieces, places):
        height, columns = piece.shape
        at = pl.multiple_of(starts[i] + low, 16)
        nodes[pl.ds(at, height), pl.ds(first, columns)] = piece[...]
    copies = []
    for c in range(ready.shape[0]):
        step = ready.shape[2]
        mixed = dot(weight[...], nodes[:, pl.ds(c * step, step)], NN)
        ready[c] = jnp.maximum(mixed + bias[:, :1], 0.0).astype(out.dtype)
        copies.append(
            pltpu.make_async_copy(ready.at[c], out.at[:, pl.ds(c * step, step)], sems.at[c])
        )
        copies[-1].start()
    for copy in copies:
        copy.wait()


def mix(starts, weight, bias, placed, nodes):
    places, pieces = tuple(placed), list(placed.values())
    hidden, width = weight.shape
    step = min(512, nodes)
    return pl.pallas_call(
        functools.partial(mix_kernel, places),
        out_shape=jax.ShapeDtypeStruct((hidden, nodes), jnp.bfloat16),
        in_specs=[SMEM] + [VMEM] * (2 + len(pieces)),
        out_specs=ANY,
        scratch_shapes=[
            pltpu.VMEM((width, nodes), jnp.bfloat16),
            pltpu.VMEM((nodes // step, hidden, step), jnp.bfloat16),
            pltpu.SemaphoreType.DMA((nodes // step,)),
        ],
        compiler_params=pltpu.CompilerParams(vmem_limit_bytes=16 * 2**20),
        cost_estimate=pl.CostEstimate(
            flops=2 * hidden * width * nodes, bytes_accessed=5 * 2**20, transcendentals=0
        ),
        name="mix",
    )(starts, weight, bias, *pieces)


def on_device(features, tile_rows, tile_cols, tile_weights, order, weight, bias):
    width, nodes = features.shape
    _, blocks, slots, tile, _ = tile_weights.shape
    groups = lax.axis_size("grp")
    me = lax.axis_index("grp")
    share = nodes // groups
    ranges = cuts(width)
    rows = tile_rows.reshape(blocks, slots)
    cols = tile_cols.reshape(blocks, slots)
    counts = tile_weights.reshape(blocks * slots, tile, tile)

    ranks = list(range(groups - 1, -1, -1))
    whose = me ^ jnp.asarray(ranks, jnp.int32)
    far = groups - 2
    picks = [lax.dynamic_slice(order, ((me ^ k) * share,), (share,)) for k in ranks]

    asked = [shifted(cols, "blk", -s) for s in range(1, blocks)]
    *asked, panel = lax.optimization_barrier((*asked, staged(features)))
    sent = []
    for low, size in ranges:
        source = features if sent else panel
        sent.append(list(pack(source, asked, low, size, tile)))
        *asked, sent[-1][0] = lax.optimization_barrier((*asked, sent[-1][0]))
    accs, inverse, column = own(features, rows, cols, counts, bias, ranges)
    accs, across, picks, starts = lax.optimization_barrier(
        (accs, weight.T, picks, whose * width)
    )

    got = []
    for p, leaving in enumerate(sent):
        if p:
            leaving, got[-1], accs = lax.optimization_barrier((leaving, got[-1], accs))
        got.append([shifted(value, "blk", s + 1) for s, value in enumerate(leaving)])

    pieces, waits, kept = {}, {}, {}
    acc, late = accs[0], 1
    for p, (low, size) in enumerate(ranges[:-1]):
        total, out_far = gather_far(acc, inverse, rows, picks[:far], counts, got[p], 1)
        for i, piece in enumerate(out_far):
            waits[i, low, 0] = traded(piece, "grp", ranks[i])
        beside, kept = gather_next(total, picks[far:], [(share,), (share,)])
        early, late = got[p + 1][:-1], blocks - 1
        acc = add_early(accs[p + 1], inverse, rows, counts, early, 1)
        beside, kept, acc, got[p + 1] = lax.optimization_barrier(
            (beside, kept, acc, got[p + 1])
        )
        waits[far, low, 0] = traded(beside, "grp", 1)
        pieces[far + 1, low, 0] = kept

    low, size = ranges[-1]
    total, out_far = gather_far(acc, inverse, rows, picks[:1], counts, got[-1][late - 1 :], late)
    pieces[0, low, 0] = traded(out_far[0], "grp", ranks[0])
    for i in range(1, groups):
        widths = (share,)
        if i < far:
            total, waits = lax.optimization_barrier((total, waits))
            pieces.update(waits)
            widths = (share // 4 * 3, share // 4)
        elif i == far:
            widths = (share // 2, share // 2)
        first = 0
        for piece in gather_next(total, [picks[i]], [widths]):
            pieces[i, low, first] = traded(piece, "grp", ranks[i]) if ranks[i] else piece
            first += piece.shape[1]
    pieces.update(waits)
    return mix(starts, across, column, pieces, share)


def solution(mesh):
    in_specs = (
        P("grp", ("parts", "blk")),
        P(("parts", "blk"), None, None),
        P(("parts", "blk"), None, None),
        P(("parts", "blk"), None, None, None, None),
        P(("parts", "blk")),
        P(),
        P(),
    )
    out_specs = P(None, ("parts", "blk", "grp"))
    return jax.shard_map(
        on_device, mesh=mesh, in_specs=in_specs, out_specs=out_specs, check_vma=False
    )
```

```python
import functools

import jax
import jax.numpy as jnp
from jax import lax
from jax.experimental import pallas as pl
from jax.experimental.pallas import tpu as pltpu
from jax.sharding import PartitionSpec as P

NN = (((1,), (0,)), ((), ()))
NT = (((1,), (1,)), ((), ()))
VMEM = pl.BlockSpec(memory_space=pltpu.VMEM)
SMEM = pl.BlockSpec(memory_space=pltpu.SMEM)
ANY = pl.BlockSpec(memory_space=pl.ANY)
CHUNK = 256
UNROLL = 64


def dot(a, b, dims):
    return lax.dot_general(a, b, dims, preferred_element_type=jnp.float32)


def padded(shape, dtype):
    rows = 1
    for extent in shape[:-1]:
        rows *= extent
    return rows * -(-shape[-1] // 128) * 128 * jnp.dtype(dtype).itemsize


def call(kernel, name, scalars, arrays, outs, scratch=(), moved=2**16):
    held = sum(padded(a.shape, a.dtype) for a in list(arrays) + list(outs))
    held += sum(padded(shape, dtype) for shape, dtype in scratch)
    return pl.pallas_call(
        kernel,
        out_shape=list(outs),
        in_specs=[SMEM] * len(scalars) + [VMEM] * len(arrays),
        out_specs=[VMEM] * len(outs),
        scratch_shapes=[pltpu.VMEM(shape, dtype) for shape, dtype in scratch],
        compiler_params=pltpu.CompilerParams(vmem_limit_bytes=held + 2**20),
        cost_estimate=pl.CostEstimate(flops=0, bytes_accessed=moved, transcendentals=0),
        name=name,
    )(*scalars, *arrays)


def shifted(value, axis, steps):
    count = lax.axis_size(axis)
    pairs = [(source, (source + steps) % count) for source in range(count)]
    return lax.ppermute(value, axis, pairs)


def traded(value, axis, k):
    return lax.ppermute(value, axis, [(i, i ^ k) for i in range(lax.axis_size(axis))])


def cuts(width):
    first = width * 5 // 8 // 16 * 16
    return ((0, first), (first, width - first))


def identity(size):
    row = lax.broadcasted_iota(jnp.int32, (size, size), 0)
    col = lax.broadcasted_iota(jnp.int32, (size, size), 1)
    return (row == col).astype(jnp.float32).astype(jnp.bfloat16)


def stage_kernel(panel, out):
    out[...] = panel[...]


def staged(panel):
    shape = jax.ShapeDtypeStruct(panel.shape, panel.dtype)
    return call(stage_kernel, "stage", [], [panel], [shape])[0]


def pack_kernel(low, size, offsets, slots, tile, *refs):
    asked, panel = refs[:offsets], refs[offsets]
    outs, sems = refs[offsets + 1 : -1], refs[-1]
    for s in range(offsets):

        def body(t, carry, s=s):
            at = pl.multiple_of(asked[s][s + 1, t] * tile, tile)
            pltpu.make_async_copy(
                panel.at[pl.ds(low, size), pl.ds(at, tile)], outs[s].at[t], sems.at[s]
            ).start()
            return carry

        lax.fori_loop(0, slots, body, 0, unroll=4)
    for s in range(offsets):
        pltpu.make_async_copy(outs[s], outs[s], sems.at[s]).wait()


def pack(panel, asked, low, size, tile):
    offsets, slots = len(asked), asked[0].shape[1]
    return pl.pallas_call(
        functools.partial(pack_kernel, low, size, offsets, slots, tile),
        out_shape=[jax.ShapeDtypeStruct((slots, size, tile), panel.dtype)] * offsets,
        in_specs=[SMEM] * offsets + [ANY],
        out_specs=[ANY] * offsets,
        scratch_shapes=[pltpu.SemaphoreType.DMA((offsets,))],
        compiler_params=pltpu.CompilerParams(vmem_limit_bytes=2**20),
        cost_estimate=pl.CostEstimate(flops=0, bytes_accessed=2**16, transcendentals=0),
        name="pack",
    )(*asked, panel)


def own_kernel(ranges, blocks, slots, tile, rows, cols, panel, counts, bias, *refs):
    accs, (inverse, column, product) = refs[:-3], refs[-3:]
    lanes = inverse.shape[1]
    row_tiles = panel.shape[1] // tile
    eye = identity(tile)
    ones = jnp.ones((tile, lanes), jnp.bfloat16)
    column[...] = jnp.broadcast_to(bias[...], column.shape[::-1]).T
    inverse[...] = jnp.ones(inverse.shape, jnp.float32)

    def block(s, carry):
        def multiply(t, inner):
            product[t] = dot(counts[s * slots + t], ones, NN)
            return inner

        def add(t, inner):
            at = pl.multiple_of(rows[s, t] * tile, tile)
            inverse[pl.ds(at, tile), :] += product[t]
            return inner

        lax.fori_loop(0, slots, multiply, 0, unroll=10)
        lax.fori_loop(0, slots, add, 0)
        return carry

    lax.fori_loop(0, blocks, block, 0)

    def start(r, carry):
        at = pl.multiple_of(r * tile, tile)
        scale = 1.0 / inverse[pl.ds(at, tile), :]
        inverse[pl.ds(at, tile), :] = scale
        for acc, (low, size) in zip(accs, ranges):
            here = dot(eye, panel[pl.ds(low, size), pl.ds(at, tile)], NT)
            acc[pl.ds(at, tile), :] = here * scale[:, :size]
        return carry

    lax.fori_loop(0, row_tiles, start, 0, unroll=4)

    for acc, (low, size) in zip(accs, ranges):

        def multiply(t, carry, low=low, size=size):
            col = pl.multiple_of(cols[0, t] * tile, tile)
            product[t, :, :size] = dot(counts[t], panel[pl.ds(low, size), pl.ds(col, tile)], NT)
            return carry

        def add(t, carry, acc=acc, size=size):
            at = pl.multiple_of(rows[0, t] * tile, tile)
            acc[pl.ds(at, tile), :] += product[t, :, :size] * inverse[pl.ds(at, tile), :size]
            return carry

        lax.fori_loop(0, slots, multiply, 0, unroll=10)
        lax.fori_loop(0, slots, add, 0)


def own(panel, rows, cols, counts, bias, ranges):
    blocks, slots = rows.shape
    nodes, tile = panel.shape[1], counts.shape[-1]
    lanes = max(size for _, size in ranges)
    shapes = [jax.ShapeDtypeStruct((nodes, size), jnp.float32) for _, size in ranges]
    shapes.append(jax.ShapeDtypeStruct((nodes, lanes), jnp.float32))
    shapes.append(jax.ShapeDtypeStruct((bias.shape[0], 128), bias.dtype))
    outs = call(
        functools.partial(own_kernel, ranges, blocks, slots, tile),
        "own",
        [rows, cols],
        [panel, counts, bias[None, :]],
        shapes,
        [((slots, tile, lanes), jnp.float32)],
    )
    return outs[:-2], outs[-2], outs[-1]


def pick(order, nodes, stage, outs):
    count, size = stage.shape
    eye = identity(size)

    def group(i, carry):
        at = pl.multiple_of(i * UNROLL, UNROLL)
        for u in range(UNROLL):
            source = order[at + u]
            stage[pl.ds(at + u, 1), :] = nodes[pl.ds(source, 1), :]
        return carry

    lax.fori_loop(0, count // UNROLL, group, 0)
    first = 0
    for out in outs:
        columns = out.shape[1]
        for at in range(0, columns, CHUNK):
            chunk = stage[pl.ds(first + at, CHUNK), :].astype(jnp.bfloat16)
            out[:, pl.ds(at, CHUNK)] = dot(eye, chunk, NT).astype(out.dtype)
        first += columns


def add_tiles(first, rows, acc, inverse, counts, got, total, product):
    slots, tile, size = product.shape
    total[...] = acc[...]
    for s, tiles in enumerate(got, first):

        def multiply(t, carry, s=s, tiles=tiles):
            product[t] = dot(counts[s * slots + t], tiles[t], NT)
            return carry

        def add(t, carry, s=s):
            at = pl.multiple_of(rows[s, t] * tile, tile)
            total[pl.ds(at, tile), :] += product[t] * inverse[pl.ds(at, tile), :size]
            return carry

        lax.fori_loop(0, slots, multiply, 0, unroll=10)
        lax.fori_loop(0, slots, add, 0, unroll=2)


def early_kernel(first, offsets, rows, acc, inverse, counts, *refs):
    add_tiles(first, rows, acc, inverse, counts, refs[:offsets], *refs[offsets:])


def add_early(acc, inverse, rows, counts, got, first):
    slots, tile = rows.shape[1], counts.shape[-1]
    return call(
        functools.partial(early_kernel, first, len(got)),
        "add_early",
        [rows],
        [acc, inverse, counts, *got],
        [jax.ShapeDtypeStruct(acc.shape, jnp.float32)],
        [((slots, tile, acc.shape[1]), jnp.float32)],
    )[0]


def far_kernel(first, offsets, far, rows, *refs):
    orders, (acc, inverse, counts) = refs[:far], refs[far : far + 3]
    got, total = refs[far + 3 : far + 3 + offsets], refs[far + 3 + offsets]
    outs, (product, stage) = refs[far + 4 + offsets : -2], refs[-2:]
    add_tiles(first, rows, acc, inverse, counts, got, total, product)
    for order, out in zip(orders, outs):
        pick(order, total, stage, [out])


def gather_far(acc, inverse, rows, orders, counts, got, first):
    nodes, size = acc.shape
    slots, tile = rows.shape[1], counts.shape[-1]
    share, far = orders[0].shape[0], len(orders)
    outs = call(
        functools.partial(far_kernel, first, len(got), far),
        "gather_far",
        [rows, *orders],
        [acc, inverse, counts, *got],
        [jax.ShapeDtypeStruct((nodes, size), jnp.float32)]
        + [jax.ShapeDtypeStruct((size, share), jnp.bfloat16)] * far,
        [((slots, tile, size), jnp.float32), ((share, size), jnp.float32)],
        2**20,
    )
    return outs[0], outs[1:]


def next_kernel(orders, cuts_of, *refs):
    order, total, outs, stage = refs[:orders], refs[orders], refs[orders + 1 : -1], refs[-1]
    first = 0
    for indices, count in zip(order, cuts_of):
        pick(indices, total, stage, outs[first : first + count])
        first += count


def gather_next(total, orders, widths):
    size = total.shape[1]
    return call(
        functools.partial(next_kernel, len(orders), tuple(len(w) for w in widths)),
        "gather_next",
        orders,
        [total],
        [jax.ShapeDtypeStruct((size, width), jnp.bfloat16) for w in widths for width in w],
        [((orders[0].shape[0], size), jnp.float32)],
    )


def mix_kernel(places, starts, weight, bias, *refs):
    pieces, (out, nodes, ready, sems) = refs[:-4], refs[-4:]
    for piece, (i, low, first) in zip(pieces, places):
        height, columns = piece.shape
        at = pl.multiple_of(starts[i] + low, 16)
        nodes[pl.ds(at, height), pl.ds(first, columns)] = piece[...]
    copies = []
    for c in range(ready.shape[0]):
        step = ready.shape[2]
        mixed = dot(weight[...], nodes[:, pl.ds(c * step, step)], NN)
        ready[c] = jnp.maximum(mixed + bias[:, :1], 0.0).astype(out.dtype)
        copies.append(
            pltpu.make_async_copy(ready.at[c], out.at[:, pl.ds(c * step, step)], sems.at[c])
        )
        copies[-1].start()
    for copy in copies:
        copy.wait()


def mix(starts, weight, bias, placed, nodes):
    places, pieces = tuple(placed), list(placed.values())
    hidden, width = weight.shape
    step = min(512, nodes)
    return pl.pallas_call(
        functools.partial(mix_kernel, places),
        out_shape=jax.ShapeDtypeStruct((hidden, nodes), jnp.bfloat16),
        in_specs=[SMEM] + [VMEM] * (2 + len(pieces)),
        out_specs=ANY,
        scratch_shapes=[
            pltpu.VMEM((width, nodes), jnp.bfloat16),
            pltpu.VMEM((nodes // step, hidden, step), jnp.bfloat16),
            pltpu.SemaphoreType.DMA((nodes // step,)),
        ],
        compiler_params=pltpu.CompilerParams(vmem_limit_bytes=16 * 2**20),
        cost_estimate=pl.CostEstimate(
            flops=2 * hidden * width * nodes, bytes_accessed=5 * 2**20, transcendentals=0
        ),
        name="mix",
    )(starts, weight, bias, *pieces)


def on_device(features, tile_rows, tile_cols, tile_weights, order, weight, bias):
    width, nodes = features.shape
    _, blocks, slots, tile, _ = tile_weights.shape
    groups = lax.axis_size("grp")
    me = lax.axis_index("grp")
    share = nodes // groups
    ranges = cuts(width)
    rows = tile_rows.reshape(blocks, slots)
    cols = tile_cols.reshape(blocks, slots)
    counts = tile_weights.reshape(blocks * slots, tile, tile)

    ranks = list(range(groups - 1, -1, -1))
    whose = me ^ jnp.asarray(ranks, jnp.int32)
    far = groups - 2
    picks = [lax.dynamic_slice(order, ((me ^ k) * share,), (share,)) for k in ranks]

    asked = [shifted(cols, "blk", -s) for s in range(1, blocks)]
    *asked, panel = lax.optimization_barrier((*asked, staged(features)))
    sent = []
    for low, size in ranges:
        source = features if sent else panel
        sent.append(list(pack(source, asked, low, size, tile)))
        *asked, sent[-1][0] = lax.optimization_barrier((*asked, sent[-1][0]))
    accs, inverse, column = own(features, rows, cols, counts, bias, ranges)
    accs, across, picks, starts = lax.optimization_barrier(
        (accs, weight.T, picks, whose * width)
    )

    got, early = [], []
    for p, leaving in enumerate(sent):
        if p:
            leaving, got[-1], early[-1], accs = lax.optimization_barrier(
                (leaving, got[-1], early[-1], accs)
            )
        got.append([shifted(value, "blk", s + 1) for s, value in enumerate(leaving)])
        early.append(add_early(accs[p], inverse, rows, counts, got[p][:-1], 1))

    pieces, across_x, beside = {}, {}, {}
    for p, (low, size) in enumerate(ranges[:-1]):
        total, out_far = gather_far(
            early[p], inverse, rows, picks[:far], counts, got[p][-1:], blocks - 1
        )
        for i, piece in enumerate(out_far):
            across_x[i, low, 0] = traded(piece, "grp", ranks[i])
        halves = (share // 2, share // 2)
        near = gather_next(total, picks[far:], [halves, (share,)])
        near, early[p + 1], got[p + 1] = lax.optimization_barrier(
            (near, early[p + 1], got[p + 1])
        )
        beside[far, low, 0] = traded(near[0], "grp", 1)
        beside[far, low, share // 2] = traded(near[1], "grp", 1)
        pieces[far + 1, low, 0] = near[2]

    low, size = ranges[-1]
    total, out_far = gather_far(
        early[-1], inverse, rows, picks[:1], counts, got[-1][-1:], blocks - 1
    )
    pieces[0, low, 0] = traded(out_far[0], "grp", ranks[0])
    for i in range(1, groups):
        widths = (share,)
        if i < far:
            total, beside = lax.optimization_barrier((total, beside))
            widths = (share // 4 * 3, share // 4)
        elif i == far:
            total, across_x = lax.optimization_barrier((total, across_x))
            widths = (share // 2, share // 2)
        first = 0
        for piece in gather_next(total, [picks[i]], [widths]):
            pieces[i, low, first] = traded(piece, "grp", ranks[i]) if ranks[i] else piece
            first += piece.shape[1]
    pieces.update(beside)
    pieces.update(across_x)
    return mix(starts, across, column, pieces, share)


def solution(mesh):
    in_specs = (
        P("grp", ("parts", "blk")),
        P(("parts", "blk"), None, None),
        P(("parts", "blk"), None, None),
        P(("parts", "blk"), None, None, None, None),
        P(("parts", "blk")),
        P(),
        P(),
    )
    out_specs = P(None, ("parts", "blk", "grp"))
    return jax.shard_map(
        on_device, mesh=mesh, in_specs=in_specs, out_specs=out_specs, check_vma=False
    )
```

```python
import functools

import jax
import jax.numpy as jnp
from jax import lax
from jax.experimental import pallas as pl
from jax.experimental.pallas import tpu as pltpu
from jax.sharding import PartitionSpec as P

NN = (((1,), (0,)), ((), ()))
NT = (((1,), (1,)), ((), ()))
VMEM = pl.BlockSpec(memory_space=pltpu.VMEM)
SMEM = pl.BlockSpec(memory_space=pltpu.SMEM)
ANY = pl.BlockSpec(memory_space=pl.ANY)
CHUNK = 256
UNROLL = 64


def dot(a, b, dims):
    return lax.dot_general(a, b, dims, preferred_element_type=jnp.float32)


def padded(shape, dtype):
    rows = 1
    for extent in shape[:-1]:
        rows *= extent
    return rows * -(-shape[-1] // 128) * 128 * jnp.dtype(dtype).itemsize


def call(kernel, name, scalars, arrays, outs, scratch=(), moved=2**16):
    held = sum(padded(a.shape, a.dtype) for a in list(arrays) + list(outs))
    held += sum(padded(shape, dtype) for shape, dtype in scratch)
    return pl.pallas_call(
        kernel,
        out_shape=list(outs),
        in_specs=[SMEM] * len(scalars) + [VMEM] * len(arrays),
        out_specs=[VMEM] * len(outs),
        scratch_shapes=[pltpu.VMEM(shape, dtype) for shape, dtype in scratch],
        compiler_params=pltpu.CompilerParams(vmem_limit_bytes=held + 2**20),
        cost_estimate=pl.CostEstimate(flops=0, bytes_accessed=moved, transcendentals=0),
        name=name,
    )(*scalars, *arrays)


def shifted(value, axis, steps):
    count = lax.axis_size(axis)
    pairs = [(source, (source + steps) % count) for source in range(count)]
    return lax.ppermute(value, axis, pairs)


def traded(value, axis, k):
    return lax.ppermute(value, axis, [(i, i ^ k) for i in range(lax.axis_size(axis))])


def cuts(width):
    first = width * 5 // 8 // 16 * 16
    return ((0, first), (first, width - first))


def identity(size):
    row = lax.broadcasted_iota(jnp.int32, (size, size), 0)
    col = lax.broadcasted_iota(jnp.int32, (size, size), 1)
    return (row == col).astype(jnp.float32).astype(jnp.bfloat16)


def stage_kernel(panel, out):
    out[...] = panel[...]


def staged(panel):
    shape = jax.ShapeDtypeStruct(panel.shape, panel.dtype)
    return call(stage_kernel, "stage", [], [panel], [shape])[0]


def pack_kernel(low, size, offsets, slots, tile, *refs):
    asked, panel = refs[:offsets], refs[offsets]
    outs, sems = refs[offsets + 1 : -1], refs[-1]
    for s in range(offsets):

        def body(t, carry, s=s):
            at = pl.multiple_of(asked[s][s + 1, t] * tile, tile)
            pltpu.make_async_copy(
                panel.at[pl.ds(low, size), pl.ds(at, tile)], outs[s].at[t], sems.at[s]
            ).start()
            return carry

        lax.fori_loop(0, slots, body, 0, unroll=4)
    for s in range(offsets):
        pltpu.make_async_copy(outs[s], outs[s], sems.at[s]).wait()


def pack(panel, asked, low, size, tile):
    offsets, slots = len(asked), asked[0].shape[1]
    return pl.pallas_call(
        functools.partial(pack_kernel, low, size, offsets, slots, tile),
        out_shape=[jax.ShapeDtypeStruct((slots, size, tile), panel.dtype)] * offsets,
        in_specs=[SMEM] * offsets + [ANY],
        out_specs=[ANY] * offsets,
        scratch_shapes=[pltpu.SemaphoreType.DMA((offsets,))],
        compiler_params=pltpu.CompilerParams(vmem_limit_bytes=2**20),
        cost_estimate=pl.CostEstimate(flops=0, bytes_accessed=2**16, transcendentals=0),
        name="pack",
    )(*asked, panel)


def own_kernel(
    ranges, blocks, slots, tile, rows, cols, starts, panel, counts, bias, weight, *refs
):
    accs, (inverse, column, across, product, sorted_rows) = refs[:-5], refs[-5:]
    lanes = inverse.shape[1]
    row_tiles = panel.shape[1] // tile
    eye = identity(tile)
    ones = jnp.ones((tile, lanes), jnp.bfloat16)
    column[...] = jnp.broadcast_to(bias[...], column.shape[::-1]).T
    groups = starts.shape[0]
    for low, size in ranges:
        for i in range(groups):
            source = pl.multiple_of(starts[i] + low, 16)
            sorted_rows[pl.ds(groups * low + i * size, size), :] = weight[pl.ds(source, size), :]
    across[...] = dot(identity(across.shape[0]), sorted_rows[...], NT).astype(across.dtype)
    inverse[...] = jnp.ones(inverse.shape, jnp.float32)

    def block(s, carry):
        def multiply(t, inner):
            product[t] = dot(counts[s * slots + t], ones, NN)
            return inner

        def add(t, inner):
            at = pl.multiple_of(rows[s, t] * tile, tile)
            inverse[pl.ds(at, tile), :] += product[t]
            return inner

        lax.fori_loop(0, slots, multiply, 0, unroll=10)
        lax.fori_loop(0, slots, add, 0)
        return carry

    lax.fori_loop(0, blocks, block, 0)

    def start(r, carry):
        at = pl.multiple_of(r * tile, tile)
        scale = 1.0 / inverse[pl.ds(at, tile), :]
        inverse[pl.ds(at, tile), :] = scale
        for acc, (low, size) in zip(accs, ranges):
            here = dot(eye, panel[pl.ds(low, size), pl.ds(at, tile)], NT)
            acc[pl.ds(at, tile), :] = here * scale[:, :size]
        return carry

    lax.fori_loop(0, row_tiles, start, 0, unroll=4)

    for acc, (low, size) in zip(accs, ranges):

        def multiply(t, carry, low=low, size=size):
            col = pl.multiple_of(cols[0, t] * tile, tile)
            product[t, :, :size] = dot(counts[t], panel[pl.ds(low, size), pl.ds(col, tile)], NT)
            return carry

        def add(t, carry, acc=acc, size=size):
            at = pl.multiple_of(rows[0, t] * tile, tile)
            acc[pl.ds(at, tile), :] += product[t, :, :size] * inverse[pl.ds(at, tile), :size]
            return carry

        lax.fori_loop(0, slots, multiply, 0, unroll=10)
        lax.fori_loop(0, slots, add, 0)


def own(panel, rows, cols, starts, counts, bias, weight, ranges):
    blocks, slots = rows.shape
    nodes, tile = panel.shape[1], counts.shape[-1]
    lanes = max(size for _, size in ranges)
    shapes = [jax.ShapeDtypeStruct((nodes, size), jnp.float32) for _, size in ranges]
    shapes.append(jax.ShapeDtypeStruct((nodes, lanes), jnp.float32))
    shapes.append(jax.ShapeDtypeStruct((bias.shape[0], 128), bias.dtype))
    shapes.append(jax.ShapeDtypeStruct(weight.shape[::-1], weight.dtype))
    outs = call(
        functools.partial(own_kernel, ranges, blocks, slots, tile),
        "own",
        [rows, cols, starts],
        [panel, counts, bias[None, :], weight],
        shapes,
        [((slots, tile, lanes), jnp.float32), (weight.shape, weight.dtype)],
    )
    return outs[:-3], *outs[-3:]


def pick(order, nodes, stage, outs):
    count, size = stage.shape
    eye = identity(size)

    def group(i, carry):
        at = pl.multiple_of(i * UNROLL, UNROLL)
        for u in range(UNROLL):
            source = order[at + u]
            stage[pl.ds(at + u, 1), :] = nodes[pl.ds(source, 1), :]
        return carry

    lax.fori_loop(0, count // UNROLL, group, 0)
    first = 0
    for out in outs:
        columns = out.shape[1]
        for at in range(0, columns, CHUNK):
            chunk = stage[pl.ds(first + at, CHUNK), :].astype(jnp.bfloat16)
            out[:, pl.ds(at, CHUNK)] = dot(eye, chunk, NT).astype(out.dtype)
        first += columns


def add_tiles(first, rows, acc, inverse, counts, got, total, product):
    slots, tile, size = product.shape
    total[...] = acc[...]
    for s, tiles in enumerate(got, first):

        def multiply(t, carry, s=s, tiles=tiles):
            product[t] = dot(counts[s * slots + t], tiles[t], NT)
            return carry

        def add(t, carry, s=s):
            at = pl.multiple_of(rows[s, t] * tile, tile)
            total[pl.ds(at, tile), :] += product[t] * inverse[pl.ds(at, tile), :size]
            return carry

        lax.fori_loop(0, slots, multiply, 0, unroll=10)
        lax.fori_loop(0, slots, add, 0, unroll=2)


def early_kernel(first, offsets, rows, acc, inverse, counts, *refs):
    add_tiles(first, rows, acc, inverse, counts, refs[:offsets], *refs[offsets:])


def add_early(acc, inverse, rows, counts, got, first):
    slots, tile = rows.shape[1], counts.shape[-1]
    return call(
        functools.partial(early_kernel, first, len(got)),
        "add_early",
        [rows],
        [acc, inverse, counts, *got],
        [jax.ShapeDtypeStruct(acc.shape, jnp.float32)],
        [((slots, tile, acc.shape[1]), jnp.float32)],
    )[0]


def far_kernel(first, offsets, far, rows, *refs):
    orders, (acc, inverse, counts) = refs[:far], refs[far : far + 3]
    got, total = refs[far + 3 : far + 3 + offsets], refs[far + 3 + offsets]
    outs, (product, stage) = refs[far + 4 + offsets : -2], refs[-2:]
    add_tiles(first, rows, acc, inverse, counts, got, total, product)
    for order, out in zip(orders, outs):
        pick(order, total, stage, [out])


def gather_far(acc, inverse, rows, orders, counts, got, first):
    nodes, size = acc.shape
    slots, tile = rows.shape[1], counts.shape[-1]
    share, far = orders[0].shape[0], len(orders)
    outs = call(
        functools.partial(far_kernel, first, len(got), far),
        "gather_far",
        [rows, *orders],
        [acc, inverse, counts, *got],
        [jax.ShapeDtypeStruct((nodes, size), jnp.float32)]
        + [jax.ShapeDtypeStruct((size, share), jnp.bfloat16)] * far,
        [((slots, tile, size), jnp.float32), ((share, size), jnp.float32)],
        2**20,
    )
    return outs[0], outs[1:]


def next_kernel(orders, cuts_of, *refs):
    order, total, outs, stage = refs[:orders], refs[orders], refs[orders + 1 : -1], refs[-1]
    first = 0
    for indices, count in zip(order, cuts_of):
        pick(indices, total, stage, outs[first : first + count])
        first += count


def gather_next(total, orders, widths, moved=2**16):
    size = total.shape[1]
    return call(
        functools.partial(next_kernel, len(orders), tuple(len(w) for w in widths)),
        "gather_next",
        orders,
        [total],
        [jax.ShapeDtypeStruct((size, width), jnp.bfloat16) for w in widths for width in w],
        [((orders[0].shape[0], size), jnp.float32)],
        moved,
    )


def mix_kernel(places, weight, bias, *refs):
    pieces, (out, nodes, ready, sems) = refs[:-4], refs[-4:]
    copies = []
    for c in range(ready.shape[0]):
        step = ready.shape[2]
        low, high = c * step, (c + 1) * step
        for piece, (row, first) in zip(pieces, places):
            height, columns = piece.shape
            start, stop = max(low, first), min(high, first + columns)
            if start < stop:
                nodes[pl.ds(row, height), pl.ds(start, stop - start)] = piece[
                    :, pl.ds(start - first, stop - start)
                ]
        mixed = dot(weight[...], nodes[:, pl.ds(low, step)], NN)
        ready[c] = jnp.maximum(mixed + bias[:, :1], 0.0).astype(out.dtype)
        copies.append(
            pltpu.make_async_copy(ready.at[c], out.at[:, pl.ds(low, step)], sems.at[c])
        )
        copies[-1].start()
    for copy in copies:
        copy.wait()


def mix(weight, bias, placed, nodes):
    places, pieces = tuple(placed), list(placed.values())
    hidden, width = weight.shape
    step = min(512, nodes)
    return pl.pallas_call(
        functools.partial(mix_kernel, places),
        out_shape=jax.ShapeDtypeStruct((hidden, nodes), jnp.bfloat16),
        in_specs=[VMEM] * (2 + len(pieces)),
        out_specs=ANY,
        scratch_shapes=[
            pltpu.VMEM((width, nodes), jnp.bfloat16),
            pltpu.VMEM((nodes // step, hidden, step), jnp.bfloat16),
            pltpu.SemaphoreType.DMA((nodes // step,)),
        ],
        compiler_params=pltpu.CompilerParams(vmem_limit_bytes=16 * 2**20),
        cost_estimate=pl.CostEstimate(
            flops=2 * hidden * width * nodes, bytes_accessed=5 * 2**20, transcendentals=0
        ),
        name="mix",
    )(weight, bias, *pieces)


def on_device(features, tile_rows, tile_cols, tile_weights, order, weight, bias):
    width, nodes = features.shape
    _, blocks, slots, tile, _ = tile_weights.shape
    groups = lax.axis_size("grp")
    me = lax.axis_index("grp")
    share = nodes // groups
    ranges = cuts(width)
    rows = tile_rows.reshape(blocks, slots)
    cols = tile_cols.reshape(blocks, slots)
    counts = tile_weights.reshape(blocks * slots, tile, tile)

    ranks = list(range(groups - 1, -1, -1))
    whose = me ^ jnp.asarray(ranks, jnp.int32)
    far = groups - 2
    picks = [lax.dynamic_slice(order, ((me ^ k) * share,), (share,)) for k in ranks]

    asked = [shifted(cols, "blk", -s) for s in range(1, blocks)]
    *asked, panel = lax.optimization_barrier((*asked, staged(features)))
    sent = []
    for low, size in ranges:
        source = features if sent else panel
        sent.append(list(pack(source, asked, low, size, tile)))
        *asked, sent[-1][0] = lax.optimization_barrier((*asked, sent[-1][0]))
    accs, inverse, column, across = own(
        features, rows, cols, whose * width, counts, bias, weight, ranges
    )
    accs, picks = lax.optimization_barrier((accs, picks))

    got, early = [], []
    for p, leaving in enumerate(sent):
        if p:
            leaving, got[-1], early[-1], accs = lax.optimization_barrier(
                (leaving, got[-1], early[-1], accs)
            )
        got.append([shifted(value, "blk", s + 1) for s, value in enumerate(leaving)])
        early.append(add_early(accs[p], inverse, rows, counts, got[p][:-1], 1))

    pieces, across_x, beside = {}, {}, {}
    for p, (low, size) in enumerate(ranges[:-1]):
        at = [groups * low + i * size for i in range(groups)]
        total, out_far = gather_far(
            early[p], inverse, rows, picks[:far], counts, got[p][-1:], blocks - 1
        )
        for i, piece in enumerate(out_far):
            across_x[at[i], 0] = traded(piece, "grp", ranks[i])
        halves = (share // 2, share // 2)
        near = gather_next(total, picks[far:], [halves, (share,)])
        near, early[p + 1], got[p + 1] = lax.optimization_barrier(
            (near, early[p + 1], got[p + 1])
        )
        beside[at[far], 0] = traded(near[0], "grp", 1)
        beside[at[far], share // 2] = traded(near[1], "grp", 1)
        pieces[at[far + 1], 0] = near[2]

    low, size = ranges[-1]
    at = [groups * low + i * size for i in range(groups)]
    total, (piece,) = gather_far(
        early[-1], inverse, rows, picks[:1], counts, got[-1][-1:], blocks - 1
    )
    first = traded(piece, "grp", ranks[0])
    for i in range(1, groups):
        widths, moved = (share,), 2**16
        if i < far:
            total, beside = lax.optimization_barrier((total, beside))
        elif i == far:
            total, across_x = lax.optimization_barrier((total, across_x))
            widths = (share // 2, share // 2)
        else:
            total, first = lax.optimization_barrier((total, first))
            moved = 2**22
        column_at = 0
        for piece in gather_next(total, [picks[i]], [widths], moved):
            pieces[at[i], column_at] = traded(piece, "grp", ranks[i]) if ranks[i] else piece
            column_at += piece.shape[1]
    pieces[at[0], 0] = first
    pieces.update(beside)
    pieces.update(across_x)
    return mix(across, column, pieces, share)


def solution(mesh):
    in_specs = (
        P("grp", ("parts", "blk")),
        P(("parts", "blk"), None, None),
        P(("parts", "blk"), None, None),
        P(("parts", "blk"), None, None, None, None),
        P(("parts", "blk")),
        P(),
        P(),
    )
    out_specs = P(None, ("parts", "blk", "grp"))
    return jax.shard_map(
        on_device, mesh=mesh, in_specs=in_specs, out_specs=out_specs, check_vma=False
    )
```

```python
import functools

import jax
import jax.numpy as jnp
from jax import lax
from jax.experimental import pallas as pl
from jax.experimental.pallas import tpu as pltpu
from jax.sharding import PartitionSpec as P

NN = (((1,), (0,)), ((), ()))
NT = (((1,), (1,)), ((), ()))
VMEM = pl.BlockSpec(memory_space=pltpu.VMEM)
SMEM = pl.BlockSpec(memory_space=pltpu.SMEM)
ANY = pl.BlockSpec(memory_space=pl.ANY)
CHUNK = 256
UNROLL = 64


def dot(a, b, dims):
    return lax.dot_general(a, b, dims, preferred_element_type=jnp.float32)


def padded(shape, dtype):
    rows = 1
    for extent in shape[:-1]:
        rows *= extent
    return rows * -(-shape[-1] // 128) * 128 * jnp.dtype(dtype).itemsize


def call(kernel, name, scalars, arrays, outs, scratch=(), moved=2**16):
    held = sum(padded(a.shape, a.dtype) for a in list(arrays) + list(outs))
    held += sum(padded(shape, dtype) for shape, dtype in scratch)
    return pl.pallas_call(
        kernel,
        out_shape=list(outs),
        in_specs=[SMEM] * len(scalars) + [VMEM] * len(arrays),
        out_specs=[VMEM] * len(outs),
        scratch_shapes=[pltpu.VMEM(shape, dtype) for shape, dtype in scratch],
        compiler_params=pltpu.CompilerParams(vmem_limit_bytes=held + 2**20),
        cost_estimate=pl.CostEstimate(flops=0, bytes_accessed=moved, transcendentals=0),
        name=name,
    )(*scalars, *arrays)


def shifted(value, axis, steps):
    count = lax.axis_size(axis)
    pairs = [(source, (source + steps) % count) for source in range(count)]
    return lax.ppermute(value, axis, pairs)


def traded(value, axis, k):
    return lax.ppermute(value, axis, [(i, i ^ k) for i in range(lax.axis_size(axis))])


def cuts(width):
    first = width * 5 // 8 // 16 * 16
    return ((0, first), (first, width - first))


def identity(size):
    row = lax.broadcasted_iota(jnp.int32, (size, size), 0)
    col = lax.broadcasted_iota(jnp.int32, (size, size), 1)
    return (row == col).astype(jnp.float32).astype(jnp.bfloat16)


def stage_kernel(panel, out):
    out[...] = panel[...]


def staged(panel):
    shape = jax.ShapeDtypeStruct(panel.shape, panel.dtype)
    return call(stage_kernel, "stage", [], [panel], [shape])[0]


def pack_kernel(low, size, offsets, slots, tile, *refs):
    asked, panel = refs[:offsets], refs[offsets]
    outs, sems = refs[offsets + 1 : -1], refs[-1]
    for s in range(offsets):

        def body(t, carry, s=s):
            at = pl.multiple_of(asked[s][s + 1, t] * tile, tile)
            pltpu.make_async_copy(
                panel.at[pl.ds(low, size), pl.ds(at, tile)], outs[s].at[t], sems.at[s]
            ).start()
            return carry

        lax.fori_loop(0, slots, body, 0, unroll=4)
    for s in range(offsets):
        pltpu.make_async_copy(outs[s], outs[s], sems.at[s]).wait()


def pack(panel, asked, low, size, tile):
    offsets, slots = len(asked), asked[0].shape[1]
    return pl.pallas_call(
        functools.partial(pack_kernel, low, size, offsets, slots, tile),
        out_shape=[jax.ShapeDtypeStruct((slots, size, tile), panel.dtype)] * offsets,
        in_specs=[SMEM] * offsets + [ANY],
        out_specs=[ANY] * offsets,
        scratch_shapes=[pltpu.SemaphoreType.DMA((offsets,))],
        compiler_params=pltpu.CompilerParams(vmem_limit_bytes=2**20),
        cost_estimate=pl.CostEstimate(flops=0, bytes_accessed=2**16, transcendentals=0),
        name="pack",
    )(*asked, panel)


def own_kernel(
    ranges, blocks, slots, tile, rows, cols, starts, panel, counts, bias, weight, *refs
):
    accs, (inverse, column, across, product, sorted_rows) = refs[:-5], refs[-5:]
    lanes = inverse.shape[1]
    row_tiles = panel.shape[1] // tile
    eye = identity(tile)
    ones = jnp.ones((tile, lanes), jnp.bfloat16)
    column[...] = jnp.broadcast_to(bias[...], column.shape[::-1]).T
    groups = starts.shape[0]
    for low, size in ranges:
        for i in range(groups):
            source = pl.multiple_of(starts[i] + low, 16)
            sorted_rows[pl.ds(groups * low + i * size, size), :] = weight[pl.ds(source, size), :]
    across[...] = dot(identity(across.shape[0]), sorted_rows[...], NT).astype(across.dtype)
    inverse[...] = jnp.ones(inverse.shape, jnp.float32)

    def block(s, carry):
        def multiply(t, inner):
            product[t] = dot(counts[s * slots + t], ones, NN)
            return inner

        def add(t, inner):
            at = pl.multiple_of(rows[s, t] * tile, tile)
            inverse[pl.ds(at, tile), :] += product[t]
            return inner

        lax.fori_loop(0, slots, multiply, 0, unroll=10)
        lax.fori_loop(0, slots, add, 0)
        return carry

    lax.fori_loop(0, blocks, block, 0)

    def start(r, carry):
        at = pl.multiple_of(r * tile, tile)
        scale = 1.0 / inverse[pl.ds(at, tile), :]
        inverse[pl.ds(at, tile), :] = scale
        for acc, (low, size) in zip(accs, ranges):
            here = dot(eye, panel[pl.ds(low, size), pl.ds(at, tile)], NT)
            acc[pl.ds(at, tile), :] = here * scale[:, :size]
        return carry

    lax.fori_loop(0, row_tiles, start, 0, unroll=4)

    for acc, (low, size) in zip(accs, ranges):

        def multiply(t, carry, low=low, size=size):
            col = pl.multiple_of(cols[0, t] * tile, tile)
            product[t, :, :size] = dot(counts[t], panel[pl.ds(low, size), pl.ds(col, tile)], NT)
            return carry

        def add(t, carry, acc=acc, size=size):
            at = pl.multiple_of(rows[0, t] * tile, tile)
            acc[pl.ds(at, tile), :] += product[t, :, :size] * inverse[pl.ds(at, tile), :size]
            return carry

        lax.fori_loop(0, slots, multiply, 0, unroll=10)
        lax.fori_loop(0, slots, add, 0)


def own(panel, rows, cols, starts, counts, bias, weight, ranges):
    blocks, slots = rows.shape
    nodes, tile = panel.shape[1], counts.shape[-1]
    lanes = max(size for _, size in ranges)
    shapes = [jax.ShapeDtypeStruct((nodes, size), jnp.float32) for _, size in ranges]
    shapes.append(jax.ShapeDtypeStruct((nodes, lanes), jnp.float32))
    shapes.append(jax.ShapeDtypeStruct((bias.shape[0], 128), bias.dtype))
    shapes.append(jax.ShapeDtypeStruct(weight.shape[::-1], weight.dtype))
    outs = call(
        functools.partial(own_kernel, ranges, blocks, slots, tile),
        "own",
        [rows, cols, starts],
        [panel, counts, bias[None, :], weight],
        shapes,
        [((slots, tile, lanes), jnp.float32), (weight.shape, weight.dtype)],
    )
    return outs[:-3], *outs[-3:]


def pick(order, nodes, stage, outs):
    count, size = stage.shape
    eye = identity(size)

    def group(i, carry):
        at = pl.multiple_of(i * UNROLL, UNROLL)
        for u in range(UNROLL):
            source = order[at + u]
            row = nodes[pl.ds(source, 1), :] if len(nodes.shape) == 2 else nodes[source]
            stage[pl.ds(at + u, 1), :] = row
        return carry

    lax.fori_loop(0, count // UNROLL, group, 0)
    first = 0
    for out in outs:
        columns = out.shape[1]
        for at in range(0, columns, CHUNK):
            chunk = stage[pl.ds(first + at, CHUNK), :].astype(jnp.bfloat16)
            out[:, pl.ds(at, CHUNK)] = dot(eye, chunk, NT).astype(out.dtype)
        first += columns


def add_tiles(first, rows, acc, inverse, counts, got, total, product):
    slots, tile, size = product.shape
    total[...] = acc[...]
    for s, tiles in enumerate(got, first):

        def multiply(t, carry, s=s, tiles=tiles):
            product[t] = dot(counts[s * slots + t], tiles[t], NT)
            return carry

        def add(t, carry, s=s):
            at = pl.multiple_of(rows[s, t] * tile, tile)
            total[pl.ds(at, tile), :] += product[t] * inverse[pl.ds(at, tile), :size]
            return carry

        lax.fori_loop(0, slots, multiply, 0, unroll=10)
        lax.fori_loop(0, slots, add, 0, unroll=2)


def early_kernel(first, offsets, rows, acc, inverse, counts, *refs):
    add_tiles(first, rows, acc, inverse, counts, refs[:offsets], *refs[offsets:])


def add_early(acc, inverse, rows, counts, got, first):
    slots, tile = rows.shape[1], counts.shape[-1]
    return call(
        functools.partial(early_kernel, first, len(got)),
        "add_early",
        [rows],
        [acc, inverse, counts, *got],
        [jax.ShapeDtypeStruct(acc.shape, jnp.float32)],
        [((slots, tile, acc.shape[1]), jnp.float32)],
    )[0]


def far_kernel(first, offsets, far, rows, *refs):
    orders, (acc, inverse, counts) = refs[:far], refs[far : far + 3]
    got, total = refs[far + 3 : far + 3 + offsets], refs[far + 3 + offsets]
    outs, (product, stage) = refs[far + 4 + offsets : -2], refs[-2:]
    add_tiles(first, rows, acc, inverse, counts, got, total, product)
    for order, out in zip(orders, outs):
        pick(order, total, stage, [out])


def gather_far(acc, inverse, rows, orders, counts, got, first):
    nodes, size = acc.shape
    slots, tile = rows.shape[1], counts.shape[-1]
    share, far = orders[0].shape[0], len(orders)
    outs = call(
        functools.partial(far_kernel, first, len(got), far),
        "gather_far",
        [rows, *orders],
        [acc, inverse, counts, *got],
        [jax.ShapeDtypeStruct((nodes, size), jnp.float32)]
        + [jax.ShapeDtypeStruct((size, share), jnp.bfloat16)] * far,
        [((slots, tile, size), jnp.float32), ((share, size), jnp.float32)],
        2**20,
    )
    return outs[0], outs[1:]


def next_kernel(orders, cuts_of, *refs):
    order, total, outs, stage = refs[:orders], refs[orders], refs[orders + 1 : -1], refs[-1]
    first = 0
    for indices, count in zip(order, cuts_of):
        pick(indices, total, stage, outs[first : first + count])
        first += count


def gather_next(total, orders, widths, moved=2**16):
    nodes, size = total.shape
    total = total.reshape(nodes, 1, size)
    return call(
        functools.partial(next_kernel, len(orders), tuple(len(w) for w in widths)),
        "gather_next",
        orders,
        [total],
        [jax.ShapeDtypeStruct((size, width), jnp.bfloat16) for w in widths for width in w],
        [((orders[0].shape[0], size), jnp.float32)],
        moved,
    )


def mix_kernel(places, weight, bias, *refs):
    pieces, (out, nodes, ready, sems) = refs[:-4], refs[-4:]
    copies = []
    for c in range(ready.shape[0]):
        step = ready.shape[2]
        low, high = c * step, (c + 1) * step
        for piece, (row, first) in zip(pieces, places):
            height, columns = piece.shape
            start, stop = max(low, first), min(high, first + columns)
            if start < stop:
                nodes[pl.ds(row, height), pl.ds(start, stop - start)] = piece[
                    :, pl.ds(start - first, stop - start)
                ]
        mixed = dot(weight[...], nodes[:, pl.ds(low, step)], NN)
        ready[c] = jnp.maximum(mixed + bias[:, :1], 0.0).astype(out.dtype)
        copies.append(
            pltpu.make_async_copy(ready.at[c], out.at[:, pl.ds(low, step)], sems.at[c])
        )
        copies[-1].start()
    for copy in copies:
        copy.wait()


def mix(weight, bias, placed, nodes):
    places, pieces = tuple(placed), list(placed.values())
    hidden, width = weight.shape
    step = min(512, nodes)
    return pl.pallas_call(
        functools.partial(mix_kernel, places),
        out_shape=jax.ShapeDtypeStruct((hidden, nodes), jnp.bfloat16),
        in_specs=[VMEM] * (2 + len(pieces)),
        out_specs=ANY,
        scratch_shapes=[
            pltpu.VMEM((width, nodes), jnp.bfloat16),
            pltpu.VMEM((nodes // step, hidden, step), jnp.bfloat16),
            pltpu.SemaphoreType.DMA((nodes // step,)),
        ],
        compiler_params=pltpu.CompilerParams(vmem_limit_bytes=16 * 2**20),
        cost_estimate=pl.CostEstimate(
            flops=2 * hidden * width * nodes, bytes_accessed=5 * 2**20, transcendentals=0
        ),
        name="mix",
    )(weight, bias, *pieces)


def on_device(features, tile_rows, tile_cols, tile_weights, order, weight, bias):
    width, nodes = features.shape
    _, blocks, slots, tile, _ = tile_weights.shape
    groups = lax.axis_size("grp")
    me = lax.axis_index("grp")
    share = nodes // groups
    ranges = cuts(width)
    rows = tile_rows.reshape(blocks, slots)
    cols = tile_cols.reshape(blocks, slots)
    counts = tile_weights.reshape(blocks * slots, tile, tile)

    ranks = list(range(groups - 1, -1, -1))
    whose = me ^ jnp.asarray(ranks, jnp.int32)
    far = groups - 2
    picks = [lax.dynamic_slice(order, ((me ^ k) * share,), (share,)) for k in ranks]

    asked = [shifted(cols, "blk", -s) for s in range(1, blocks)]
    *asked, panel = lax.optimization_barrier((*asked, staged(features)))
    sent = []
    for low, size in ranges:
        source = features if sent else panel
        sent.append(list(pack(source, asked, low, size, tile)))
        *asked, sent[-1][0] = lax.optimization_barrier((*asked, sent[-1][0]))
    accs, inverse, column, across = own(
        features, rows, cols, whose * width, counts, bias, weight, ranges
    )
    accs, picks = lax.optimization_barrier((accs, picks))

    got, early = [], []
    for p, leaving in enumerate(sent):
        if p:
            leaving, got[-1], early[-1], accs = lax.optimization_barrier(
                (leaving, got[-1], early[-1], accs)
            )
        got.append([shifted(value, "blk", s + 1) for s, value in enumerate(leaving)])
        early.append(add_early(accs[p], inverse, rows, counts, got[p][:-1], 1))

    pieces, across_x, beside = {}, {}, {}
    for p, (low, size) in enumerate(ranges[:-1]):
        at = [groups * low + i * size for i in range(groups)]
        total, out_far = gather_far(
            early[p], inverse, rows, picks[:far], counts, got[p][-1:], blocks - 1
        )
        for i, piece in enumerate(out_far):
            across_x[at[i], 0] = traded(piece, "grp", ranks[i])
        halves = (share // 2, share // 2)
        near = gather_next(total, picks[far:], [halves, (share,)])
        near, early[p + 1], got[p + 1] = lax.optimization_barrier(
            (near, early[p + 1], got[p + 1])
        )
        beside[at[far], 0] = traded(near[0], "grp", 1)
        beside[at[far], share // 2] = traded(near[1], "grp", 1)
        pieces[at[far + 1], 0] = near[2]

    low, size = ranges[-1]
    at = [groups * low + i * size for i in range(groups)]
    total, (piece,) = gather_far(
        early[-1], inverse, rows, picks[:1], counts, got[-1][-1:], blocks - 1
    )
    first = traded(piece, "grp", ranks[0])
    for i in range(1, groups):
        widths, moved = (share,), 2**16
        if i < far:
            total, beside = lax.optimization_barrier((total, beside))
        elif i == far:
            total, across_x = lax.optimization_barrier((total, across_x))
            widths = (share // 2, share // 2)
        else:
            total, first = lax.optimization_barrier((total, first))
            moved = 2**22
        column_at = 0
        for piece in gather_next(total, [picks[i]], [widths], moved):
            pieces[at[i], column_at] = traded(piece, "grp", ranks[i]) if ranks[i] else piece
            column_at += piece.shape[1]
    pieces[at[0], 0] = first
    pieces.update(beside)
    pieces.update(across_x)
    return mix(across, column, pieces, share)


def solution(mesh):
    in_specs = (
        P("grp", ("parts", "blk")),
        P(("parts", "blk"), None, None),
        P(("parts", "blk"), None, None),
        P(("parts", "blk"), None, None, None, None),
        P(("parts", "blk")),
        P(),
        P(),
    )
    out_specs = P(None, ("parts", "blk", "grp"))
    return jax.shard_map(
        on_device, mesh=mesh, in_specs=in_specs, out_specs=out_specs, check_vma=False
    )
```

```python
import functools

import jax
import jax.numpy as jnp
from jax import lax
from jax.experimental import pallas as pl
from jax.experimental.pallas import tpu as pltpu
from jax.sharding import PartitionSpec as P

NN = (((1,), (0,)), ((), ()))
NT = (((1,), (1,)), ((), ()))
VMEM = pl.BlockSpec(memory_space=pltpu.VMEM)
SMEM = pl.BlockSpec(memory_space=pltpu.SMEM)
ANY = pl.BlockSpec(memory_space=pl.ANY)
CHUNK = 256
UNROLL = 64


def dot(a, b, dims):
    return lax.dot_general(a, b, dims, preferred_element_type=jnp.float32)


def padded(shape, dtype):
    rows = 1
    for extent in shape[:-1]:
        rows *= extent
    return rows * -(-shape[-1] // 128) * 128 * jnp.dtype(dtype).itemsize


def call(kernel, name, scalars, arrays, outs, scratch=(), moved=2**16):
    held = sum(padded(a.shape, a.dtype) for a in list(arrays) + list(outs))
    held += sum(padded(shape, dtype) for shape, dtype in scratch)
    return pl.pallas_call(
        kernel,
        out_shape=list(outs),
        in_specs=[SMEM] * len(scalars) + [VMEM] * len(arrays),
        out_specs=[VMEM] * len(outs),
        scratch_shapes=[pltpu.VMEM(shape, dtype) for shape, dtype in scratch],
        compiler_params=pltpu.CompilerParams(vmem_limit_bytes=held + 2**20),
        cost_estimate=pl.CostEstimate(flops=0, bytes_accessed=moved, transcendentals=0),
        name=name,
    )(*scalars, *arrays)


def shifted(value, axis, steps):
    count = lax.axis_size(axis)
    pairs = [(source, (source + steps) % count) for source in range(count)]
    return lax.ppermute(value, axis, pairs)


def traded(value, axis, k):
    return lax.ppermute(value, axis, [(i, i ^ k) for i in range(lax.axis_size(axis))])


def cuts(width):
    first = width * 5 // 8 // 16 * 16
    return ((0, first), (first, width - first))


def identity(size):
    row = lax.broadcasted_iota(jnp.int32, (size, size), 0)
    col = lax.broadcasted_iota(jnp.int32, (size, size), 1)
    return (row == col).astype(jnp.float32).astype(jnp.bfloat16)


def stage_kernel(panel, out):
    out[...] = panel[...]


def staged(panel):
    shape = jax.ShapeDtypeStruct(panel.shape, panel.dtype)
    return call(stage_kernel, "stage", [], [panel], [shape])[0]


def pack_kernel(low, size, offsets, slots, tile, *refs):
    asked, panel = refs[:offsets], refs[offsets]
    outs, sems = refs[offsets + 1 : -1], refs[-1]
    for s in range(offsets):

        def body(t, carry, s=s):
            at = pl.multiple_of(asked[s][s + 1, t] * tile, tile)
            pltpu.make_async_copy(
                panel.at[pl.ds(low, size), pl.ds(at, tile)], outs[s].at[t], sems.at[s]
            ).start()
            return carry

        lax.fori_loop(0, slots, body, 0, unroll=4)
    for s in range(offsets):
        pltpu.make_async_copy(outs[s], outs[s], sems.at[s]).wait()


def pack(panel, asked, low, size, tile):
    offsets, slots = len(asked), asked[0].shape[1]
    return pl.pallas_call(
        functools.partial(pack_kernel, low, size, offsets, slots, tile),
        out_shape=[jax.ShapeDtypeStruct((slots, size, tile), panel.dtype)] * offsets,
        in_specs=[SMEM] * offsets + [ANY],
        out_specs=[ANY] * offsets,
        scratch_shapes=[pltpu.SemaphoreType.DMA((offsets,))],
        compiler_params=pltpu.CompilerParams(vmem_limit_bytes=2**20),
        cost_estimate=pl.CostEstimate(flops=0, bytes_accessed=2**16, transcendentals=0),
        name="pack",
    )(*asked, panel)


def own_kernel(
    ranges, blocks, slots, tile, rows, cols, starts, panel, counts, bias, weight, *refs
):
    accs, (inverse, column, across, product, sorted_rows) = refs[:-5], refs[-5:]
    lanes = inverse.shape[1]
    row_tiles = panel.shape[1] // tile
    eye = identity(tile)
    ones = jnp.ones((tile, lanes), jnp.bfloat16)
    column[...] = jnp.broadcast_to(bias[...], column.shape[::-1]).T
    groups = starts.shape[0]
    for low, size in ranges:
        for i in range(groups):
            source = pl.multiple_of(starts[i] + low, 16)
            sorted_rows[pl.ds(groups * low + i * size, size), :] = weight[pl.ds(source, size), :]
    across[...] = dot(identity(across.shape[0]), sorted_rows[...], NT).astype(across.dtype)
    inverse[...] = jnp.ones(inverse.shape, jnp.float32)

    def block(s, carry):
        def multiply(t, inner):
            product[t] = dot(counts[s * slots + t], ones, NN)
            return inner

        def add(t, inner):
            at = pl.multiple_of(rows[s, t] * tile, tile)
            inverse[pl.ds(at, tile), :] += product[t]
            return inner

        lax.fori_loop(0, slots, multiply, 0, unroll=10)
        lax.fori_loop(0, slots, add, 0)
        return carry

    lax.fori_loop(0, blocks, block, 0)

    def start(r, carry):
        at = pl.multiple_of(r * tile, tile)
        scale = 1.0 / inverse[pl.ds(at, tile), :]
        inverse[pl.ds(at, tile), :] = scale
        for acc, (low, size) in zip(accs, ranges):
            here = dot(eye, panel[pl.ds(low, size), pl.ds(at, tile)], NT)
            acc[pl.ds(at, tile), :] = here * scale[:, :size]
        return carry

    lax.fori_loop(0, row_tiles, start, 0, unroll=4)

    for acc, (low, size) in zip(accs, ranges):

        def multiply(t, carry, low=low, size=size):
            col = pl.multiple_of(cols[0, t] * tile, tile)
            product[t, :, :size] = dot(counts[t], panel[pl.ds(low, size), pl.ds(col, tile)], NT)
            return carry

        def add(t, carry, acc=acc, size=size):
            at = pl.multiple_of(rows[0, t] * tile, tile)
            acc[pl.ds(at, tile), :] += product[t, :, :size] * inverse[pl.ds(at, tile), :size]
            return carry

        lax.fori_loop(0, slots, multiply, 0, unroll=10)
        lax.fori_loop(0, slots, add, 0)


def own(panel, rows, cols, starts, counts, bias, weight, ranges):
    blocks, slots = rows.shape
    nodes, tile = panel.shape[1], counts.shape[-1]
    lanes = max(size for _, size in ranges)
    shapes = [jax.ShapeDtypeStruct((nodes, size), jnp.float32) for _, size in ranges]
    shapes.append(jax.ShapeDtypeStruct((nodes, lanes), jnp.float32))
    shapes.append(jax.ShapeDtypeStruct((bias.shape[0], 128), bias.dtype))
    shapes.append(jax.ShapeDtypeStruct(weight.shape[::-1], weight.dtype))
    outs = call(
        functools.partial(own_kernel, ranges, blocks, slots, tile),
        "own",
        [rows, cols, starts],
        [panel, counts, bias[None, :], weight],
        shapes,
        [((slots, tile, lanes), jnp.float32), (weight.shape, weight.dtype)],
    )
    return outs[:-3], *outs[-3:]


def pick(order, nodes, stage, outs):
    count, size = stage.shape
    eye = identity(size)
    place = lax.broadcasted_iota(jnp.int32, (8, size), 0)
    odd = [(place >> bit) & 1 == 1 for bit in range(3)]

    def group(i, carry):
        at = pl.multiple_of(i * UNROLL, UNROLL)
        for first in range(0, UNROLL, 8):
            rows = [
                jnp.broadcast_to(nodes[pl.ds(order[at + first + u], 1), :], (8, size))
                for u in range(8)
            ]
            for mask in odd:
                rows = [jnp.where(mask, b, a) for a, b in zip(rows[::2], rows[1::2])]
            stage[pl.ds(at + first, 8), :] = rows[0]
        return carry

    lax.fori_loop(0, count // UNROLL, group, 0)
    first = 0
    for out in outs:
        columns = out.shape[1]
        for at in range(0, columns, CHUNK):
            chunk = stage[pl.ds(first + at, CHUNK), :].astype(jnp.bfloat16)
            out[:, pl.ds(at, CHUNK)] = dot(eye, chunk, NT).astype(out.dtype)
        first += columns


def add_tiles(first, rows, acc, inverse, counts, got, total, product):
    slots, tile, size = product.shape
    total[...] = acc[...]
    for s, tiles in enumerate(got, first):

        def multiply(t, carry, s=s, tiles=tiles):
            product[t] = dot(counts[s * slots + t], tiles[t], NT)
            return carry

        def add(t, carry, s=s):
            at = pl.multiple_of(rows[s, t] * tile, tile)
            total[pl.ds(at, tile), :] += product[t] * inverse[pl.ds(at, tile), :size]
            return carry

        lax.fori_loop(0, slots, multiply, 0, unroll=10)
        lax.fori_loop(0, slots, add, 0, unroll=2)


def early_kernel(first, offsets, rows, acc, inverse, counts, *refs):
    add_tiles(first, rows, acc, inverse, counts, refs[:offsets], *refs[offsets:])


def add_early(acc, inverse, rows, counts, got, first):
    slots, tile = rows.shape[1], counts.shape[-1]
    return call(
        functools.partial(early_kernel, first, len(got)),
        "add_early",
        [rows],
        [acc, inverse, counts, *got],
        [jax.ShapeDtypeStruct(acc.shape, jnp.float32)],
        [((slots, tile, acc.shape[1]), jnp.float32)],
    )[0]


def far_kernel(first, offsets, far, rows, *refs):
    orders, (acc, inverse, counts) = refs[:far], refs[far : far + 3]
    got, total = refs[far + 3 : far + 3 + offsets], refs[far + 3 + offsets]
    outs, (product, stage) = refs[far + 4 + offsets : -2], refs[-2:]
    add_tiles(first, rows, acc, inverse, counts, got, total, product)
    for order, out in zip(orders, outs):
        pick(order, total, stage, [out])


def gather_far(acc, inverse, rows, orders, counts, got, first):
    nodes, size = acc.shape
    slots, tile = rows.shape[1], counts.shape[-1]
    share, far = orders[0].shape[0], len(orders)
    outs = call(
        functools.partial(far_kernel, first, len(got), far),
        "gather_far",
        [rows, *orders],
        [acc, inverse, counts, *got],
        [jax.ShapeDtypeStruct((nodes, size), jnp.float32)]
        + [jax.ShapeDtypeStruct((size, share), jnp.bfloat16)] * far,
        [((slots, tile, size), jnp.float32), ((share, size), jnp.float32)],
        2**20,
    )
    return outs[0], outs[1:]


def next_kernel(orders, cuts_of, *refs):
    order, total, outs, stage = refs[:orders], refs[orders], refs[orders + 1 : -1], refs[-1]
    first = 0
    for indices, count in zip(order, cuts_of):
        pick(indices, total, stage, outs[first : first + count])
        first += count


def gather_next(total, orders, widths, moved=2**16):
    size = total.shape[1]
    return call(
        functools.partial(next_kernel, len(orders), tuple(len(w) for w in widths)),
        "gather_next",
        orders,
        [total],
        [jax.ShapeDtypeStruct((size, width), jnp.bfloat16) for w in widths for width in w],
        [((orders[0].shape[0], size), jnp.float32)],
        moved,
    )


def mix_kernel(places, weight, bias, *refs):
    pieces, (out, nodes, ready, sems) = refs[:-4], refs[-4:]
    copies = []
    for c in range(ready.shape[0]):
        step = ready.shape[2]
        low, high = c * step, (c + 1) * step
        for piece, (row, first) in zip(pieces, places):
            height, columns = piece.shape
            start, stop = max(low, first), min(high, first + columns)
            if start < stop:
                nodes[pl.ds(row, height), pl.ds(start, stop - start)] = piece[
                    :, pl.ds(start - first, stop - start)
                ]
        mixed = dot(weight[...], nodes[:, pl.ds(low, step)], NN)
        ready[c] = jnp.maximum(mixed + bias[:, :1], 0.0).astype(out.dtype)
        copies.append(
            pltpu.make_async_copy(ready.at[c], out.at[:, pl.ds(low, step)], sems.at[c])
        )
        copies[-1].start()
    for copy in copies:
        copy.wait()


def mix(weight, bias, placed, nodes):
    places, pieces = tuple(placed), list(placed.values())
    hidden, width = weight.shape
    step = min(512, nodes)
    return pl.pallas_call(
        functools.partial(mix_kernel, places),
        out_shape=jax.ShapeDtypeStruct((hidden, nodes), jnp.bfloat16),
        in_specs=[VMEM] * (2 + len(pieces)),
        out_specs=ANY,
        scratch_shapes=[
            pltpu.VMEM((width, nodes), jnp.bfloat16),
            pltpu.VMEM((nodes // step, hidden, step), jnp.bfloat16),
            pltpu.SemaphoreType.DMA((nodes // step,)),
        ],
        compiler_params=pltpu.CompilerParams(vmem_limit_bytes=16 * 2**20),
        cost_estimate=pl.CostEstimate(
            flops=2 * hidden * width * nodes, bytes_accessed=5 * 2**20, transcendentals=0
        ),
        name="mix",
    )(weight, bias, *pieces)


def on_device(features, tile_rows, tile_cols, tile_weights, order, weight, bias):
    width, nodes = features.shape
    _, blocks, slots, tile, _ = tile_weights.shape
    groups = lax.axis_size("grp")
    me = lax.axis_index("grp")
    share = nodes // groups
    ranges = cuts(width)
    rows = tile_rows.reshape(blocks, slots)
    cols = tile_cols.reshape(blocks, slots)
    counts = tile_weights.reshape(blocks * slots, tile, tile)

    ranks = list(range(groups - 1, -1, -1))
    whose = me ^ jnp.asarray(ranks, jnp.int32)
    far = groups - 2
    picks = [lax.dynamic_slice(order, ((me ^ k) * share,), (share,)) for k in ranks]

    asked = [shifted(cols, "blk", -s) for s in range(1, blocks)]
    *asked, panel = lax.optimization_barrier((*asked, staged(features)))
    sent = []
    for low, size in ranges:
        source = features if sent else panel
        sent.append(list(pack(source, asked, low, size, tile)))
        *asked, sent[-1][0] = lax.optimization_barrier((*asked, sent[-1][0]))
    accs, inverse, column, across = own(
        features, rows, cols, whose * width, counts, bias, weight, ranges
    )
    accs, picks = lax.optimization_barrier((accs, picks))

    got, early = [], []
    for p, leaving in enumerate(sent):
        if p:
            leaving, got[-1], early[-1], accs = lax.optimization_barrier(
                (leaving, got[-1], early[-1], accs)
            )
        got.append([shifted(value, "blk", s + 1) for s, value in enumerate(leaving)])
        early.append(add_early(accs[p], inverse, rows, counts, got[p][:-1], 1))

    pieces, across_x, beside = {}, {}, {}
    for p, (low, size) in enumerate(ranges[:-1]):
        at = [groups * low + i * size for i in range(groups)]
        total, out_far = gather_far(
            early[p], inverse, rows, picks[:far], counts, got[p][-1:], blocks - 1
        )
        for i, piece in enumerate(out_far):
            across_x[at[i], 0] = traded(piece, "grp", ranks[i])
        halves = (share // 2, share // 2)
        near = gather_next(total, picks[far:], [halves, (share,)])
        near, early[p + 1], got[p + 1] = lax.optimization_barrier(
            (near, early[p + 1], got[p + 1])
        )
        beside[at[far], 0] = traded(near[0], "grp", 1)
        beside[at[far], share // 2] = traded(near[1], "grp", 1)
        pieces[at[far + 1], 0] = near[2]

    low, size = ranges[-1]
    at = [groups * low + i * size for i in range(groups)]
    total, (piece,) = gather_far(
        early[-1], inverse, rows, picks[:1], counts, got[-1][-1:], blocks - 1
    )
    first = traded(piece, "grp", ranks[0])
    for i in range(1, groups):
        widths, moved = (share,), 2**16
        if i < far:
            total, beside = lax.optimization_barrier((total, beside))
        elif i == far:
            total, across_x = lax.optimization_barrier((total, across_x))
            widths = (share // 2, share // 2)
        else:
            total, first = lax.optimization_barrier((total, first))
            moved = 2**22
        column_at = 0
        for piece in gather_next(total, [picks[i]], [widths], moved):
            pieces[at[i], column_at] = traded(piece, "grp", ranks[i]) if ranks[i] else piece
            column_at += piece.shape[1]
    pieces[at[0], 0] = first
    pieces.update(beside)
    pieces.update(across_x)
    return mix(across, column, pieces, share)


def solution(mesh):
    in_specs = (
        P("grp", ("parts", "blk")),
        P(("parts", "blk"), None, None),
        P(("parts", "blk"), None, None),
        P(("parts", "blk"), None, None, None, None),
        P(("parts", "blk")),
        P(),
        P(),
    )
    out_specs = P(None, ("parts", "blk", "grp"))
    return jax.shard_map(
        on_device, mesh=mesh, in_specs=in_specs, out_specs=out_specs, check_vma=False
    )
```

```python
import functools

import jax
import jax.numpy as jnp
from jax import lax
from jax.experimental import pallas as pl
from jax.experimental.pallas import tpu as pltpu
from jax.sharding import PartitionSpec as P

NN = (((1,), (0,)), ((), ()))
NT = (((1,), (1,)), ((), ()))
VMEM = pl.BlockSpec(memory_space=pltpu.VMEM)
SMEM = pl.BlockSpec(memory_space=pltpu.SMEM)
ANY = pl.BlockSpec(memory_space=pl.ANY)
CHUNK = 256
UNROLL = 32


def dot(a, b, dims):
    return lax.dot_general(a, b, dims, preferred_element_type=jnp.float32)


def padded(shape, dtype):
    rows = 1
    for extent in shape[:-1]:
        rows *= extent
    return rows * -(-shape[-1] // 128) * 128 * jnp.dtype(dtype).itemsize


def call(kernel, name, scalars, arrays, outs, scratch=(), moved=2**16):
    held = sum(padded(a.shape, a.dtype) for a in list(arrays) + list(outs))
    held += sum(padded(shape, dtype) for shape, dtype in scratch)
    return pl.pallas_call(
        kernel,
        out_shape=list(outs),
        in_specs=[SMEM] * len(scalars) + [VMEM] * len(arrays),
        out_specs=[VMEM] * len(outs),
        scratch_shapes=[pltpu.VMEM(shape, dtype) for shape, dtype in scratch],
        compiler_params=pltpu.CompilerParams(vmem_limit_bytes=held + 2**20),
        cost_estimate=pl.CostEstimate(flops=0, bytes_accessed=moved, transcendentals=0),
        name=name,
    )(*scalars, *arrays)


def shifted(value, axis, steps):
    count = lax.axis_size(axis)
    pairs = [(source, (source + steps) % count) for source in range(count)]
    return lax.ppermute(value, axis, pairs)


def traded(value, axis, k):
    return lax.ppermute(value, axis, [(i, i ^ k) for i in range(lax.axis_size(axis))])


def cuts(width):
    first = width * 5 // 8 // 16 * 16
    return ((0, first), (first, width - first))


def identity(size):
    row = lax.broadcasted_iota(jnp.int32, (size, size), 0)
    col = lax.broadcasted_iota(jnp.int32, (size, size), 1)
    return (row == col).astype(jnp.float32).astype(jnp.bfloat16)


def stage_kernel(panel, out):
    out[...] = panel[...]


def staged(panel):
    shape = jax.ShapeDtypeStruct(panel.shape, panel.dtype)
    return call(stage_kernel, "stage", [], [panel], [shape])[0]


def pack_kernel(low, size, offsets, slots, tile, *refs):
    asked, panel = refs[:offsets], refs[offsets]
    outs, sems = refs[offsets + 1 : -1], refs[-1]
    for s in range(offsets):

        def body(t, carry, s=s):
            at = pl.multiple_of(asked[s][s + 1, t] * tile, tile)
            pltpu.make_async_copy(
                panel.at[pl.ds(low, size), pl.ds(at, tile)], outs[s].at[t], sems.at[s]
            ).start()
            return carry

        lax.fori_loop(0, slots, body, 0, unroll=4)
    for s in range(offsets):
        pltpu.make_async_copy(outs[s], outs[s], sems.at[s]).wait()


def pack(panel, asked, low, size, tile):
    offsets, slots = len(asked), asked[0].shape[1]
    return pl.pallas_call(
        functools.partial(pack_kernel, low, size, offsets, slots, tile),
        out_shape=[jax.ShapeDtypeStruct((slots, size, tile), panel.dtype)] * offsets,
        in_specs=[SMEM] * offsets + [ANY],
        out_specs=[ANY] * offsets,
        scratch_shapes=[pltpu.SemaphoreType.DMA((offsets,))],
        compiler_params=pltpu.CompilerParams(vmem_limit_bytes=2**20),
        cost_estimate=pl.CostEstimate(flops=0, bytes_accessed=2**16, transcendentals=0),
        name="pack",
    )(*asked, panel)


def own_kernel(
    ranges, blocks, slots, tile, rows, cols, starts, panel, counts, bias, weight, *refs
):
    accs, (inverse, column, across, product, sorted_rows) = refs[:-5], refs[-5:]
    lanes = inverse.shape[1]
    row_tiles = panel.shape[1] // tile
    eye = identity(tile)
    ones = jnp.ones((tile, lanes), jnp.bfloat16)
    column[...] = jnp.broadcast_to(bias[...], column.shape[::-1]).T
    groups = starts.shape[0]
    for low, size in ranges:
        for i in range(groups):
            source = pl.multiple_of(starts[i] + low, 16)
            sorted_rows[pl.ds(groups * low + i * size, size), :] = weight[pl.ds(source, size), :]
    across[...] = dot(identity(across.shape[0]), sorted_rows[...], NT).astype(across.dtype)
    inverse[...] = jnp.ones(inverse.shape, jnp.float32)

    def block(s, carry):
        def multiply(t, inner):
            product[t] = dot(counts[s * slots + t], ones, NN)
            return inner

        def add(t, inner):
            at = pl.multiple_of(rows[s, t] * tile, tile)
            inverse[pl.ds(at, tile), :] += product[t]
            return inner

        lax.fori_loop(0, slots, multiply, 0, unroll=10)
        lax.fori_loop(0, slots, add, 0)
        return carry

    lax.fori_loop(0, blocks, block, 0)

    def start(r, carry):
        at = pl.multiple_of(r * tile, tile)
        scale = 1.0 / inverse[pl.ds(at, tile), :]
        inverse[pl.ds(at, tile), :] = scale
        for acc, (low, size) in zip(accs, ranges):
            here = dot(eye, panel[pl.ds(low, size), pl.ds(at, tile)], NT)
            acc[pl.ds(at, tile), :] = here * scale[:, :size]
        return carry

    lax.fori_loop(0, row_tiles, start, 0, unroll=4)

    for acc, (low, size) in zip(accs, ranges):

        def multiply(t, carry, low=low, size=size):
            col = pl.multiple_of(cols[0, t] * tile, tile)
            product[t, :, :size] = dot(counts[t], panel[pl.ds(low, size), pl.ds(col, tile)], NT)
            return carry

        def add(t, carry, acc=acc, size=size):
            at = pl.multiple_of(rows[0, t] * tile, tile)
            acc[pl.ds(at, tile), :] += product[t, :, :size] * inverse[pl.ds(at, tile), :size]
            return carry

        lax.fori_loop(0, slots, multiply, 0, unroll=10)
        lax.fori_loop(0, slots, add, 0)


def own(panel, rows, cols, starts, counts, bias, weight, ranges):
    blocks, slots = rows.shape
    nodes, tile = panel.shape[1], counts.shape[-1]
    lanes = max(size for _, size in ranges)
    shapes = [jax.ShapeDtypeStruct((nodes, size), jnp.float32) for _, size in ranges]
    shapes.append(jax.ShapeDtypeStruct((nodes, lanes), jnp.float32))
    shapes.append(jax.ShapeDtypeStruct((bias.shape[0], 128), bias.dtype))
    shapes.append(jax.ShapeDtypeStruct(weight.shape[::-1], weight.dtype))
    outs = call(
        functools.partial(own_kernel, ranges, blocks, slots, tile),
        "own",
        [rows, cols, starts],
        [panel, counts, bias[None, :], weight],
        shapes,
        [((slots, tile, lanes), jnp.float32), (weight.shape, weight.dtype)],
    )
    return outs[:-3], *outs[-3:]


def paired(order):
    half = order.shape[0] // 2
    return order[:half] | (order[half:] << 16)


def pick(order, nodes, stage, outs):
    half, size = stage.shape[0] // 2, stage.shape[1]
    eye = identity(size)

    def group(i, carry):
        at = pl.multiple_of(i * UNROLL, UNROLL)
        for u in range(UNROLL):
            pair = order[at + u]
            lower, upper = pair & 0xFFFF, lax.shift_right_logical(pair, 16)
            stage[pl.ds(at + u, 1), :] = nodes[pl.ds(lower, 1), :]
            stage[pl.ds(half + at + u, 1), :] = nodes[pl.ds(upper, 1), :]
        return carry

    lax.fori_loop(0, half // UNROLL, group, 0)
    first = 0
    for out in outs:
        columns = out.shape[1]
        for at in range(0, columns, CHUNK):
            chunk = stage[pl.ds(first + at, CHUNK), :].astype(jnp.bfloat16)
            out[:, pl.ds(at, CHUNK)] = dot(eye, chunk, NT).astype(out.dtype)
        first += columns


def add_tiles(first, rows, acc, inverse, counts, got, total, product):
    slots, tile, size = product.shape
    total[...] = acc[...]
    for s, tiles in enumerate(got, first):

        def multiply(t, carry, s=s, tiles=tiles):
            product[t] = dot(counts[s * slots + t], tiles[t], NT)
            return carry

        def add(t, carry, s=s):
            at = pl.multiple_of(rows[s, t] * tile, tile)
            total[pl.ds(at, tile), :] += product[t] * inverse[pl.ds(at, tile), :size]
            return carry

        lax.fori_loop(0, slots, multiply, 0, unroll=10)
        lax.fori_loop(0, slots, add, 0, unroll=2)


def early_kernel(first, offsets, rows, acc, inverse, counts, *refs):
    add_tiles(first, rows, acc, inverse, counts, refs[:offsets], *refs[offsets:])


def add_early(acc, inverse, rows, counts, got, first):
    slots, tile = rows.shape[1], counts.shape[-1]
    return call(
        functools.partial(early_kernel, first, len(got)),
        "add_early",
        [rows],
        [acc, inverse, counts, *got],
        [jax.ShapeDtypeStruct(acc.shape, jnp.float32)],
        [((slots, tile, acc.shape[1]), jnp.float32)],
    )[0]


def far_kernel(first, offsets, far, rows, *refs):
    orders, (acc, inverse, counts) = refs[:far], refs[far : far + 3]
    got, total = refs[far + 3 : far + 3 + offsets], refs[far + 3 + offsets]
    outs, (product, stage) = refs[far + 4 + offsets : -2], refs[-2:]
    add_tiles(first, rows, acc, inverse, counts, got, total, product)
    for order, out in zip(orders, outs):
        pick(order, total, stage, [out])


def gather_far(acc, inverse, rows, orders, counts, got, first):
    nodes, size = acc.shape
    slots, tile = rows.shape[1], counts.shape[-1]
    share, far = 2 * orders[0].shape[0], len(orders)
    outs = call(
        functools.partial(far_kernel, first, len(got), far),
        "gather_far",
        [rows, *orders],
        [acc, inverse, counts, *got],
        [jax.ShapeDtypeStruct((nodes, size), jnp.float32)]
        + [jax.ShapeDtypeStruct((size, share), jnp.bfloat16)] * far,
        [((slots, tile, size), jnp.float32), ((share, size), jnp.float32)],
        2**20,
    )
    return outs[0], outs[1:]


def next_kernel(orders, cuts_of, *refs):
    order, total, outs, stage = refs[:orders], refs[orders], refs[orders + 1 : -1], refs[-1]
    first = 0
    for indices, count in zip(order, cuts_of):
        pick(indices, total, stage, outs[first : first + count])
        first += count


def gather_next(total, orders, widths, moved=2**16):
    size = total.shape[1]
    return call(
        functools.partial(next_kernel, len(orders), tuple(len(w) for w in widths)),
        "gather_next",
        orders,
        [total],
        [jax.ShapeDtypeStruct((size, width), jnp.bfloat16) for w in widths for width in w],
        [((2 * orders[0].shape[0], size), jnp.float32)],
        moved,
    )


def mix_kernel(places, weight, bias, *refs):
    pieces, (out, nodes, ready, sems) = refs[:-4], refs[-4:]
    copies = []
    for c in range(ready.shape[0]):
        step = ready.shape[2]
        low, high = c * step, (c + 1) * step
        for piece, (row, first) in zip(pieces, places):
            height, columns = piece.shape
            start, stop = max(low, first), min(high, first + columns)
            if start < stop:
                nodes[pl.ds(row, height), pl.ds(start, stop - start)] = piece[
                    :, pl.ds(start - first, stop - start)
                ]
        mixed = dot(weight[...], nodes[:, pl.ds(low, step)], NN)
        ready[c] = jnp.maximum(mixed + bias[:, :1], 0.0).astype(out.dtype)
        copies.append(
            pltpu.make_async_copy(ready.at[c], out.at[:, pl.ds(low, step)], sems.at[c])
        )
        copies[-1].start()
    for copy in copies:
        copy.wait()


def mix(weight, bias, placed, nodes):
    places, pieces = tuple(placed), list(placed.values())
    hidden, width = weight.shape
    step = min(512, nodes)
    return pl.pallas_call(
        functools.partial(mix_kernel, places),
        out_shape=jax.ShapeDtypeStruct((hidden, nodes), jnp.bfloat16),
        in_specs=[VMEM] * (2 + len(pieces)),
        out_specs=ANY,
        scratch_shapes=[
            pltpu.VMEM((width, nodes), jnp.bfloat16),
            pltpu.VMEM((nodes // step, hidden, step), jnp.bfloat16),
            pltpu.SemaphoreType.DMA((nodes // step,)),
        ],
        compiler_params=pltpu.CompilerParams(vmem_limit_bytes=16 * 2**20),
        cost_estimate=pl.CostEstimate(
            flops=2 * hidden * width * nodes, bytes_accessed=5 * 2**20, transcendentals=0
        ),
        name="mix",
    )(weight, bias, *pieces)


def on_device(features, tile_rows, tile_cols, tile_weights, order, weight, bias):
    width, nodes = features.shape
    _, blocks, slots, tile, _ = tile_weights.shape
    groups = lax.axis_size("grp")
    me = lax.axis_index("grp")
    share = nodes // groups
    ranges = cuts(width)
    rows = tile_rows.reshape(blocks, slots)
    cols = tile_cols.reshape(blocks, slots)
    counts = tile_weights.reshape(blocks * slots, tile, tile)

    ranks = list(range(groups - 1, -1, -1))
    whose = me ^ jnp.asarray(ranks, jnp.int32)
    far = groups - 2
    picks = [paired(lax.dynamic_slice(order, ((me ^ k) * share,), (share,))) for k in ranks]

    asked = [shifted(cols, "blk", -s) for s in range(1, blocks)]
    *asked, panel = lax.optimization_barrier((*asked, staged(features)))
    sent = []
    for low, size in ranges:
        source = features if sent else panel
        sent.append(list(pack(source, asked, low, size, tile)))
        *asked, sent[-1][0] = lax.optimization_barrier((*asked, sent[-1][0]))
    accs, inverse, column, across = own(
        features, rows, cols, whose * width, counts, bias, weight, ranges
    )
    accs, picks = lax.optimization_barrier((accs, picks))

    got, early = [], []
    for p, leaving in enumerate(sent):
        if p:
            leaving, got[-1], early[-1], accs = lax.optimization_barrier(
                (leaving, got[-1], early[-1], accs)
            )
        got.append([shifted(value, "blk", s + 1) for s, value in enumerate(leaving)])
        early.append(add_early(accs[p], inverse, rows, counts, got[p][:-1], 1))

    pieces, across_x, beside = {}, {}, {}
    for p, (low, size) in enumerate(ranges[:-1]):
        at = [groups * low + i * size for i in range(groups)]
        total, out_far = gather_far(
            early[p], inverse, rows, picks[:far], counts, got[p][-1:], blocks - 1
        )
        for i, piece in enumerate(out_far):
            across_x[at[i], 0] = traded(piece, "grp", ranks[i])
        halves = (share // 2, share // 2)
        near = gather_next(total, picks[far:], [halves, (share,)])
        near, early[p + 1], got[p + 1] = lax.optimization_barrier(
            (near, early[p + 1], got[p + 1])
        )
        beside[at[far], 0] = traded(near[0], "grp", 1)
        beside[at[far], share // 2] = traded(near[1], "grp", 1)
        pieces[at[far + 1], 0] = near[2]

    low, size = ranges[-1]
    at = [groups * low + i * size for i in range(groups)]
    total, (piece,) = gather_far(
        early[-1], inverse, rows, picks[:1], counts, got[-1][-1:], blocks - 1
    )
    first = traded(piece, "grp", ranks[0])
    for i in range(1, groups):
        widths, moved = (share,), 2**16
        if i < far:
            total, beside = lax.optimization_barrier((total, beside))
        elif i == far:
            total, across_x = lax.optimization_barrier((total, across_x))
            widths = (share // 2, share // 2)
        else:
            total, first = lax.optimization_barrier((total, first))
            moved = 2**22
        column_at = 0
        for piece in gather_next(total, [picks[i]], [widths], moved):
            pieces[at[i], column_at] = traded(piece, "grp", ranks[i]) if ranks[i] else piece
            column_at += piece.shape[1]
    pieces[at[0], 0] = first
    pieces.update(beside)
    pieces.update(across_x)
    return mix(across, column, pieces, share)


def solution(mesh):
    in_specs = (
        P("grp", ("parts", "blk")),
        P(("parts", "blk"), None, None),
        P(("parts", "blk"), None, None),
        P(("parts", "blk"), None, None, None, None),
        P(("parts", "blk")),
        P(),
        P(),
    )
    out_specs = P(None, ("parts", "blk", "grp"))
    return jax.shard_map(
        on_device, mesh=mesh, in_specs=in_specs, out_specs=out_specs, check_vma=False
    )
```

```python
import functools

import jax
import jax.numpy as jnp
from jax import lax
from jax.experimental import pallas as pl
from jax.experimental.pallas import tpu as pltpu
from jax.sharding import PartitionSpec as P

NN = (((1,), (0,)), ((), ()))
NT = (((1,), (1,)), ((), ()))
VMEM = pl.BlockSpec(memory_space=pltpu.VMEM)
SMEM = pl.BlockSpec(memory_space=pltpu.SMEM)
ANY = pl.BlockSpec(memory_space=pl.ANY)
CHUNK = 256
UNROLL = 64


def dot(a, b, dims):
    return lax.dot_general(a, b, dims, preferred_element_type=jnp.float32)


def padded(shape, dtype):
    rows = 1
    for extent in shape[:-1]:
        rows *= extent
    return rows * -(-shape[-1] // 128) * 128 * jnp.dtype(dtype).itemsize


def call(kernel, name, scalars, arrays, outs, scratch=(), moved=2**16):
    held = sum(padded(a.shape, a.dtype) for a in list(arrays) + list(outs))
    held += sum(padded(shape, dtype) for shape, dtype in scratch)
    return pl.pallas_call(
        kernel,
        out_shape=list(outs),
        in_specs=[SMEM] * len(scalars) + [VMEM] * len(arrays),
        out_specs=[VMEM] * len(outs),
        scratch_shapes=[pltpu.VMEM(shape, dtype) for shape, dtype in scratch],
        compiler_params=pltpu.CompilerParams(vmem_limit_bytes=held + 2**20),
        cost_estimate=pl.CostEstimate(flops=0, bytes_accessed=moved, transcendentals=0),
        name=name,
    )(*scalars, *arrays)


def shifted(value, axis, steps):
    count = lax.axis_size(axis)
    pairs = [(source, (source + steps) % count) for source in range(count)]
    return lax.ppermute(value, axis, pairs)


def traded(value, axis, k):
    return lax.ppermute(value, axis, [(i, i ^ k) for i in range(lax.axis_size(axis))])


def cuts(width):
    first = width * 5 // 8 // 16 * 16
    return ((0, first), (first, width - first))


def identity(size):
    row = lax.broadcasted_iota(jnp.int32, (size, size), 0)
    col = lax.broadcasted_iota(jnp.int32, (size, size), 1)
    return (row == col).astype(jnp.float32).astype(jnp.bfloat16)


def stage_kernel(panel, out):
    out[...] = panel[...]


def staged(panel):
    shape = jax.ShapeDtypeStruct(panel.shape, panel.dtype)
    return call(stage_kernel, "stage", [], [panel], [shape])[0]


def pack_kernel(low, size, slots, tile, block, asked, panel, *refs):
    outs, sems = refs[:-1], refs[-1]
    offsets = len(outs)
    for s in range(offsets):
        to = lax.rem(block[0] + s + 1, asked.shape[0])

        def body(t, carry, s=s, to=to):
            at = pl.multiple_of(asked[to, s + 1, t] * tile, tile)
            pltpu.make_async_copy(
                panel.at[pl.ds(low, size), pl.ds(at, tile)], outs[s].at[t], sems.at[s]
            ).start()
            return carry

        lax.fori_loop(0, slots, body, 0, unroll=4)
    for s in range(offsets):
        pltpu.make_async_copy(outs[s], outs[s], sems.at[s]).wait()


def pack(panel, block, asked, low, size, tile):
    offsets, slots = asked.shape[1] - 1, asked.shape[2]
    return pl.pallas_call(
        functools.partial(pack_kernel, low, size, slots, tile),
        out_shape=[jax.ShapeDtypeStruct((slots, size, tile), panel.dtype)] * offsets,
        in_specs=[SMEM, SMEM, ANY],
        out_specs=[ANY] * offsets,
        scratch_shapes=[pltpu.SemaphoreType.DMA((offsets,))],
        compiler_params=pltpu.CompilerParams(vmem_limit_bytes=2**20),
        cost_estimate=pl.CostEstimate(flops=0, bytes_accessed=2**16, transcendentals=0),
        name="pack",
    )(block, asked, panel)


def own_kernel(
    ranges, blocks, slots, tile, rows, cols, starts, panel, counts, bias, weight, *refs
):
    accs, (inverse, column, across, product, sorted_rows) = refs[:-5], refs[-5:]
    lanes = inverse.shape[1]
    row_tiles = panel.shape[1] // tile
    eye = identity(tile)
    ones = jnp.ones((tile, lanes), jnp.bfloat16)
    column[...] = jnp.broadcast_to(bias[...], column.shape[::-1]).T
    groups = starts.shape[0]
    for low, size in ranges:
        for i in range(groups):
            source = pl.multiple_of(starts[i] + low, 16)
            sorted_rows[pl.ds(groups * low + i * size, size), :] = weight[pl.ds(source, size), :]
    across[...] = dot(identity(across.shape[0]), sorted_rows[...], NT).astype(across.dtype)
    inverse[...] = jnp.ones(inverse.shape, jnp.float32)

    def block(s, carry):
        def multiply(t, inner):
            product[t] = dot(counts[s * slots + t], ones, NN)
            return inner

        def add(t, inner):
            at = pl.multiple_of(rows[s, t] * tile, tile)
            inverse[pl.ds(at, tile), :] += product[t]
            return inner

        lax.fori_loop(0, slots, multiply, 0, unroll=10)
        lax.fori_loop(0, slots, add, 0)
        return carry

    lax.fori_loop(0, blocks, block, 0)

    def start(r, carry):
        at = pl.multiple_of(r * tile, tile)
        scale = 1.0 / inverse[pl.ds(at, tile), :]
        inverse[pl.ds(at, tile), :] = scale
        for acc, (low, size) in zip(accs, ranges):
            here = dot(eye, panel[pl.ds(low, size), pl.ds(at, tile)], NT)
            acc[pl.ds(at, tile), :] = here * scale[:, :size]
        return carry

    lax.fori_loop(0, row_tiles, start, 0, unroll=4)

    for acc, (low, size) in zip(accs, ranges):

        def multiply(t, carry, low=low, size=size):
            col = pl.multiple_of(cols[0, t] * tile, tile)
            product[t, :, :size] = dot(counts[t], panel[pl.ds(low, size), pl.ds(col, tile)], NT)
            return carry

        def add(t, carry, acc=acc, size=size):
            at = pl.multiple_of(rows[0, t] * tile, tile)
            acc[pl.ds(at, tile), :] += product[t, :, :size] * inverse[pl.ds(at, tile), :size]
            return carry

        lax.fori_loop(0, slots, multiply, 0, unroll=10)
        lax.fori_loop(0, slots, add, 0)


def own(panel, rows, cols, starts, counts, bias, weight, ranges):
    blocks, slots = rows.shape
    nodes, tile = panel.shape[1], counts.shape[-1]
    lanes = max(size for _, size in ranges)
    shapes = [jax.ShapeDtypeStruct((nodes, size), jnp.float32) for _, size in ranges]
    shapes.append(jax.ShapeDtypeStruct((nodes, lanes), jnp.float32))
    shapes.append(jax.ShapeDtypeStruct((bias.shape[0], 128), bias.dtype))
    shapes.append(jax.ShapeDtypeStruct(weight.shape[::-1], weight.dtype))
    outs = call(
        functools.partial(own_kernel, ranges, blocks, slots, tile),
        "own",
        [rows, cols, starts],
        [panel, counts, bias[None, :], weight],
        shapes,
        [((slots, tile, lanes), jnp.float32), (weight.shape, weight.dtype)],
    )
    return outs[:-3], *outs[-3:]


def pick(order, nodes, stage, outs):
    count, size = stage.shape
    eye = identity(size)

    def group(i, carry):
        at = pl.multiple_of(i * UNROLL, UNROLL)
        for u in range(UNROLL):
            source = order[at + u]
            stage[pl.ds(at + u, 1), :] = nodes[pl.ds(source, 1), :]
        return carry

    lax.fori_loop(0, count // UNROLL, group, 0)
    first = 0
    for out in outs:
        columns = out.shape[1]
        for at in range(0, columns, CHUNK):
            chunk = stage[pl.ds(first + at, CHUNK), :].astype(jnp.bfloat16)
            out[:, pl.ds(at, CHUNK)] = dot(eye, chunk, NT).astype(out.dtype)
        first += columns


def add_tiles(first, rows, acc, inverse, counts, got, total, product):
    slots, tile, size = product.shape
    total[...] = acc[...]
    for s, tiles in enumerate(got, first):

        def multiply(t, carry, s=s, tiles=tiles):
            product[t] = dot(counts[s * slots + t], tiles[t], NT)
            return carry

        def add(t, carry, s=s):
            at = pl.multiple_of(rows[s, t] * tile, tile)
            total[pl.ds(at, tile), :] += product[t] * inverse[pl.ds(at, tile), :size]
            return carry

        lax.fori_loop(0, slots, multiply, 0, unroll=10)
        lax.fori_loop(0, slots, add, 0, unroll=2)


def early_kernel(first, offsets, rows, acc, inverse, counts, *refs):
    add_tiles(first, rows, acc, inverse, counts, refs[:offsets], *refs[offsets:])


def add_early(acc, inverse, rows, counts, got, first):
    slots, tile = rows.shape[1], counts.shape[-1]
    return call(
        functools.partial(early_kernel, first, len(got)),
        "add_early",
        [rows],
        [acc, inverse, counts, *got],
        [jax.ShapeDtypeStruct(acc.shape, jnp.float32)],
        [((slots, tile, acc.shape[1]), jnp.float32)],
    )[0]


def far_kernel(first, offsets, far, rows, *refs):
    orders, (acc, inverse, counts) = refs[:far], refs[far : far + 3]
    got, total = refs[far + 3 : far + 3 + offsets], refs[far + 3 + offsets]
    outs, (product, stage) = refs[far + 4 + offsets : -2], refs[-2:]
    add_tiles(first, rows, acc, inverse, counts, got, total, product)
    for order, out in zip(orders, outs):
        pick(order, total, stage, [out])


def gather_far(acc, inverse, rows, orders, counts, got, first):
    nodes, size = acc.shape
    slots, tile = rows.shape[1], counts.shape[-1]
    share, far = orders[0].shape[0], len(orders)
    outs = call(
        functools.partial(far_kernel, first, len(got), far),
        "gather_far",
        [rows, *orders],
        [acc, inverse, counts, *got],
        [jax.ShapeDtypeStruct((nodes, size), jnp.float32)]
        + [jax.ShapeDtypeStruct((size, share), jnp.bfloat16)] * far,
        [((slots, tile, size), jnp.float32), ((share, size), jnp.float32)],
        2**20,
    )
    return outs[0], outs[1:]


def next_kernel(orders, cuts_of, *refs):
    order, total, outs, stage = refs[:orders], refs[orders], refs[orders + 1 : -1], refs[-1]
    first = 0
    for indices, count in zip(order, cuts_of):
        pick(indices, total, stage, outs[first : first + count])
        first += count


def gather_next(total, orders, widths, moved=2**16):
    size = total.shape[1]
    return call(
        functools.partial(next_kernel, len(orders), tuple(len(w) for w in widths)),
        "gather_next",
        orders,
        [total],
        [jax.ShapeDtypeStruct((size, width), jnp.bfloat16) for w in widths for width in w],
        [((orders[0].shape[0], size), jnp.float32)],
        moved,
    )


def mix_kernel(places, weight, bias, *refs):
    pieces, (out, nodes, ready, sems) = refs[:-4], refs[-4:]
    copies = []
    for c in range(ready.shape[0]):
        step = ready.shape[2]
        low, high = c * step, (c + 1) * step
        for piece, (row, first) in zip(pieces, places):
            height, columns = piece.shape
            start, stop = max(low, first), min(high, first + columns)
            if start < stop:
                nodes[pl.ds(row, height), pl.ds(start, stop - start)] = piece[
                    :, pl.ds(start - first, stop - start)
                ]
        mixed = dot(weight[...], nodes[:, pl.ds(low, step)], NN)
        ready[c] = jnp.maximum(mixed + bias[:, :1], 0.0).astype(out.dtype)
        copies.append(
            pltpu.make_async_copy(ready.at[c], out.at[:, pl.ds(low, step)], sems.at[c])
        )
        copies[-1].start()
    for copy in copies:
        copy.wait()


def mix(weight, bias, placed, nodes):
    places, pieces = tuple(placed), list(placed.values())
    hidden, width = weight.shape
    step = min(512, nodes)
    return pl.pallas_call(
        functools.partial(mix_kernel, places),
        out_shape=jax.ShapeDtypeStruct((hidden, nodes), jnp.bfloat16),
        in_specs=[VMEM] * (2 + len(pieces)),
        out_specs=ANY,
        scratch_shapes=[
            pltpu.VMEM((width, nodes), jnp.bfloat16),
            pltpu.VMEM((nodes // step, hidden, step), jnp.bfloat16),
            pltpu.SemaphoreType.DMA((nodes // step,)),
        ],
        compiler_params=pltpu.CompilerParams(vmem_limit_bytes=16 * 2**20),
        cost_estimate=pl.CostEstimate(
            flops=2 * hidden * width * nodes, bytes_accessed=5 * 2**20, transcendentals=0
        ),
        name="mix",
    )(weight, bias, *pieces)


def on_device(features, tile_rows, tile_cols, tile_weights, order, weight, bias):
    width, nodes = features.shape
    _, blocks, slots, tile, _ = tile_weights.shape
    groups = lax.axis_size("grp")
    me = lax.axis_index("grp")
    share = nodes // groups
    ranges = cuts(width)
    rows = tile_rows.reshape(blocks, slots)
    cols = tile_cols.reshape(blocks, slots)
    counts = tile_weights.reshape(blocks * slots, tile, tile)

    ranks = list(range(groups - 1, -1, -1))
    whose = me ^ jnp.asarray(ranks, jnp.int32)
    far = groups - 2
    picks = [lax.dynamic_slice(order, ((me ^ k) * share,), (share,)) for k in ranks]

    block = lax.axis_index("blk").astype(jnp.int32)[None]
    told = jnp.broadcast_to(cols[None], (blocks, *cols.shape))
    told, panel, block = lax.optimization_barrier((told, staged(features), block))
    asked = lax.all_to_all(told, "blk", 0, 0, tiled=True)
    sent = []
    for low, size in ranges:
        source = features if sent else panel
        sent.append(list(pack(source, block, asked, low, size, tile)))
        asked, sent[-1][0] = lax.optimization_barrier((asked, sent[-1][0]))
    accs, inverse, column, across = own(
        features, rows, cols, whose * width, counts, bias, weight, ranges
    )
    accs, picks = lax.optimization_barrier((accs, picks))

    got, early = [], []
    for p, leaving in enumerate(sent):
        if p:
            leaving, got[-1], early[-1], accs = lax.optimization_barrier(
                (leaving, got[-1], early[-1], accs)
            )
        got.append([shifted(value, "blk", s + 1) for s, value in enumerate(leaving)])
        early.append(add_early(accs[p], inverse, rows, counts, got[p][:-1], 1))

    pieces, across_x, beside = {}, {}, {}
    for p, (low, size) in enumerate(ranges[:-1]):
        at = [groups * low + i * size for i in range(groups)]
        total, out_far = gather_far(
            early[p], inverse, rows, picks[:far], counts, got[p][-1:], blocks - 1
        )
        for i, piece in enumerate(out_far):
            across_x[at[i], 0] = traded(piece, "grp", ranks[i])
        halves = (share // 2, share // 2)
        near = gather_next(total, picks[far:], [halves, (share,)])
        near, early[p + 1], got[p + 1] = lax.optimization_barrier(
            (near, early[p + 1], got[p + 1])
        )
        beside[at[far], 0] = traded(near[0], "grp", 1)
        beside[at[far], share // 2] = traded(near[1], "grp", 1)
        pieces[at[far + 1], 0] = near[2]

    low, size = ranges[-1]
    at = [groups * low + i * size for i in range(groups)]
    total, (piece,) = gather_far(
        early[-1], inverse, rows, picks[:1], counts, got[-1][-1:], blocks - 1
    )
    first = traded(piece, "grp", ranks[0])
    for i in range(1, groups):
        widths, moved = (share,), 2**16
        if i < far:
            total, beside = lax.optimization_barrier((total, beside))
        elif i == far:
            total, across_x = lax.optimization_barrier((total, across_x))
            widths = (share // 2, share // 2)
        else:
            total, first = lax.optimization_barrier((total, first))
            moved = 2**22
        column_at = 0
        for piece in gather_next(total, [picks[i]], [widths], moved):
            pieces[at[i], column_at] = traded(piece, "grp", ranks[i]) if ranks[i] else piece
            column_at += piece.shape[1]
    pieces[at[0], 0] = first
    pieces.update(beside)
    pieces.update(across_x)
    return mix(across, column, pieces, share)


def solution(mesh):
    in_specs = (
        P("grp", ("parts", "blk")),
        P(("parts", "blk"), None, None),
        P(("parts", "blk"), None, None),
        P(("parts", "blk"), None, None, None, None),
        P(("parts", "blk")),
        P(),
        P(),
    )
    out_specs = P(None, ("parts", "blk", "grp"))
    return jax.shard_map(
        on_device, mesh=mesh, in_specs=in_specs, out_specs=out_specs, check_vma=False
    )
```

```python
import functools

import jax
import jax.numpy as jnp
from jax import lax
from jax.experimental import pallas as pl
from jax.experimental.pallas import tpu as pltpu
from jax.sharding import PartitionSpec as P

NN = (((1,), (0,)), ((), ()))
NT = (((1,), (1,)), ((), ()))
VMEM = pl.BlockSpec(memory_space=pltpu.VMEM)
SMEM = pl.BlockSpec(memory_space=pltpu.SMEM)
ANY = pl.BlockSpec(memory_space=pl.ANY)
CHUNK = 256
UNROLL = 64


def dot(a, b, dims):
    return lax.dot_general(a, b, dims, preferred_element_type=jnp.float32)


def padded(shape, dtype):
    rows = 1
    for extent in shape[:-1]:
        rows *= extent
    return rows * -(-shape[-1] // 128) * 128 * jnp.dtype(dtype).itemsize


def call(kernel, name, scalars, arrays, outs, scratch=(), moved=2**16):
    held = sum(padded(a.shape, a.dtype) for a in list(arrays) + list(outs))
    held += sum(padded(shape, dtype) for shape, dtype in scratch)
    return pl.pallas_call(
        kernel,
        out_shape=list(outs),
        in_specs=[SMEM] * len(scalars) + [VMEM] * len(arrays),
        out_specs=[VMEM] * len(outs),
        scratch_shapes=[pltpu.VMEM(shape, dtype) for shape, dtype in scratch],
        compiler_params=pltpu.CompilerParams(vmem_limit_bytes=held + 2**20),
        cost_estimate=pl.CostEstimate(flops=0, bytes_accessed=moved, transcendentals=0),
        name=name,
    )(*scalars, *arrays)


def shifted(value, axis, steps):
    count = lax.axis_size(axis)
    pairs = [(source, (source + steps) % count) for source in range(count)]
    return lax.ppermute(value, axis, pairs)


def traded(value, axis, k):
    return lax.ppermute(value, axis, [(i, i ^ k) for i in range(lax.axis_size(axis))])


def cuts(width):
    first = width * 5 // 8 // 16 * 16
    return ((0, first), (first, width - first))


def identity(size):
    row = lax.broadcasted_iota(jnp.int32, (size, size), 0)
    col = lax.broadcasted_iota(jnp.int32, (size, size), 1)
    return (row == col).astype(jnp.float32).astype(jnp.bfloat16)


def stage_kernel(panel, out):
    out[...] = panel[...]


def staged(panel):
    shape = jax.ShapeDtypeStruct(panel.shape, panel.dtype)
    return call(stage_kernel, "stage", [], [panel], [shape])[0]


def pack_kernel(low, size, offsets, slots, tile, *refs):
    asked, panel = refs[:offsets], refs[offsets]
    outs, sems = refs[offsets + 1 : -1], refs[-1]
    for s in range(offsets):

        def body(t, carry, s=s):
            at = pl.multiple_of(asked[s][s + 1, t] * tile, tile)
            pltpu.make_async_copy(
                panel.at[pl.ds(low, size), pl.ds(at, tile)], outs[s].at[t], sems.at[s]
            ).start()
            return carry

        lax.fori_loop(0, slots, body, 0, unroll=4)
    for s in range(offsets):
        pltpu.make_async_copy(outs[s], outs[s], sems.at[s]).wait()


def pack(panel, asked, low, size, tile):
    offsets, slots = len(asked), asked[0].shape[1]
    return pl.pallas_call(
        functools.partial(pack_kernel, low, size, offsets, slots, tile),
        out_shape=[jax.ShapeDtypeStruct((slots, size, tile), panel.dtype)] * offsets,
        in_specs=[SMEM] * offsets + [ANY],
        out_specs=[ANY] * offsets,
        scratch_shapes=[pltpu.SemaphoreType.DMA((offsets,))],
        compiler_params=pltpu.CompilerParams(vmem_limit_bytes=2**20),
        cost_estimate=pl.CostEstimate(flops=0, bytes_accessed=2**16, transcendentals=0),
        name="pack",
    )(*asked, panel)


def own_kernel(
    ranges, blocks, slots, tile, rows, cols, starts, panel, counts, bias, weight, *refs
):
    accs, (inverse, column, across, product, sorted_rows) = refs[:-5], refs[-5:]
    lanes = inverse.shape[1]
    row_tiles = panel.shape[1] // tile
    eye = identity(tile)
    ones = jnp.ones((tile, lanes), jnp.bfloat16)
    column[...] = jnp.broadcast_to(bias[...], column.shape[::-1]).T
    groups = starts.shape[0]
    for low, size in ranges:
        for i in range(groups):
            source = pl.multiple_of(starts[i] + low, 16)
            sorted_rows[pl.ds(groups * low + i * size, size), :] = weight[pl.ds(source, size), :]
    across[...] = dot(identity(across.shape[0]), sorted_rows[...], NT).astype(across.dtype)
    inverse[...] = jnp.ones(inverse.shape, jnp.float32)

    def block(s, carry):
        def multiply(t, inner):
            product[t] = dot(counts[s * slots + t], ones, NN)
            return inner

        def add(t, inner):
            at = pl.multiple_of(rows[s, t] * tile, tile)
            inverse[pl.ds(at, tile), :] += product[t]
            return inner

        lax.fori_loop(0, slots, multiply, 0, unroll=10)
        lax.fori_loop(0, slots, add, 0)
        return carry

    lax.fori_loop(0, blocks, block, 0)

    def start(r, carry):
        at = pl.multiple_of(r * tile, tile)
        scale = 1.0 / inverse[pl.ds(at, tile), :]
        inverse[pl.ds(at, tile), :] = scale
        for acc, (low, size) in zip(accs, ranges):
            here = dot(eye, panel[pl.ds(low, size), pl.ds(at, tile)], NT)
            acc[pl.ds(at, tile), :] = here * scale[:, :size]
        return carry

    lax.fori_loop(0, row_tiles, start, 0, unroll=4)

    for acc, (low, size) in zip(accs, ranges):

        def multiply(t, carry, low=low, size=size):
            col = pl.multiple_of(cols[0, t] * tile, tile)
            product[t, :, :size] = dot(counts[t], panel[pl.ds(low, size), pl.ds(col, tile)], NT)
            return carry

        def add(t, carry, acc=acc, size=size):
            at = pl.multiple_of(rows[0, t] * tile, tile)
            acc[pl.ds(at, tile), :] += product[t, :, :size] * inverse[pl.ds(at, tile), :size]
            return carry

        lax.fori_loop(0, slots, multiply, 0, unroll=10)
        lax.fori_loop(0, slots, add, 0)


def own(panel, rows, cols, starts, counts, bias, weight, ranges):
    blocks, slots = rows.shape
    nodes, tile = panel.shape[1], counts.shape[-1]
    lanes = max(size for _, size in ranges)
    shapes = [jax.ShapeDtypeStruct((nodes, size), jnp.float32) for _, size in ranges]
    shapes.append(jax.ShapeDtypeStruct((nodes, lanes), jnp.float32))
    shapes.append(jax.ShapeDtypeStruct((bias.shape[0], 128), bias.dtype))
    shapes.append(jax.ShapeDtypeStruct(weight.shape[::-1], weight.dtype))
    outs = call(
        functools.partial(own_kernel, ranges, blocks, slots, tile),
        "own",
        [rows, cols, starts],
        [panel, counts, bias[None, :], weight],
        shapes,
        [((slots, tile, lanes), jnp.float32), (weight.shape, weight.dtype)],
    )
    return outs[:-3], *outs[-3:]


def pick(order, nodes, stage, outs):
    count, size = stage.shape
    eye = identity(size)

    def group(i, carry):
        at = pl.multiple_of(i * UNROLL, UNROLL)
        for u in range(UNROLL):
            source = order[at + u]
            stage[pl.ds(at + u, 1), :] = nodes[pl.ds(source, 1), :]
        return carry

    lax.fori_loop(0, count // UNROLL, group, 0)
    first = 0
    for out in outs:
        columns = out.shape[1]
        for at in range(0, columns, CHUNK):
            chunk = stage[pl.ds(first + at, CHUNK), :].astype(jnp.bfloat16)
            out[:, pl.ds(at, CHUNK)] = dot(eye, chunk, NT).astype(out.dtype)
        first += columns


def add_tiles(first, rows, acc, inverse, counts, got, total, product):
    slots, tile, size = product.shape
    total[...] = acc[...]
    for s, tiles in enumerate(got, first):

        def multiply(t, carry, s=s, tiles=tiles):
            product[t] = dot(counts[s * slots + t], tiles[t], NT)
            return carry

        def add(t, carry, s=s):
            at = pl.multiple_of(rows[s, t] * tile, tile)
            total[pl.ds(at, tile), :] += product[t] * inverse[pl.ds(at, tile), :size]
            return carry

        lax.fori_loop(0, slots, multiply, 0, unroll=10)
        lax.fori_loop(0, slots, add, 0, unroll=2)


def early_kernel(first, offsets, rows, acc, inverse, counts, *refs):
    add_tiles(first, rows, acc, inverse, counts, refs[:offsets], *refs[offsets:])


def add_early(acc, inverse, rows, counts, got, first):
    slots, tile = rows.shape[1], counts.shape[-1]
    return call(
        functools.partial(early_kernel, first, len(got)),
        "add_early",
        [rows],
        [acc, inverse, counts, *got],
        [jax.ShapeDtypeStruct(acc.shape, jnp.float32)],
        [((slots, tile, acc.shape[1]), jnp.float32)],
    )[0]


def far_kernel(first, offsets, far, rows, *refs):
    orders, (acc, inverse, counts) = refs[:far], refs[far : far + 3]
    got, total = refs[far + 3 : far + 3 + offsets], refs[far + 3 + offsets]
    outs, (product, stage) = refs[far + 4 + offsets : -2], refs[-2:]
    add_tiles(first, rows, acc, inverse, counts, got, total, product)
    for order, out in zip(orders, outs):
        pick(order, total, stage, [out])


def gather_far(acc, inverse, rows, orders, counts, got, first):
    nodes, size = acc.shape
    slots, tile = rows.shape[1], counts.shape[-1]
    share, far = orders[0].shape[0], len(orders)
    outs = call(
        functools.partial(far_kernel, first, len(got), far),
        "gather_far",
        [rows, *orders],
        [acc, inverse, counts, *got],
        [jax.ShapeDtypeStruct((nodes, size), jnp.float32)]
        + [jax.ShapeDtypeStruct((size, share), jnp.bfloat16)] * far,
        [((slots, tile, size), jnp.float32), ((share, size), jnp.float32)],
        2**20,
    )
    return outs[0], outs[1:]


def next_kernel(orders, cuts_of, *refs):
    order, total, outs, stage = refs[:orders], refs[orders], refs[orders + 1 : -1], refs[-1]
    first = 0
    for indices, count in zip(order, cuts_of):
        pick(indices, total, stage, outs[first : first + count])
        first += count


def gather_next(total, orders, widths, moved=2**16):
    size = total.shape[1]
    return call(
        functools.partial(next_kernel, len(orders), tuple(len(w) for w in widths)),
        "gather_next",
        orders,
        [total],
        [jax.ShapeDtypeStruct((size, width), jnp.bfloat16) for w in widths for width in w],
        [((orders[0].shape[0], size), jnp.float32)],
        moved,
    )


def mix_kernel(places, weight, bias, *refs):
    pieces, (out, nodes, ready, sems) = refs[:-4], refs[-4:]
    copies = []
    for c in range(ready.shape[0]):
        step = ready.shape[2]
        low, high = c * step, (c + 1) * step
        for piece, (row, first) in zip(pieces, places):
            height, columns = piece.shape
            start, stop = max(low, first), min(high, first + columns)
            if start < stop:
                nodes[pl.ds(row, height), pl.ds(start, stop - start)] = piece[
                    :, pl.ds(start - first, stop - start)
                ]
        mixed = dot(weight[...], nodes[:, pl.ds(low, step)], NN)
        ready[c] = jnp.maximum(mixed + bias[:, :1], 0.0).astype(out.dtype)
        copies.append(
            pltpu.make_async_copy(ready.at[c], out.at[:, pl.ds(low, step)], sems.at[c])
        )
        copies[-1].start()
    for copy in copies:
        copy.wait()


def mix(weight, bias, placed, nodes):
    places, pieces = tuple(placed), list(placed.values())
    hidden, width = weight.shape
    step = min(512, nodes)
    return pl.pallas_call(
        functools.partial(mix_kernel, places),
        out_shape=jax.ShapeDtypeStruct((hidden, nodes), jnp.bfloat16),
        in_specs=[VMEM] * (2 + len(pieces)),
        out_specs=ANY,
        scratch_shapes=[
            pltpu.VMEM((width, nodes), jnp.bfloat16),
            pltpu.VMEM((nodes // step, hidden, step), jnp.bfloat16),
            pltpu.SemaphoreType.DMA((nodes // step,)),
        ],
        compiler_params=pltpu.CompilerParams(vmem_limit_bytes=16 * 2**20),
        cost_estimate=pl.CostEstimate(
            flops=2 * hidden * width * nodes, bytes_accessed=5 * 2**20, transcendentals=0
        ),
        name="mix",
    )(weight, bias, *pieces)


def on_device(features, tile_rows, tile_cols, tile_weights, order, weight, bias):
    width, nodes = features.shape
    _, blocks, slots, tile, _ = tile_weights.shape
    groups = lax.axis_size("grp")
    me = lax.axis_index("grp")
    share = nodes // groups
    ranges = cuts(width)
    rows = tile_rows.reshape(blocks, slots)
    cols = tile_cols.reshape(blocks, slots)
    counts = tile_weights.reshape(blocks * slots, tile, tile)

    ranks = list(range(groups - 1, -1, -1))
    whose = me ^ jnp.asarray(ranks, jnp.int32)
    far = groups - 2
    picks = [lax.dynamic_slice(order, ((me ^ k) * share,), (share,)) for k in ranks]

    asked = [shifted(cols, "blk", -s) for s in range(1, blocks)]
    *asked, panel = lax.optimization_barrier((*asked, staged(features)))
    sent = []
    for low, size in ranges:
        source = features if sent else panel
        sent.append(list(pack(source, asked, low, size, tile)))
        *asked, sent[-1][0] = lax.optimization_barrier((*asked, sent[-1][0]))
    accs, inverse, column, across = own(
        features, rows, cols, whose * width, counts, bias, weight, ranges
    )
    accs, picks = lax.optimization_barrier((accs, picks))

    got, early = [], []
    for p, leaving in enumerate(sent):
        if p:
            leaving, got[-1], early[-1], accs = lax.optimization_barrier(
                (leaving, got[-1], early[-1], accs)
            )
        got.append([shifted(value, "blk", s + 1) for s, value in enumerate(leaving)])
        early.append(add_early(accs[p], inverse, rows, counts, got[p][:1], 1))

    pieces, across_x, beside = {}, {}, {}
    for p, (low, size) in enumerate(ranges[:-1]):
        at = [groups * low + i * size for i in range(groups)]
        total, out_far = gather_far(
            early[p], inverse, rows, picks[:far], counts, got[p][1:], 2
        )
        for i, piece in enumerate(out_far):
            across_x[at[i], 0] = traded(piece, "grp", ranks[i])
        halves = (share // 2, share // 2)
        near = gather_next(total, picks[far:], [halves, (share,)])
        near, early[p + 1], got[p + 1] = lax.optimization_barrier(
            (near, early[p + 1], got[p + 1])
        )
        beside[at[far], 0] = traded(near[0], "grp", 1)
        beside[at[far], share // 2] = traded(near[1], "grp", 1)
        pieces[at[far + 1], 0] = near[2]

    low, size = ranges[-1]
    at = [groups * low + i * size for i in range(groups)]
    total, (piece,) = gather_far(
        early[-1], inverse, rows, picks[:1], counts, got[-1][1:], 2
    )
    first = traded(piece, "grp", ranks[0])
    for i in range(1, groups):
        widths, moved = (share,), 2**16
        if i < far:
            total, beside = lax.optimization_barrier((total, beside))
        elif i == far:
            total, across_x = lax.optimization_barrier((total, across_x))
            widths = (share // 2, share // 2)
        else:
            total, first = lax.optimization_barrier((total, first))
            moved = 2**22
        column_at = 0
        for piece in gather_next(total, [picks[i]], [widths], moved):
            pieces[at[i], column_at] = traded(piece, "grp", ranks[i]) if ranks[i] else piece
            column_at += piece.shape[1]
    pieces[at[0], 0] = first
    pieces.update(beside)
    pieces.update(across_x)
    return mix(across, column, pieces, share)


def solution(mesh):
    in_specs = (
        P("grp", ("parts", "blk")),
        P(("parts", "blk"), None, None),
        P(("parts", "blk"), None, None),
        P(("parts", "blk"), None, None, None, None),
        P(("parts", "blk")),
        P(),
        P(),
    )
    out_specs = P(None, ("parts", "blk", "grp"))
    return jax.shard_map(
        on_device, mesh=mesh, in_specs=in_specs, out_specs=out_specs, check_vma=False
    )
```
